32 devices in a mesh: dp: 8 (over y, x, core), mp: 4 (over z).
Axes of the slice: x: 2, y: 2, z: 4, core: 2. Of those that a mesh axis runs over, the one named last changes fastest.
Arguments:
- prefix_tokens: bfloat16 [16, 560, 2048], P('dp', 'mp'), may hold values from -6 to 6
- action_tokens: bfloat16 [16, 48, 1024], P('dp', 'mp'), may hold values from -6 to 6
- block_ids: int32 [16, 608], P('dp'), may hold values from 0 to 2, as said below
- live_dims: int32 [16, 32], P('dp'), may hold values from 0 to 1, as said below
- hidden_counts: int32 [4], replicated, may hold values from 256 to 2048, as said below
- pre_attn_gain: float32 [2048], replicated, may hold values from 0.5 to 1.5
- pre_mlp_gain: float32 [2048], replicated, may hold values from 0.5 to 1.5
- act_attn_gain: float32 [1024], replicated, may hold values from 0.5 to 1.5
- act_mlp_gain: float32 [1024], replicated, may hold values from 0.5 to 1.5
- pre_query: bfloat16 [2048, 2048], P(('dp', 'mp')), may hold values from -0.125 to 0.125
- pre_keyval: bfloat16 [2048, 512], P(('dp', 'mp')), may hold values from -0.125 to 0.125
- pre_output: bfloat16 [2048, 2048], P(('dp', 'mp')), may hold values from -3 to 3
- act_query: bfloat16 [1024, 2048], P(('dp', 'mp')), may hold values from -0.1875 to 0.1875
- act_keyval: bfloat16 [1024, 512], P(('dp', 'mp')), may hold values from -0.1875 to 0.1875
- act_output: bfloat16 [2048, 1024], P(('dp', 'mp')), may hold values from -3 to 3
- pre_gate: bfloat16 [2048, 16384], P('dp', 'mp'), may hold values from -0.125 to 0.125
- pre_up: bfloat16 [2048, 16384], P('dp', 'mp'), may hold values from -0.125 to 0.125
- pre_down: bfloat16 [16384, 2048], P('mp', 'dp'), may hold values from -0.046875 to 0.046875
- act_gate: bfloat16 [1024, 8192], P('dp', 'mp'), may hold values from -0.1875 to 0.1875
- act_up: bfloat16 [1024, 8192], P('dp', 'mp'), may hold values from -0.1875 to 0.1875
- act_down: bfloat16 [8192, 1024], P('mp', 'dp'), may hold values from -0.09375 to 0.09375
- action_head: bfloat16 [1024, 32], replicated, may hold values from -0.5 to 0.5
- prefix_cot: bfloat16 [16, 560, 2048], P('dp', 'mp'), may hold values from -6 to 6
- pred_cot: float32 [16, 48, 32], P('dp', 'mp'), may hold values from -6 to 6
Outputs:
- prefix_out: bfloat16 [16, 560, 2048], P('dp', 'mp')
- action_pred: float32 [16, 48, 32], P('dp', 'mp')
- prefix_grad: float32 [16, 560, 2048], P('dp', 'mp')
- action_grad: float32 [16, 48, 1024], P('dp', 'mp')
- grad_pre_attn_gain: float32 [2048], P(('dp', 'mp'))
- grad_pre_mlp_gain: float32 [2048], P(('dp', 'mp'))
- grad_act_attn_gain: float32 [1024], P(('dp', 'mp'))
- grad_act_mlp_gain: float32 [1024], P(('dp', 'mp'))
- grad_pre_query: float32 [2048, 2048], P(('dp', 'mp'))
- grad_pre_keyval: float32 [2048, 512], P(('dp', 'mp'))
- grad_pre_output: float32 [2048, 2048], P(('dp', 'mp'))
- grad_act_query: float32 [1024, 2048], P(('dp', 'mp'))
- grad_act_keyval: float32 [1024, 512], P(('dp', 'mp'))
- grad_act_output: float32 [2048, 1024], P(('dp', 'mp'))
- grad_pre_gate: float32 [2048, 16384], P('dp', 'mp')
- grad_pre_up: float32 [2048, 16384], P('dp', 'mp')
- grad_pre_down: float32 [16384, 2048], P('mp', 'dp')
- grad_act_gate: float32 [1024, 8192], P('dp', 'mp')
- grad_act_up: float32 [1024, 8192], P('dp', 'mp')
- grad_act_down: float32 [8192, 1024], P('mp', 'dp')
- grad_action_head: float32 [1024, 32], P(('dp', 'mp'))
The draws below stay inside these ranges and needn't reach their ends.
Inputs may be any that keep to these rules, and one draw needn't show every extreme that they name: `block_ids`: along each item: 0 from its first position up to a split inside the prefix, 1 for the rest of its first 560 positions, 2 for its 48 action positions. `live_dims`: each row is 1 on its leading 7 to 18 entries and 0 after; some row has 18 ones and another 7. `hidden_counts`: multiples of 256 that sum to 4096; exactly one equals 2048.
All inputs are finite; a program needn't handle non-finite values.
Results may differ from the reference program's by a relative error of at most 0.018.
Values may be sent and summed in bfloat16 or wider, within the bound.
No kernel may reach another device: no remote copies, remote signals or barrier semaphores. Data moves between devices by JAX's collectives and lax.ppermute only.
A program may use at most 320 MiB of HBM per device.

```python
import jax
import jax.numpy as jnp
from jax import lax

D = 2048
FF = 16384
DA = 1024
FFA = 4096
HEADS = 8
HD = 256
ADIM = 32
ACT = 48
PLEN = 560
SEQ = 608
BATCH = 16
UNIT = 256
CAPA = 2048
SLOTS = 8192


def draw_block_ids(key, part):
    key = jax.random.fold_in(key, 11)
    split_at = jax.random.randint(key, (BATCH, 1), PLEN // 4, PLEN)
    position = jnp.arange(SEQ)[None, :]
    return jnp.where(position < split_at, 0, jnp.where(position < PLEN, 1, 2)).astype(jnp.int32)


def draw_live_dims(key, part):
    key = jax.random.fold_in(key, 12)
    key_count, key_top, key_bottom = jax.random.split(key, 3)
    counts = jax.random.randint(key_count, (BATCH,), 7, 19)
    top_row = jax.random.randint(key_top, (), 0, BATCH)
    bottom_row = (top_row + jax.random.randint(key_bottom, (), 1, BATCH)) % BATCH
    row_ids = jnp.arange(BATCH)
    counts = jnp.where(row_ids == top_row, 18, jnp.where(row_ids == bottom_row, 7, counts))
    return (jnp.arange(ADIM)[None, :] < counts[:, None]).astype(jnp.int32)


def draw_hidden_counts(key, part):
    key = jax.random.fold_in(key, 13)
    devices = SLOTS // CAPA
    key_heavy, key_loop = jax.random.split(key)
    heavy_device = jax.random.randint(key_heavy, (), 0, devices)
    device_ids = jnp.arange(devices)
    unit_counts = jnp.where(device_ids == heavy_device, 8, 1).astype(jnp.int32)

    def add_unit(counter, current):
        scores = jax.random.randint(jax.random.fold_in(key_loop, counter), (devices,), 0, 1 << 20) * devices + device_ids
        open_device = (current < 7) & (device_ids != heavy_device)
        scores = jnp.where(open_device, scores, -1)
        winner = jnp.argmax(scores)
        return current + (device_ids == winner).astype(jnp.int32)
    unit_counts = lax.fori_loop(0, 3 * devices - 7, add_unit, unit_counts)
    return (unit_counts * UNIT).astype(jnp.int32)


def block_scale(own_key, shape, cuts, low, top_value):
    def one(axis_at, shards_of):
        heights = jax.random.uniform(jax.random.fold_in(jax.random.fold_in(own_key, 6), axis_at), (shards_of,), jnp.float32, low / len(cuts), top_value / len(cuts))
        return jnp.repeat(jnp.exp(heights), shape[axis_at] // shards_of).reshape((-1,) + (1,) * (len(shape) - axis_at - 1))

    loudness = one(*cuts[0])
    for cut in cuts[1:]:
        loudness = loudness * one(*cut)
    return loudness


def bell_draw(key, shape, deviation, reach, cuts=(), kind=jnp.bfloat16):
    factor_of = block_scale(key, shape, cuts, -0.22, 0.18) if cuts else 1.0
    result = jax.random.normal(key, shape, jnp.float32) * deviation * factor_of
    return jnp.minimum(jnp.maximum(result, -reach), reach).astype(kind)


def setup_inputs(seed: int = 0) -> dict:
    arg_keys = jax.random.split(jax.random.key(seed), 25)
    prefix_tokens = bell_draw(arg_keys[0], (BATCH, PLEN, D), 1.0, 6.0, ((0, 8), (1, 4)))
    action_tokens = bell_draw(arg_keys[1], (BATCH, ACT, DA), 1.0, 6.0, ((0, 8), (1, 4)))
    block_ids = draw_block_ids(jax.random.fold_in(arg_keys[24], 71), 0)
    live_dims = draw_live_dims(jax.random.fold_in(arg_keys[24], 71), 0)
    hidden_counts = draw_hidden_counts(jax.random.fold_in(arg_keys[24], 71), 0)
    pre_attn_gain = jnp.clip(1.0 + 0.1 * jax.random.normal(arg_keys[5], (D,), jnp.float32), 0.5, 1.5)
    pre_mlp_gain = jnp.clip(1.0 + 0.1 * jax.random.normal(arg_keys[6], (D,), jnp.float32), 0.5, 1.5)
    act_attn_gain = jnp.clip(1.0 + 0.1 * jax.random.normal(arg_keys[7], (DA,), jnp.float32), 0.5, 1.5)
    act_mlp_gain = jnp.clip(1.0 + 0.1 * jax.random.normal(arg_keys[8], (DA,), jnp.float32), 0.5, 1.5)
    pre_query = bell_draw(arg_keys[9], (D, HEADS * HD), D ** -0.5, 0.125, ((0, 32),))
    pre_keyval = bell_draw(arg_keys[10], (D, 2 * HD), D ** -0.5, 0.125, ((0, 32),))
    pre_output = bell_draw(arg_keys[11], (HEADS * HD, D), (max(4, HEADS * HD // SEQ)) ** -0.5, 3.0, ((0, 32),))
    act_query = bell_draw(arg_keys[12], (DA, HEADS * HD), DA ** -0.5, 0.1875, ((0, 32),))
    act_keyval = bell_draw(arg_keys[13], (DA, 2 * HD), DA ** -0.5, 0.1875, ((0, 32),))
    act_output = bell_draw(arg_keys[14], (HEADS * HD, DA), (max(4, HEADS * HD // SEQ)) ** -0.5, 3.0, ((0, 32),))
    pre_gate = bell_draw(arg_keys[15], (D, FF), D ** -0.5, 0.125, ((0, 8), (1, 4)))
    pre_up = bell_draw(arg_keys[16], (D, FF), D ** -0.5, 0.125, ((0, 8), (1, 4)))
    pre_down = bell_draw(arg_keys[17], (FF, D), FF ** -0.5, 0.046875, ((0, 4), (1, 8)))
    act_gate = bell_draw(arg_keys[18], (DA, SLOTS), DA ** -0.5, 0.1875, ((0, 8), (1, 4)))
    act_up = bell_draw(arg_keys[19], (DA, SLOTS), DA ** -0.5, 0.1875, ((0, 8), (1, 4)))
    act_down = bell_draw(arg_keys[20], (SLOTS, DA), FFA ** -0.5, 0.09375, ((0, 4), (1, 8)))
    action_head = bell_draw(arg_keys[21], (DA, ADIM), (DA // 8) ** -0.5, 0.5)
    prefix_cot = bell_draw(arg_keys[22], (BATCH, PLEN, D), 1.0, 6.0, ((0, 8), (1, 4)))
    pred_cot = bell_draw(arg_keys[23], (BATCH, ACT, ADIM), 1.0, 6.0, ((0, 8), (1, 4)), jnp.float32)
    return dict(prefix_tokens=prefix_tokens, action_tokens=action_tokens, block_ids=block_ids, live_dims=live_dims, hidden_counts=hidden_counts, pre_attn_gain=pre_attn_gain, pre_mlp_gain=pre_mlp_gain, act_attn_gain=act_attn_gain, act_mlp_gain=act_mlp_gain, pre_query=pre_query, pre_keyval=pre_keyval, pre_output=pre_output, act_query=act_query, act_keyval=act_keyval, act_output=act_output, pre_gate=pre_gate, pre_up=pre_up, pre_down=pre_down, act_gate=act_gate, act_up=act_up, act_down=act_down, action_head=action_head, prefix_cot=prefix_cot, pred_cot=pred_cot)


@jax.custom_vjp
def low(v):
    return lax.optimization_barrier(v.astype(jnp.bfloat16)).astype(jnp.float32)

@jax.custom_vjp
def low_back(v):
    return v

def low_keep(v):
    return (low(v), None)

def low_pass(kept, grad):
    return (grad,)

def back_keep(v):
    return (v, None)

def back_low(kept, grad):
    return (low(grad),)
low.defvjp(low_keep, low_pass)
low_back.defvjp(back_keep, back_low)
NORM_EPS = 1e-06
ROPE_BASE = 10000.0
HIGH = lax.Precision.HIGHEST
MASKED = -1e+30

def matmul_hi(left, right):
    return jnp.dot(left, right, precision=HIGH)

def rms_norm(values, gain_vec):
    return values * lax.rsqrt(lax.optimization_barrier(jnp.mean(values * values, axis=-1, keepdims=True)) + NORM_EPS) * gain_vec

def rope_tables(positions, head_dim):
    half_dim = head_dim // 2
    inverse = ROPE_BASE ** (-2.0 * jnp.arange(half_dim).astype(jnp.float32) / head_dim)
    angles = positions.astype(jnp.float32)[:, None] * inverse[None, :]
    return (jnp.cos(angles), jnp.sin(angles))

def rotate(values, cosine_tab, sine_tab):
    half_dim = values.shape[-1] // 2
    lower_half = values[..., :half_dim]
    upper_half = values[..., half_dim:]
    return jnp.concatenate([lower_half * cosine_tab - upper_half * sine_tab, upper_half * cosine_tab + lower_half * sine_tab], axis=-1)

def geglu(gate_pre, upward, live_mask):
    return jax.nn.gelu(gate_pre, approximate=True) * upward * live_mask

def item_forward(params, prefix_rows, action_rows, blocks_row, live_row, slot_live, cosine_tab, sine_tab):
    pre_attn_gain, pre_mlp_gain, act_attn_gain, act_mlp_gain, pre_query, pre_keyval, pre_output, act_query, act_keyval, act_output, pre_gate, pre_up, pre_down, act_gate, act_up, act_down, action_head = params
    pre_normed = low(rms_norm(prefix_rows, pre_attn_gain))
    act_normed = low(rms_norm(action_rows, act_attn_gain))
    query_raw = jnp.concatenate([matmul_hi(pre_normed, pre_query), matmul_hi(act_normed, act_query)], axis=0)
    query_rows = low(rotate(low_back(query_raw).reshape(SEQ, HEADS, HD), cosine_tab[:, None, :], sine_tab[:, None, :]))
    keyval_raw = low_back(jnp.concatenate([matmul_hi(pre_normed, pre_keyval), matmul_hi(act_normed, act_keyval)], axis=0))
    key_rows = low(rotate(keyval_raw[:, :HD], cosine_tab, sine_tab))
    value_rows = low(keyval_raw[:, HD:])
    scores = low_back(jnp.einsum('qhd,kd->hqk', query_rows, key_rows, precision=HIGH) * HD ** (-0.5))
    allowed = blocks_row[None, :] <= blocks_row[:, None]
    scores = jnp.where(allowed[None, :, :], scores, MASKED)
    probs = low(jax.nn.softmax(scores, axis=-1))
    attended = low(low_back(jnp.einsum('hqk,kd->qhd', probs, value_rows, precision=HIGH))).reshape(SEQ, HEADS * HD)
    pre_mid = prefix_rows + low_back(matmul_hi(attended[:PLEN], pre_output))
    act_mid = action_rows + low_back(matmul_hi(attended[PLEN:], act_output))
    pre_second = low(rms_norm(pre_mid, pre_mlp_gain))
    act_second = low(rms_norm(act_mid, act_mlp_gain))
    pre_hidden = low(geglu(low_back(matmul_hi(pre_second, pre_gate)), low_back(matmul_hi(pre_second, pre_up)), 1.0))
    act_hidden = low(geglu(low_back(matmul_hi(act_second, act_gate)), low_back(matmul_hi(act_second, act_up)), slot_live))
    pre_final = pre_mid + low_back(matmul_hi(pre_hidden, pre_down))
    act_final = act_mid + low_back(matmul_hi(act_hidden, act_down))
    prediction = low_back(matmul_hi(low(act_final), action_head)) * live_row
    return (pre_final, prediction)

def reference(prefix_tokens, action_tokens, block_ids, live_dims, hidden_counts, pre_attn_gain, pre_mlp_gain, act_attn_gain, act_mlp_gain, pre_query, pre_keyval, pre_output, act_query, act_keyval, act_output, pre_gate, pre_up, pre_down, act_gate, act_up, act_down, action_head, prefix_cot, pred_cot):
    params = tuple((weight.astype(jnp.float32) for weight in (pre_attn_gain, pre_mlp_gain, act_attn_gain, act_mlp_gain, pre_query, pre_keyval, pre_output, act_query, act_keyval, act_output, pre_gate, pre_up, pre_down, act_gate, act_up, act_down, action_head)))
    slot_ids = jnp.arange(SLOTS).astype(jnp.int32)
    slot_live = (slot_ids % CAPA < hidden_counts[slot_ids // CAPA]).astype(jnp.float32)
    cosine_tab, sine_tab = rope_tables(jnp.arange(SEQ).astype(jnp.int32), HD)
    zero_grads = tuple((jnp.zeros_like(weight) for weight in params))

    def one_item(running, item_data):
        prefix_rows, action_rows, blocks_row, live_row, prefix_back, pred_back = item_data

        def forward(weights, prefix_in, action_in):
            return item_forward(weights, prefix_in, action_in, blocks_row, live_row, slot_live, cosine_tab, sine_tab)
        outputs, pullback = jax.vjp(forward, params, prefix_rows, action_rows)
        weight_grads, prefix_back_grad, action_back_grad = pullback((prefix_back, pred_back))
        running = tuple((earlier + grad_part for earlier, grad_part in zip(running, weight_grads)))
        return (running, (outputs[0].astype(jnp.bfloat16), outputs[1], prefix_back_grad, action_back_grad))
    totals, stacked = lax.scan(one_item, zero_grads, (prefix_tokens.astype(jnp.float32), action_tokens.astype(jnp.float32), block_ids, live_dims.astype(jnp.float32), prefix_cot.astype(jnp.float32), pred_cot))
    return (stacked[0], stacked[1], stacked[2], stacked[3], totals[0], totals[1], totals[2], totals[3], totals[4], totals[5], totals[6], totals[7], totals[8], totals[9], totals[10], totals[11], totals[12], totals[13], totals[14], totals[15], totals[16])
```

```python
import jax
import jax.numpy as jnp
from jax import lax
from jax.experimental import pallas as pl
from jax.experimental.pallas import tpu as pltpu
from jax.sharding import PartitionSpec as P

NORM_EPS = 1e-06
ROPE_BASE = 10000.0
MASKED = -1e30
F32 = jnp.float32
BF16 = jnp.bfloat16


def hop(value, bit):
    size = lax.axis_size("dp")
    return lax.ppermute(value, "dp", [(d, d ^ bit) for d in range(size)])


def ring_up(value):
    size = lax.axis_size("mp")
    return lax.ppermute(value, "mp", [(d, (d + 1) % size) for d in range(size)])


def ring_down(value):
    size = lax.axis_size("mp")
    return lax.ppermute(value, "mp", [(d, (d - 1) % size) for d in range(size)])


def ring_gather(value):
    out = [value]
    for _ in range(lax.axis_size("mp") - 1):
        out.append(ring_up(out[-1]))
    return out


def ring_scatter(parts):
    total = parts[-1].astype(BF16)
    for part in parts[-2::-1]:
        total = ring_down(total.astype(BF16)).astype(F32) + part.astype(F32)
    return total


def chip_order(size):
    return sorted(range(1, size), key=lambda c: (bin(c).count("1"), c))


def rel_blocks():
    size = lax.axis_size("dp")
    place = jnp.arange(size, dtype=jnp.int32)
    half = size // 2
    rel = (place % half) * 2 + place // half
    return jnp.bitwise_xor(rel, lax.axis_index("dp").astype(jnp.int32))


def dp_gather(shard):
    chips = lax.axis_size("dp") // 2
    half = shard.shape[0] // 2
    got = {0: [shard]}

    def top(c):
        return got[c][0] if len(got[c]) == 2 else got[c][0][:half]

    def bottom(c):
        return got[c][1] if len(got[c]) == 2 else got[c][0][half:]

    for c in chip_order(chips):
        high, low = 1 << (c.bit_length() - 1), c & -c
        if high == low:
            got[c] = [hop(shard, 2 * high)]
        else:
            got[c] = [hop(top(c ^ high), 2 * high), hop(bottom(c ^ low), 2 * low)]
    own = [piece for c in range(chips) for piece in got[c]]
    return own + [hop(piece, 1) for piece in own]


def dp_scatter(own, other):
    chips = lax.axis_size("dp") // 2
    rows = own.shape[0] // chips
    half = rows // 2
    other = hop(other, 1)

    def term(start):
        cut = slice(start, start + half)
        return own[cut].astype(F32) + other[cut].astype(F32)

    acc = {c: [term(c * rows), term(c * rows + half)] for c in range(chips)}
    for c in reversed(chip_order(chips)):
        high, low = 1 << (c.bit_length() - 1), c & -c
        up, down = (piece.astype(BF16) for piece in acc[c])
        acc[c ^ high][0] = acc[c ^ high][0] + hop(up, 2 * high).astype(F32)
        acc[c ^ low][1] = acc[c ^ low][1] + hop(down, 2 * low).astype(F32)
    return jnp.concatenate(acc[0], axis=0)


def _copy_block(_, src, dst):
    dst[...] = src[...]


def permute_columns(values, order, inverse=False):
    count = order.shape[0]
    rows, width = values.shape
    block = width // count
    if block % 128:
        hit = order[:, None] == jnp.arange(count, dtype=order.dtype)[None, :]
        places = jnp.arange(count, dtype=order.dtype)
        back = jnp.sum(jnp.where(hit, places[:, None], 0), axis=0) if inverse else order
        split = values.reshape(rows, count, block)
        cuts = [lax.dynamic_slice_in_dim(split, back[g], 1, 1) for g in range(count)]
        return jnp.concatenate(cuts, axis=1).reshape(rows, width)
    here = pl.BlockSpec((rows, block), lambda g, idx: (0, g))
    there = pl.BlockSpec((rows, block), lambda g, idx: (0, idx[g]))
    return pl.pallas_call(
        _copy_block,
        grid_spec=pltpu.PrefetchScalarGridSpec(
            num_scalar_prefetch=1,
            grid=(count,),
            in_specs=[here if inverse else there],
            out_specs=there if inverse else here,
        ),
        out_shape=jax.ShapeDtypeStruct(values.shape, values.dtype),
    )(order, values)


def inverse_rms(values):
    return lax.rsqrt(jnp.mean(values * values, axis=-1, keepdims=True) + NORM_EPS)


def rms_norm(values, gain_vec):
    return values * inverse_rms(values) * gain_vec


def rms_back(values, gain_vec, grads):
    inverse = inverse_rms(values)
    unit = values * inverse
    scaled = gain_vec * grads
    mean = jnp.mean(unit * scaled, axis=-1, keepdims=True)
    return inverse * (scaled - unit * mean), jnp.sum(grads * unit, axis=0)


def rope_tables(positions, head_dim):
    half_dim = head_dim // 2
    inverse = ROPE_BASE ** (-2.0 * jnp.arange(half_dim).astype(F32) / head_dim)
    angles = positions.astype(F32)[:, None] * inverse[None, :]
    return (jnp.cos(angles), jnp.sin(angles))


def rotate(values, cosine_tab, sine_tab):
    half_dim = values.shape[-1] // 2
    lower_half = values[..., :half_dim]
    upper_half = values[..., half_dim:]
    return jnp.concatenate(
        [
            lower_half * cosine_tab - upper_half * sine_tab,
            upper_half * cosine_tab + lower_half * sine_tab,
        ],
        axis=-1,
    )


def mm(left, right):
    return lax.dot_general(left, right, (((1,), (0,)), ((), ())), preferred_element_type=F32)


def mm_nt(left, right):
    return lax.dot_general(left, right, (((1,), (1,)), ((), ())), preferred_element_type=F32)


def mm_tn(left, right):
    return lax.dot_general(left, right, (((0,), (0,)), ((), ())), preferred_element_type=F32)


def geglu(gate_val, up_val, live_mask):
    return jax.nn.gelu(gate_val, approximate=True) * up_val * live_mask


def feed_forward(rows, cot_rows, gate, up, down_t, live_mask):
    gate_val = mm(rows, gate)
    up_val = mm(rows, up)
    hidden_back = mm(cot_rows, down_t)
    hidden, pull = jax.vjp(lambda g, u: geglu(g, u, live_mask), gate_val, up_val)
    gate_back, up_back = pull(hidden_back)
    return hidden.astype(BF16), gate_back.astype(BF16), up_back.astype(BF16)


def shards(
    prefix_tokens,
    action_tokens,
    block_ids,
    live_dims,
    hidden_counts,
    pre_attn_gain,
    pre_mlp_gain,
    act_attn_gain,
    act_mlp_gain,
    pre_query,
    pre_keyval,
    pre_output,
    act_query,
    act_keyval,
    act_output,
    pre_gate,
    pre_up,
    pre_down,
    act_gate,
    act_up,
    act_down,
    action_head,
    prefix_cot,
    pred_cot,
):
    groups = lax.axis_size("mp")
    ways = lax.axis_size("dp")
    member = lax.axis_index("mp")
    items, pre_rows, width = prefix_tokens.shape
    act_rows, act_width = action_tokens.shape[1:]
    pre_len = pre_rows * groups
    head_dim = pre_keyval.shape[1] // 2
    query_width = pre_query.shape[1]
    heads = query_width // head_dim
    local_len = pre_rows + act_rows
    scale = head_dim ** (-0.5)
    order = rel_blocks()

    pre_part, act_part, out_part = pre_query.shape[0], act_query.shape[0], pre_output.shape[0]
    qkv_own = jnp.concatenate(
        [
            jnp.concatenate([pre_query, pre_keyval], axis=1),
            jnp.concatenate([act_query, act_keyval], axis=1),
        ],
        axis=0,
    )
    out_own = jnp.concatenate([pre_output, act_output], axis=1)

    def in_place(pieces):
        size = pieces[0].shape[0]
        twice = jnp.concatenate(pieces[::-1] * 2, axis=0)
        return lax.dynamic_slice_in_dim(twice, (groups - 1 - member) * size, groups * size, 0)

    qkv_ring = ring_gather(qkv_own)
    out_ring = ring_gather(out_own)
    qkv_block = jnp.concatenate(
        [
            in_place([piece[:pre_part] for piece in qkv_ring]),
            in_place([piece[pre_part:] for piece in qkv_ring]),
        ],
        axis=0,
    )
    pre_block = groups * pre_part
    out_block = in_place(out_ring)
    qkv_pieces = dp_gather(qkv_block)
    out_full = jnp.concatenate(dp_gather(out_block), axis=0)
    qkv_all = jnp.concatenate(qkv_pieces, axis=0).reshape(ways, -1, qkv_own.shape[1])
    pre_qkv = qkv_all[:, :pre_block].reshape(width, -1)
    act_qkv = qkv_all[:, pre_block:].reshape(act_width, -1)
    pre_out_w = out_full[:, :width]
    act_out_w = out_full[:, width:]

    gate_full = jnp.concatenate(dp_gather(pre_gate), axis=0)
    up_full = jnp.concatenate(dp_gather(pre_up), axis=0)
    down_full = jnp.concatenate(dp_gather(pre_down.T), axis=0)
    act_stack = jnp.concatenate([act_gate, act_up, act_down.T], axis=0)
    act_all = jnp.concatenate(dp_gather(act_stack), axis=0).reshape(ways, 3, -1, act_gate.shape[1])
    act_gate_full, act_up_full, act_down_full = (
        act_all[:, n].reshape(act_width, -1) for n in range(3)
    )

    pre_flat = prefix_tokens.reshape(items * pre_rows, width)
    act_flat = action_tokens.reshape(items * act_rows, act_width)
    cot_flat = prefix_cot.reshape(items * pre_rows, width)
    pre_x = pre_flat.astype(F32)
    act_x = act_flat.astype(F32)
    live_mask = live_dims[:, None, :].astype(F32)
    pred_back = (pred_cot * live_mask).astype(BF16).reshape(items * act_rows, -1)
    act_final_back = mm_nt(pred_back, action_head)
    cot_rel = permute_columns(cot_flat, order)
    act_cot_rel = permute_columns(act_final_back.astype(BF16), order)
    cot_all = jnp.concatenate(ring_gather(cot_rel), axis=0)
    act_cot_all = jnp.concatenate(ring_gather(act_cot_rel), axis=0)

    local_pos = jnp.concatenate(
        [
            member * pre_rows + jnp.arange(pre_rows),
            pre_len + member * act_rows + jnp.arange(act_rows),
        ]
    )
    cosine_tab, sine_tab = rope_tables(local_pos, head_dim)

    def blocks_of(which):
        return jnp.concatenate(
            [
                lax.dynamic_slice_in_dim(block_ids, which * pre_rows, pre_rows, 1),
                lax.dynamic_slice_in_dim(block_ids, pre_len + which * act_rows, act_rows, 1),
            ],
            axis=1,
        )

    local_blocks = blocks_of(member)
    key_blocks = jnp.concatenate(
        [blocks_of((member - r) % groups) for r in range(groups)], axis=1
    )
    allowed = key_blocks[:, None, None, :] <= local_blocks[:, None, :, None]

    def join(pre_part_rows, act_part_rows):
        return jnp.concatenate(
            [
                pre_part_rows.reshape(items, pre_rows, -1),
                act_part_rows.reshape(items, act_rows, -1),
            ],
            axis=1,
        )

    def part(joined):
        flat = joined.shape[-1]
        return (
            joined[:, :pre_rows].reshape(items * pre_rows, flat),
            joined[:, pre_rows:].reshape(items * act_rows, flat),
        )

    pre_normed = permute_columns(rms_norm(pre_x, pre_attn_gain).astype(BF16), order)
    act_normed = permute_columns(rms_norm(act_x, act_attn_gain).astype(BF16), order)
    keyval_raw = join(mm(pre_normed, pre_qkv[:, query_width:]), mm(act_normed, act_qkv[:, query_width:]))
    keyval_rows = jnp.concatenate(
        [rotate(keyval_raw[..., :head_dim], cosine_tab, sine_tab), keyval_raw[..., head_dim:]],
        axis=-1,
    ).astype(BF16)
    all_keyval = jnp.concatenate(ring_gather(keyval_rows), axis=1)
    key_rows = all_keyval[..., :head_dim]
    value_rows = all_keyval[..., head_dim:]
    query_raw = join(mm(pre_normed, pre_qkv[:, :query_width]), mm(act_normed, act_qkv[:, :query_width]))
    query_rows = rotate(
        query_raw.reshape(items, local_len, heads, head_dim),
        cosine_tab[:, None, :],
        sine_tab[:, None, :],
    ).astype(BF16)
    scores = (
        jnp.einsum("iqhd,ikd->ihqk", query_rows, key_rows, preferred_element_type=F32) * scale
    )
    probs = jax.nn.softmax(jnp.where(allowed, scores, MASKED), axis=-1)
    probs_low = probs.astype(BF16)
    attended = jnp.einsum("ihqk,ikd->iqhd", probs_low, value_rows, preferred_element_type=F32)
    attended = attended.astype(BF16).reshape(items, local_len, query_width)
    pre_att, act_att = (permute_columns(rows, order) for rows in part(attended))
    pre_mid = pre_x + mm(pre_att, pre_out_w)
    act_mid = act_x + mm(act_att, act_out_w)

    pre_second = permute_columns(rms_norm(pre_mid, pre_mlp_gain).astype(BF16), order)
    act_second = permute_columns(rms_norm(act_mid, act_mlp_gain).astype(BF16), order)
    pre_all = jnp.concatenate(ring_gather(pre_second), axis=0)
    act_all_rows = jnp.concatenate(ring_gather(act_second), axis=0)
    slot_count = lax.dynamic_index_in_dim(hidden_counts, member, keepdims=False)
    slot_live = (jnp.arange(act_gate.shape[1]) < slot_count).astype(F32)

    pre_hidden, pre_gate_back, pre_up_back = feed_forward(
        pre_all, cot_all, gate_full, up_full, down_full, 1.0
    )
    act_hidden, act_gate_back, act_up_back = feed_forward(
        act_all_rows, act_cot_all, act_gate_full, act_up_full, act_down_full, slot_live
    )

    def weight_grad(rows, grads):
        half = rows.shape[1] // 2
        return (
            mm_tn(rows[:, :half], grads).astype(BF16),
            mm_tn(rows[:, half:], grads).astype(BF16),
        )

    grad_pre_gate = dp_scatter(*weight_grad(pre_all, pre_gate_back))
    pre_second_part = mm_nt(pre_gate_back, gate_full) + mm_nt(pre_up_back, up_full)
    act_second_part = mm_nt(act_gate_back, act_gate_full) + mm_nt(act_up_back, act_up_full)
    grad_pre_up = dp_scatter(*weight_grad(pre_all, pre_up_back))
    grad_pre_down = dp_scatter(*weight_grad(cot_all, pre_hidden)).T
    act_terms = [
        weight_grad(act_all_rows, act_gate_back),
        weight_grad(act_all_rows, act_up_back),
        weight_grad(act_cot_all, act_hidden),
    ]

    def act_stacked(which):
        parts = [term[which].reshape(ways // 2, -1, act_gate.shape[1]) for term in act_terms]
        return jnp.concatenate(parts, axis=1).reshape(-1, act_gate.shape[1])

    grad_act = dp_scatter(act_stacked(0), act_stacked(1)).reshape(3, -1, act_gate.shape[1])
    grad_act_gate, grad_act_up, grad_act_down = grad_act[0], grad_act[1], grad_act[2].T

    def row_sums(partial):
        count = partial.shape[0] // groups
        return ring_scatter([partial[r * count : (r + 1) * count] for r in range(groups)])

    pre_second_back = permute_columns(row_sums(pre_second_part), order, True)
    act_second_back = permute_columns(row_sums(act_second_part), order, True)
    pre_sums = permute_columns(row_sums(mm_nt(pre_hidden, down_full)), order, True)
    act_sums = permute_columns(row_sums(mm_nt(act_hidden, act_down_full)), order, True)

    prefix_out = (pre_mid + pre_sums).astype(BF16).reshape(prefix_tokens.shape)
    act_final_low = (act_mid + act_sums).astype(BF16)
    action_pred = mm(act_final_low, action_head).reshape(pred_cot.shape) * live_mask
    grad_head = mm_tn(act_final_low, pred_back)

    pre_mid_part, grad_pre_mlp_gain = rms_back(pre_mid, pre_mlp_gain, pre_second_back)
    act_mid_part, grad_act_mlp_gain = rms_back(act_mid, act_mlp_gain, act_second_back)
    pre_mid_grad = cot_flat.astype(F32) + pre_mid_part
    act_mid_grad = act_final_back + act_mid_part
    pre_out_back = pre_mid_grad.astype(BF16)
    act_out_back = act_mid_grad.astype(BF16)
    out_half = query_width // 2
    out_own_grad, out_other_grad = (
        jnp.concatenate(
            [mm_tn(pre_att[:, cut], pre_out_back), mm_tn(act_att[:, cut], act_out_back)], axis=1
        ).astype(BF16)
        for cut in (slice(0, out_half), slice(out_half, None))
    )
    grad_out = dp_scatter(out_own_grad, out_other_grad)
    attended_back = join(
        permute_columns(mm_nt(pre_out_back, pre_out_w).astype(BF16), order, True),
        permute_columns(mm_nt(act_out_back, act_out_w).astype(BF16), order, True),
    ).reshape(items, local_len, heads, head_dim)
    probs_back = jnp.einsum(
        "iqhd,ikd->ihqk", attended_back, value_rows, preferred_element_type=F32
    )
    value_back = jnp.einsum(
        "ihqk,iqhd->ikd", probs_low, attended_back, preferred_element_type=F32
    )
    scores_back = (
        probs * (probs_back - jnp.sum(probs * probs_back, axis=-1, keepdims=True))
    ).astype(BF16)
    key_back = (
        jnp.einsum("ihqk,iqhd->ikd", scores_back, query_rows, preferred_element_type=F32) * scale
    )
    query_back = (
        jnp.einsum("ihqk,ikd->iqhd", scores_back, key_rows, preferred_element_type=F32) * scale
    )
    keyval_back = jnp.concatenate([key_back, value_back], axis=-1).astype(BF16)
    own_kv_back = ring_scatter(
        [keyval_back[:, r * local_len : (r + 1) * local_len] for r in range(groups)]
    )
    keyval_low = jnp.concatenate(
        [rotate(own_kv_back[..., :head_dim], cosine_tab, -sine_tab), own_kv_back[..., head_dim:]],
        axis=-1,
    ).astype(BF16)
    query_low = rotate(query_back, cosine_tab[:, None, :], -sine_tab[:, None, :])
    query_low = query_low.reshape(items, local_len, query_width).astype(BF16)
    pre_back, act_back = part(jnp.concatenate([query_low, keyval_low], axis=-1))

    def qkv_term(which):
        pre_half, act_half = width // 2, act_width // 2
        pre_grad = mm_tn(pre_normed[:, which * pre_half : (which + 1) * pre_half], pre_back)
        act_grad = mm_tn(act_normed[:, which * act_half : (which + 1) * act_half], act_back)
        parts = [
            grad.astype(BF16).reshape(ways // 2, -1, grad.shape[1]) for grad in (pre_grad, act_grad)
        ]
        return jnp.concatenate(parts, axis=1).reshape(-1, pre_back.shape[1])

    grad_qkv = dp_scatter(qkv_term(0), qkv_term(1))

    def for_members(block):
        size = block.shape[0] // groups
        return [
            lax.dynamic_slice_in_dim(block, ((member - r) % groups) * size, size, 0)
            for r in range(groups)
        ]

    grad_out = ring_scatter(for_members(grad_out))
    grad_qkv = ring_scatter(
        [
            jnp.concatenate([upper, lower], axis=0)
            for upper, lower in zip(
                for_members(grad_qkv[:pre_block]), for_members(grad_qkv[pre_block:])
            )
        ]
    )
    pre_normed_back = permute_columns(mm_nt(pre_back, pre_qkv), order, True)
    act_normed_back = permute_columns(mm_nt(act_back, act_qkv), order, True)
    pre_x_part, grad_pre_attn_gain = rms_back(pre_x, pre_attn_gain, pre_normed_back)
    act_x_part, grad_act_attn_gain = rms_back(act_x, act_attn_gain, act_normed_back)
    prefix_grad = (pre_mid_grad + pre_x_part).reshape(prefix_tokens.shape)
    action_grad = (act_mid_grad + act_x_part).reshape(action_tokens.shape)

    devices = ways * groups
    small = jnp.concatenate(
        [
            value.reshape(devices, -1)
            for value in (
                grad_pre_attn_gain,
                grad_pre_mlp_gain,
                grad_act_attn_gain,
                grad_act_mlp_gain,
                grad_head,
            )
        ],
        axis=1,
    )
    bit = 1
    while bit < ways:
        small = small + hop(small, bit)
        bit *= 2
    mine = lax.axis_index("dp") * groups
    terms = [
        lax.dynamic_slice_in_dim(small, mine + (member - r) % groups, 1, 0) for r in range(groups)
    ]
    total = terms[-1]
    for term in terms[-2::-1]:
        total = ring_down(total) + term
    sizes = [width // devices] * 2 + [act_width // devices] * 2
    gains, start = [], 0
    for size in sizes:
        gains.append(total[0, start : start + size])
        start += size
    grad_head = total[0, start:].reshape(act_width // devices, -1)

    return (
        prefix_out,
        action_pred,
        prefix_grad,
        action_grad,
        *gains,
        grad_qkv[:pre_part, :query_width],
        grad_qkv[:pre_part, query_width:],
        grad_out[:, :width],
        grad_qkv[pre_part:, :query_width],
        grad_qkv[pre_part:, query_width:],
        grad_out[:, width:],
        grad_pre_gate,
        grad_pre_up,
        grad_pre_down,
        grad_act_gate,
        grad_act_up,
        grad_act_down,
        grad_head,
    )


def solution(mesh):
    rows = P("dp", "mp", None)
    both = P(("dp", "mp"), None)
    wide = P("dp", "mp")
    tall = P("mp", "dp")
    in_specs = (
        (rows, rows, P("dp", None), P("dp", None))
        + (P(),) * 5
        + (both,) * 6
        + (wide, wide, tall, wide, wide, tall, P(), rows, rows)
    )
    out_specs = (
        (rows,) * 4
        + (P(("dp", "mp")),) * 4
        + (both,) * 6
        + (wide, wide, tall, wide, wide, tall, both)
    )
    return jax.shard_map(shards, mesh=mesh, in_specs=in_specs, out_specs=out_specs, check_vma=False)
```

```python
import functools

import jax
import jax.numpy as jnp
from jax import lax
from jax.experimental import pallas as pl
from jax.experimental.pallas import tpu as pltpu
from jax.sharding import PartitionSpec as P

NORM_EPS = 1e-06
ROPE_BASE = 10000.0
MASKED = -1e30
F32 = jnp.float32
BF16 = jnp.bfloat16


class Links:
    def __init__(self, window=2):
        self.window = window
        self.done = {}

    def send(self, value, axis, pairs, link):
        sent = self.done.setdefault(link, [])
        if len(sent) >= self.window:
            value, _ = lax.optimization_barrier((value, sent[-self.window]))
        result = lax.ppermute(value, axis, pairs)
        sent.append(result)
        return result


LINKS = Links()


def hop(value, bit):
    size = lax.axis_size("dp")
    pairs = [(d, d ^ bit) for d in range(size)]
    if bit == 1:
        return lax.ppermute(value, "dp", pairs)
    return LINKS.send(value, "dp", pairs, bit)


LOOSE = None


def ring(value, step, link="mp"):
    size = lax.axis_size("mp")
    pairs = [(d, (d + step) % size) for d in range(size)]
    if link is LOOSE:
        return lax.ppermute(value, "mp", pairs)
    return LINKS.send(value, "mp", pairs, link)


def ring_gather(value, link="mp"):
    out = [value]
    for _ in range(lax.axis_size("mp") - 1):
        out.append(ring(out[-1], 1, link))
    return out


def ring_scatter(parts, steps=None):
    total = parts[-1].astype(BF16)
    for part in parts[-2::-1]:
        moved = ring(total.astype(BF16), -1, LOOSE)
        if steps is not None:
            steps.append(moved)
        total = moved.astype(F32) + part.astype(F32)
    return total


def chip_order(size):
    return sorted(range(1, size), key=lambda c: (bin(c).count("1"), c))


def rel_blocks():
    size = lax.axis_size("dp")
    place = jnp.arange(size, dtype=jnp.int32)
    half = size // 2
    rel = (place % half) * 2 + place // half
    return jnp.bitwise_xor(rel, lax.axis_index("dp").astype(jnp.int32))


def dp_gather(shard):
    chips = lax.axis_size("dp") // 2
    half = shard.shape[0] // 2
    got = {0: [shard]}

    def top(c):
        return got[c][0] if len(got[c]) == 2 else got[c][0][:half]

    def bottom(c):
        return got[c][1] if len(got[c]) == 2 else got[c][0][half:]

    for c in chip_order(chips):
        high, low = 1 << (c.bit_length() - 1), c & -c
        if high == low:
            got[c] = [hop(shard, 2 * high)]
        else:
            got[c] = [hop(top(c ^ high), 2 * high), hop(bottom(c ^ low), 2 * low)]
    own = [piece for c in range(chips) for piece in got[c]]
    return own + [hop(piece, 1) for piece in own]


def scatter_rows(own, other, layout):
    size = lax.axis_size("dp")
    groups = lax.axis_size("mp")
    chips = size // 2
    rows = own.shape[0] // chips
    other = hop(other, 1)

    def block(c):
        cut = slice(c * rows, (c + 1) * rows)
        return own[cut].astype(F32) + other[cut].astype(F32)

    total = block(0)
    for c in range(1, chips):
        pairs = [(d, d ^ (2 * c)) for d in range(size)]
        total = total + lax.ppermute(block(c).astype(BF16), "dp", pairs).astype(F32)
    parts = []
    for r in range(groups):
        which = (lax.axis_index("mp") - r) % groups
        cuts, start = [], 0
        for part in layout:
            cuts.append(lax.dynamic_slice_in_dim(total, start + which * part, part, 0))
            start += groups * part
        parts.append(jnp.concatenate(cuts, axis=0))
    return ring_scatter(parts)


def _permute_blocks(inverse, order, *refs):
    half = len(refs) // 2
    for src, dst in zip(refs[:half], refs[half:]):
        block = src.shape[1] // order.shape[0]
        for g in range(order.shape[0]):
            here = slice(g * block, (g + 1) * block)
            there = pl.ds(pl.multiple_of(order[g] * block, block), block)
            if inverse:
                dst[:, there] = src[:, here]
            else:
                dst[:, here] = src[:, there]


def permute_columns(arrays, order, inverse=False):
    count = order.shape[0]
    if any(values.shape[1] // count % 128 for values in arrays):
        hit = order[:, None] == jnp.arange(count, dtype=order.dtype)[None, :]
        places = jnp.arange(count, dtype=order.dtype)
        back = jnp.sum(jnp.where(hit, places[:, None], 0), axis=0) if inverse else order
        outs = []
        for values in arrays:
            split = values.reshape(values.shape[0], count, -1)
            cuts = [lax.dynamic_slice_in_dim(split, back[g], 1, 1) for g in range(count)]
            outs.append(jnp.concatenate(cuts, axis=1).reshape(values.shape))
        return outs
    return pl.pallas_call(
        functools.partial(_permute_blocks, inverse),
        in_specs=[pl.BlockSpec(memory_space=pltpu.SMEM)]
        + [pl.BlockSpec(memory_space=pltpu.VMEM)] * len(arrays),
        out_specs=[pl.BlockSpec(memory_space=pltpu.VMEM)] * len(arrays),
        out_shape=[jax.ShapeDtypeStruct(values.shape, values.dtype) for values in arrays],
        compiler_params=pltpu.CompilerParams(vmem_limit_bytes=32 * 2**20),
    )(order, *arrays)


def _spread(count, order, pre, act, joint):
    rows = pre.shape[0]
    narrow = [value.shape[1] // count for value in (pre, act)]
    joint[...] = jnp.zeros_like(joint)
    for g in range(count):
        start = g * sum(narrow)
        there = pl.ds(pl.multiple_of(order[g] * narrow[0], narrow[0]), narrow[0])
        joint[:rows, start : start + narrow[0]] = pre[:, there]
        there = pl.ds(pl.multiple_of(order[g] * narrow[1], narrow[1]), narrow[1])
        joint[rows:, start + narrow[0] : start + sum(narrow)] = act[:, there]


def _unspread(count, order, joint, pre, act):
    rows = pre.shape[0]
    narrow = [value.shape[1] // count for value in (pre, act)]
    for g in range(count):
        start = g * sum(narrow)
        there = pl.ds(pl.multiple_of(order[g] * narrow[0], narrow[0]), narrow[0])
        pre[:, there] = joint[:rows, start : start + narrow[0]]
        there = pl.ds(pl.multiple_of(order[g] * narrow[1], narrow[1]), narrow[1])
        act[:, there] = joint[rows:, start + narrow[0] : start + sum(narrow)]


def block_call(body, order, arrays, shapes):
    return pl.pallas_call(
        functools.partial(body, order.shape[0]),
        in_specs=[pl.BlockSpec(memory_space=pltpu.SMEM)]
        + [pl.BlockSpec(memory_space=pltpu.VMEM)] * len(arrays),
        out_specs=[pl.BlockSpec(memory_space=pltpu.VMEM)] * len(shapes),
        out_shape=shapes,
        compiler_params=pltpu.CompilerParams(vmem_limit_bytes=32 * 2**20),
    )(order, *arrays)


def spread(pre, act, order):
    count = order.shape[0]
    rows, lines = pre.shape[0], act.shape[0]
    wide, thin = pre.shape[1] // count, act.shape[1] // count
    if wide % 128 or thin % 128:
        upper, lower = permute_columns([pre, act], order)
        upper = jnp.pad(upper.reshape(rows, count, wide), ((0, lines), (0, 0), (0, thin)))
        lower = jnp.pad(lower.reshape(lines, count, thin), ((rows, 0), (0, 0), (wide, 0)))
        return (upper + lower).reshape(rows + lines, -1)
    shape = jax.ShapeDtypeStruct((rows + lines, pre.shape[1] + act.shape[1]), pre.dtype)
    return block_call(_spread, order, [pre, act], [shape])[0]


def unspread(joint, rows, wide, thin, order):
    count = order.shape[0]
    lines = joint.shape[0] - rows
    if wide // count % 128 or thin // count % 128:
        blocks = joint.reshape(joint.shape[0], count, -1)
        upper = blocks[:rows, :, : wide // count].reshape(rows, wide)
        lower = blocks[rows:, :, wide // count :].reshape(lines, thin)
        return permute_columns([upper, lower], order, True)
    shapes = [
        jax.ShapeDtypeStruct((rows, wide), joint.dtype),
        jax.ShapeDtypeStruct((lines, thin), joint.dtype),
    ]
    return block_call(_unspread, order, [joint], shapes)


def inverse_rms(values):
    return lax.rsqrt(jnp.mean(values * values, axis=-1, keepdims=True) + NORM_EPS)


def rms_norm(values, gain_vec):
    return values * inverse_rms(values) * gain_vec


def rms_back(values, gain_vec, grads):
    inverse = inverse_rms(values)
    unit = values * inverse
    scaled = gain_vec * grads
    mean = jnp.mean(unit * scaled, axis=-1, keepdims=True)
    return inverse * (scaled - unit * mean), jnp.sum(grads * unit, axis=0)


def rope_tables(positions, head_dim):
    half_dim = head_dim // 2
    inverse = ROPE_BASE ** (-2.0 * jnp.arange(half_dim).astype(F32) / head_dim)
    angles = positions.astype(F32)[:, None] * inverse[None, :]
    return (jnp.cos(angles), jnp.sin(angles))


def rotate(values, cosine_tab, sine_tab):
    half_dim = values.shape[-1] // 2
    lower_half = values[..., :half_dim]
    upper_half = values[..., half_dim:]
    return jnp.concatenate(
        [
            lower_half * cosine_tab - upper_half * sine_tab,
            upper_half * cosine_tab + lower_half * sine_tab,
        ],
        axis=-1,
    )


def mm(left, right):
    return lax.dot_general(left, right, (((1,), (0,)), ((), ())), preferred_element_type=F32)


def mm_nt(left, right):
    return lax.dot_general(left, right, (((1,), (1,)), ((), ())), preferred_element_type=F32)


def mm_tn(left, right):
    return lax.dot_general(left, right, (((0,), (0,)), ((), ())), preferred_element_type=F32)


def geglu(gate_val, up_val, live_mask):
    return jax.nn.gelu(gate_val, approximate=True) * up_val * live_mask


def feed_forward(rows, cot_rows, gate, up, down_t, live_mask):
    gate_val = mm(rows, gate)
    up_val = mm(rows, up)
    hidden_back = mm(cot_rows, down_t)
    hidden, pull = jax.vjp(lambda g, u: geglu(g, u, live_mask), gate_val, up_val)
    gate_back, up_back = pull(hidden_back)
    return hidden.astype(BF16), gate_back.astype(BF16), up_back.astype(BF16)


def _feed_forward_tile(groups, *refs):
    pieces, (back_ref, gate_ref, up_ref) = refs[:groups], refs[groups : groups + 3]
    hidden_ref, gate_back_ref, up_back_ref, rows_ref = refs[groups + 3 :]
    count = pieces[0].shape[0]
    root, cube = 0.7978845608028654, 0.044715

    @pl.when(pl.program_id(0) == 0)
    def _():
        for r in range(groups):
            rows_ref[r * count : (r + 1) * count, :] = pieces[r][...]

    for r in range(groups):
        cut = slice(r * count, (r + 1) * count)
        rows = pieces[r][...]
        gate_val = jnp.dot(rows, gate_ref[...], preferred_element_type=F32)
        up_val = jnp.dot(rows, up_ref[...], preferred_element_type=F32)
        back = back_ref[cut, :].astype(F32)
        square = gate_val * gate_val
        bend = jnp.tanh(root * gate_val * (1.0 + cube * square))
        half_open = 0.5 * (1.0 + bend)
        active = gate_val * half_open
        inner = (0.5 * root) * gate_val * (1.0 - bend * bend) * (1.0 + 3.0 * cube * square)
        hidden_ref[cut, :] = (active * up_val).astype(BF16)
        gate_back_ref[cut, :] = (back * up_val * (half_open + inner)).astype(BF16)
        up_back_ref[cut, :] = (back * active).astype(BF16)


def feed_forward_kernel(pieces, hidden_back, gate, up, tile=512):
    groups = len(pieces)
    count, width = pieces[0].shape
    total = groups * count
    units = gate.shape[1]
    block = pl.BlockSpec((total, tile), lambda n: (0, n))
    weight = pl.BlockSpec((width, tile), lambda n: (0, n))
    fixed = pl.BlockSpec((count, width), lambda n: (0, 0), pipeline_mode=pl.Buffered(1))
    return pl.pallas_call(
        functools.partial(_feed_forward_tile, groups),
        grid=(units // tile,),
        in_specs=[fixed] * groups + [block, weight, weight],
        out_specs=[block] * 3 + [pl.BlockSpec((total, width), lambda n: (0, 0))],
        out_shape=[jax.ShapeDtypeStruct((total, units), BF16)] * 3
        + [jax.ShapeDtypeStruct((total, width), BF16)],
        compiler_params=pltpu.CompilerParams(vmem_limit_bytes=56 * 2**20),
        cost_estimate=pl.CostEstimate(
            flops=4 * total * width * units,
            bytes_accessed=4 * width * units + 8 * total * units + 4 * total * width,
            transcendentals=total * units,
        ),
    )(*pieces, hidden_back, gate, up)


def after(value, *first):
    return lax.optimization_barrier((value, *first))[0]


def shards(
    prefix_tokens,
    action_tokens,
    block_ids,
    live_dims,
    hidden_counts,
    pre_attn_gain,
    pre_mlp_gain,
    act_attn_gain,
    act_mlp_gain,
    pre_query,
    pre_keyval,
    pre_output,
    act_query,
    act_keyval,
    act_output,
    pre_gate,
    pre_up,
    pre_down,
    act_gate,
    act_up,
    act_down,
    action_head,
    prefix_cot,
    pred_cot,
):
    groups = lax.axis_size("mp")
    ways = lax.axis_size("dp")
    member = lax.axis_index("mp")
    items, pre_rows, width = prefix_tokens.shape
    act_rows, act_width = action_tokens.shape[1:]
    pre_len = pre_rows * groups
    head_dim = pre_keyval.shape[1] // 2
    query_width = pre_query.shape[1]
    heads = query_width // head_dim
    local_len = pre_rows + act_rows
    scale = head_dim ** (-0.5)
    order = rel_blocks()
    LINKS.done.clear()

    pre_part, act_part, out_part = pre_query.shape[0], act_query.shape[0], pre_output.shape[0]
    qkv_own = jnp.concatenate(
        [
            jnp.concatenate([pre_query, pre_keyval], axis=1),
            jnp.concatenate([act_query, act_keyval], axis=1),
        ],
        axis=0,
    )
    out_own = jnp.concatenate([pre_output, act_output], axis=1)

    def in_place(pieces):
        size = pieces[0].shape[0]
        twice = jnp.concatenate(pieces[::-1] * 2, axis=0)
        return lax.dynamic_slice_in_dim(twice, (groups - 1 - member) * size, groups * size, 0)

    qkv_ring = ring_gather(qkv_own)
    out_ring = ring_gather(out_own)
    qkv_block = jnp.concatenate(
        [
            in_place([piece[:pre_part] for piece in qkv_ring]),
            in_place([piece[pre_part:] for piece in qkv_ring]),
        ],
        axis=0,
    )
    pre_block = groups * pre_part
    out_block = in_place(out_ring)
    qkv_full = jnp.concatenate(dp_gather(qkv_block), axis=0)
    out_full = jnp.concatenate(dp_gather(out_block), axis=0)
    gate_full = lax.all_gather(pre_gate, "dp", axis=0, tiled=True)
    down_full = lax.all_gather(pre_down, "dp", axis=1, tiled=True)
    act_stack = jnp.concatenate([act_gate, act_up, act_down.T], axis=0)
    act_flat_w = lax.all_gather(act_stack, "dp", axis=0, tiled=True)
    up_full = lax.all_gather(after(pre_up, act_flat_w), "dp", axis=0, tiled=True)
    act_all = act_flat_w.reshape(ways, 3, -1, act_gate.shape[1])
    act_gate_full, act_up_full, act_down_full = (
        act_all[:, n].reshape(act_width, -1) for n in range(3)
    )

    pre_flat = prefix_tokens.reshape(items * pre_rows, width)
    act_flat = action_tokens.reshape(items * act_rows, act_width)
    cot_flat = prefix_cot.reshape(items * pre_rows, width)
    pre_x = pre_flat.astype(F32)
    act_x = act_flat.astype(F32)
    live_mask = live_dims[:, None, :].astype(F32)
    pred_back = (pred_cot * live_mask).astype(BF16).reshape(items * act_rows, -1)
    act_final_back = mm_nt(pred_back, action_head)
    count = items * pre_rows
    padded = -(-count // 16) * 16
    act_count = items * act_rows

    def pad(values):
        return jnp.pad(values, ((0, padded - count), (0, 0)))

    def ring_stack(value):
        return jnp.concatenate(ring_gather(value), axis=0)

    cot_all = ring_stack(pad(cot_flat))
    act_cot_all = ring_stack(act_final_back.astype(BF16))
    hidden_back = mm_nt(cot_all, down_full).astype(BF16)

    local_pos = jnp.concatenate(
        [
            member * pre_rows + jnp.arange(pre_rows),
            pre_len + member * act_rows + jnp.arange(act_rows),
        ]
    )
    cosine_tab, sine_tab = rope_tables(local_pos, head_dim)

    def blocks_of(which):
        return jnp.concatenate(
            [
                lax.dynamic_slice_in_dim(block_ids, which * pre_rows, pre_rows, 1),
                lax.dynamic_slice_in_dim(block_ids, pre_len + which * act_rows, act_rows, 1),
            ],
            axis=1,
        )

    local_blocks = blocks_of(member)
    key_blocks = jnp.concatenate(
        [blocks_of((member - r) % groups) for r in range(groups)], axis=1
    )
    allowed = key_blocks[:, None, None, :] <= local_blocks[:, None, :, None]

    act_padded = -(-act_count // 16) * 16

    def stack(pre_part_rows, act_part_rows):
        return (
            jnp.pad(pre_part_rows, ((0, padded - count), (0, 0))),
            jnp.pad(act_part_rows, ((0, act_padded - act_count), (0, 0))),
        )

    def to_items(joint):
        return jnp.concatenate(
            [
                joint[:count].reshape(items, pre_rows, -1),
                joint[padded : padded + act_count].reshape(items, act_rows, -1),
            ],
            axis=1,
        )

    def from_items(values):
        return jnp.concatenate(
            stack(
                values[:, :pre_rows].reshape(count, -1),
                values[:, pre_rows:].reshape(act_count, -1),
            ),
            axis=0,
        )

    normed = spread(
        *stack(
            rms_norm(pre_x, pre_attn_gain).astype(BF16),
            rms_norm(act_x, act_attn_gain).astype(BF16),
        ),
        order,
    )
    keyval_raw = to_items(mm(normed, qkv_full[:, query_width:]))
    keyval_rows = jnp.concatenate(
        [rotate(keyval_raw[..., :head_dim], cosine_tab, sine_tab), keyval_raw[..., head_dim:]],
        axis=-1,
    ).astype(BF16)
    all_keyval = jnp.concatenate(ring_gather(keyval_rows), axis=1)
    key_rows = all_keyval[..., :head_dim]
    value_rows = all_keyval[..., head_dim:]
    query_raw = to_items(mm(normed, qkv_full[:, :query_width]))
    query_rows = rotate(
        query_raw.reshape(items, local_len, heads, head_dim),
        cosine_tab[:, None, :],
        sine_tab[:, None, :],
    ).astype(BF16)
    scores = (
        jnp.einsum("iqhd,ikd->ihqk", query_rows, key_rows, preferred_element_type=F32) * scale
    )
    probs = jax.nn.softmax(jnp.where(allowed, scores, MASKED), axis=-1)
    probs_low = probs.astype(BF16)
    attended = jnp.einsum("ihqk,ikd->iqhd", probs_low, value_rows, preferred_element_type=F32)
    attended = attended.astype(BF16).reshape(items, local_len, query_width)
    (att_joint,) = permute_columns([from_items(attended)], order)
    mid = mm(att_joint, out_full)
    pre_mid = pre_x + mid[:count, :width]
    act_mid = act_x + mid[padded : padded + act_count, width:]

    act_second = rms_norm(act_mid, act_mlp_gain).astype(BF16)
    act_all_rows = jnp.concatenate(ring_gather(act_second, LOOSE), axis=0)
    slot_count = lax.dynamic_index_in_dim(hidden_counts, member, keepdims=False)
    slot_live = (jnp.arange(act_gate.shape[1]) < slot_count).astype(F32)

    def scatter_sum(value, dimension):
        return lax.psum_scatter(value, "dp", scatter_dimension=dimension, tiled=True)

    def split(partial):
        size = partial.shape[0] // groups
        return [partial[r * size : (r + 1) * size] for r in range(groups)]

    act_hidden, act_gate_back, act_up_back = feed_forward(
        act_all_rows, act_cot_all, act_gate_full, act_up_full, act_down_full, slot_live
    )
    act_terms = [
        mm_tn(act_all_rows, act_gate_back).astype(BF16),
        mm_tn(act_all_rows, act_up_back).astype(BF16),
        mm_tn(act_cot_all, act_hidden).astype(BF16),
    ]
    act_second_part = split(mm_nt(act_gate_back, act_gate_full) + mm_nt(act_up_back, act_up_full))
    act_sum_part = split(mm_nt(act_hidden, act_down_full))

    pre_second = pad(rms_norm(pre_mid, pre_mlp_gain).astype(BF16))
    second_pieces = [pre_second]
    for r in range(1, groups):
        piece = ring(second_pieces[-1], 1)
        if r == 1:
            piece, hidden_back = lax.optimization_barrier((piece, hidden_back))
        if r == groups - 1:
            piece, act_terms = lax.optimization_barrier((piece, act_terms))
        second_pieces.append(piece)
    act_stacked = jnp.concatenate(
        [term.reshape(ways, -1, act_gate.shape[1]) for term in act_terms], axis=1
    ).reshape(-1, act_gate.shape[1])
    grad_act = scatter_sum(act_stacked, 0)
    grad_act = grad_act.astype(F32).reshape(3, -1, act_gate.shape[1])
    grad_act_gate, grad_act_up, grad_act_down = grad_act[0], grad_act[1], grad_act[2].T

    pre_hidden, pre_gate_back, pre_up_back, pre_all = feed_forward_kernel(
        second_pieces, hidden_back, gate_full, up_full
    )
    gate_term = mm_tn(pre_all, pre_gate_back).astype(BF16)
    gate_term, pre_up_back = lax.optimization_barrier((gate_term, pre_up_back))
    grad_pre_gate = scatter_sum(gate_term, 0)
    half = groups // 2 * padded

    def second_rows(cut, gate_rows, up_rows):
        return mm_nt(gate_rows[cut], gate_full) + mm_nt(up_rows[cut], up_full)

    later = second_rows(slice(half, None), pre_gate_back, pre_up_back)
    later, gate_rows, up_rows = lax.optimization_barrier((later, pre_gate_back, pre_up_back))
    sooner = second_rows(slice(0, half), gate_rows, up_rows)

    act_lines = act_count * act_width // width

    def pack(pre_part_rows, act_part_rows):
        return jnp.concatenate([pre_part_rows, act_part_rows.reshape(act_lines, width)], axis=0)

    def unpack(packed):
        return packed[:count], packed[count:].reshape(act_count, act_width)

    def second_part(r):
        rows = sooner if r < groups // 2 else later
        return pack(rows[r % (groups // 2) * padded :][:count], act_second_part[r])

    up_term = down_term = None
    total = second_part(groups - 1)
    for r in range(groups - 2, -1, -1):
        moved = ring(total.astype(BF16), -1, LOOSE)
        if r == groups - 2:
            moved, up_rows = lax.optimization_barrier((moved, after(up_rows, sooner)))
            up_term = mm_tn(pre_all, up_rows).astype(BF16)
        elif r == groups - 3:
            moved, up_term, pre_hidden = lax.optimization_barrier((moved, up_term, pre_hidden))
            down_term = mm_tn(pre_hidden, cot_all).astype(BF16)
        elif r == groups - 4:
            moved, down_term = lax.optimization_barrier((moved, down_term))
        total = moved.astype(F32) + second_part(r)
    grad_pre_up = scatter_sum(up_term, 0)
    grad_pre_down = scatter_sum(down_term, 1)
    pre_second_back, act_second_back = unpack(total)

    pre_mid_part, grad_pre_mlp_gain = rms_back(pre_mid, pre_mlp_gain, pre_second_back)
    act_mid_part, grad_act_mlp_gain = rms_back(act_mid, act_mlp_gain, act_second_back)
    pre_mid_grad = cot_flat.astype(F32) + pre_mid_part
    act_mid_grad = act_final_back + act_mid_part
    back_joint = jnp.concatenate(
        [
            jnp.pad(pre_mid_grad.astype(BF16), ((0, padded - count), (0, act_width))),
            jnp.pad(act_mid_grad.astype(BF16), ((0, act_padded - act_count), (width, 0))),
        ],
        axis=0,
    )
    attended_back = to_items(
        permute_columns([mm_nt(back_joint, out_full).astype(BF16)], order, True)[0]
    ).reshape(items, local_len, heads, head_dim)
    out_half = query_width // 2
    grad_out = scatter_rows(
        mm_tn(att_joint[:, :out_half], back_joint).astype(BF16),
        mm_tn(att_joint[:, out_half:], back_joint).astype(BF16),
        (out_part,),
    )
    probs_back = jnp.einsum(
        "iqhd,ikd->ihqk", attended_back, value_rows, preferred_element_type=F32
    )
    value_back = jnp.einsum(
        "ihqk,iqhd->ikd", probs_low, attended_back, preferred_element_type=F32
    )
    scores_back = (
        probs * (probs_back - jnp.sum(probs * probs_back, axis=-1, keepdims=True))
    ).astype(BF16)
    key_back = (
        jnp.einsum("ihqk,iqhd->ikd", scores_back, query_rows, preferred_element_type=F32) * scale
    )
    query_back = (
        jnp.einsum("ihqk,ikd->iqhd", scores_back, key_rows, preferred_element_type=F32) * scale
    )
    keyval_back = jnp.concatenate([key_back, value_back], axis=-1).astype(BF16)
    keyval_back, pre_hidden = lax.optimization_barrier((keyval_back, pre_hidden))
    pre_sum_part = split(mm(pre_hidden, down_full))
    pre_sums, act_sums = unpack(
        ring_scatter([pack(each[:count], rest) for each, rest in zip(pre_sum_part, act_sum_part)])
    )
    own_kv_back = ring_scatter(
        [keyval_back[:, r * local_len : (r + 1) * local_len] for r in range(groups)]
    )
    keyval_low = jnp.concatenate(
        [rotate(own_kv_back[..., :head_dim], cosine_tab, -sine_tab), own_kv_back[..., head_dim:]],
        axis=-1,
    ).astype(BF16)
    query_low = rotate(query_back, cosine_tab[:, None, :], -sine_tab[:, None, :])
    query_low = query_low.reshape(items, local_len, query_width).astype(BF16)
    back_rows = from_items(jnp.concatenate([query_low, keyval_low], axis=-1))
    back_rows, grad_pre_gate = lax.optimization_barrier((back_rows, grad_pre_gate))
    qkv_half = normed.shape[1] // 2
    grad_qkv = scatter_rows(
        mm_tn(normed[:, :qkv_half], back_rows).astype(BF16),
        mm_tn(normed[:, qkv_half:], back_rows).astype(BF16),
        (pre_part, act_part),
    )

    prefix_out = (pre_mid + pre_sums).astype(BF16).reshape(prefix_tokens.shape)
    act_final_low = (act_mid + act_sums).astype(BF16)
    action_pred = mm(act_final_low, action_head).reshape(pred_cot.shape) * live_mask
    grad_head = mm_tn(act_final_low, pred_back)

    pre_normed_back, act_normed_back = unspread(
        mm_nt(back_rows, qkv_full), padded, width, act_width, order
    )
    pre_normed_back, act_normed_back = pre_normed_back[:count], act_normed_back[:act_count]
    pre_x_part, grad_pre_attn_gain = rms_back(pre_x, pre_attn_gain, pre_normed_back)
    act_x_part, grad_act_attn_gain = rms_back(act_x, act_attn_gain, act_normed_back)
    prefix_grad = (pre_mid_grad + pre_x_part).reshape(prefix_tokens.shape)
    action_grad = (act_mid_grad + act_x_part).reshape(action_tokens.shape)

    devices = ways * groups
    small = jnp.concatenate(
        [
            value.reshape(devices, -1)
            for value in (
                grad_pre_attn_gain,
                grad_pre_mlp_gain,
                grad_act_attn_gain,
                grad_act_mlp_gain,
                grad_head,
            )
        ],
        axis=1,
    )
    bit = 1
    while bit < ways:
        small = small + hop(small, bit)
        bit *= 2
    mine = lax.axis_index("dp") * groups
    terms = [
        lax.dynamic_slice_in_dim(small, mine + (member - r) % groups, 1, 0) for r in range(groups)
    ]
    total = terms[-1]
    for term in terms[-2::-1]:
        total = ring(total, -1, LOOSE) + term
    sizes = [width // devices] * 2 + [act_width // devices] * 2
    gains, start = [], 0
    for size in sizes:
        gains.append(total[0, start : start + size])
        start += size
    grad_head = total[0, start:].reshape(act_width // devices, -1)

    return (
        prefix_out,
        action_pred,
        prefix_grad,
        action_grad,
        *gains,
        grad_qkv[:pre_part, :query_width],
        grad_qkv[:pre_part, query_width:],
        grad_out[:, :width],
        grad_qkv[pre_part:, :query_width],
        grad_qkv[pre_part:, query_width:],
        grad_out[:, width:],
        grad_pre_gate.astype(F32),
        grad_pre_up.astype(F32),
        grad_pre_down.astype(F32),
        grad_act_gate,
        grad_act_up,
        grad_act_down,
        grad_head,
    )


def solution(mesh):
    rows = P("dp", "mp", None)
    both = P(("dp", "mp"), None)
    wide = P("dp", "mp")
    tall = P("mp", "dp")
    in_specs = (
        (rows, rows, P("dp", None), P("dp", None))
        + (P(),) * 5
        + (both,) * 6
        + (wide, wide, tall, wide, wide, tall, P(), rows, rows)
    )
    out_specs = (
        (rows,) * 4
        + (P(("dp", "mp")),) * 4
        + (both,) * 6
        + (wide, wide, tall, wide, wide, tall, both)
    )
    return jax.shard_map(shards, mesh=mesh, in_specs=in_specs, out_specs=out_specs, check_vma=False)
```

```python
import functools

import jax
import jax.numpy as jnp
from jax import lax
from jax.experimental import pallas as pl
from jax.experimental.pallas import tpu as pltpu
from jax.sharding import PartitionSpec as P

NORM_EPS = 1e-06
ROPE_BASE = 10000.0
MASKED = -1e30
F32 = jnp.float32
BF16 = jnp.bfloat16


class Links:
    def __init__(self, window=2):
        self.window = window
        self.done = {}

    def send(self, value, axis, pairs, link):
        sent = self.done.setdefault(link, [])
        if len(sent) >= self.window:
            value, _ = lax.optimization_barrier((value, sent[-self.window]))
        result = lax.ppermute(value, axis, pairs)
        sent.append(result)
        return result


LINKS = Links()


def hop(value, bit):
    size = lax.axis_size("dp")
    pairs = [(d, d ^ bit) for d in range(size)]
    if bit == 1:
        return lax.ppermute(value, "dp", pairs)
    return LINKS.send(value, "dp", pairs, bit)


LOOSE = None


def ring(value, step, link="mp"):
    size = lax.axis_size("mp")
    pairs = [(d, (d + step) % size) for d in range(size)]
    if link is LOOSE:
        return lax.ppermute(value, "mp", pairs)
    return LINKS.send(value, "mp", pairs, link)


def ring_gather(value, link="mp"):
    out = [value]
    for _ in range(lax.axis_size("mp") - 1):
        out.append(ring(out[-1], 1, link))
    return out


def ring_scatter(parts, steps=None):
    total = parts[-1].astype(BF16)
    for part in parts[-2::-1]:
        moved = ring(total.astype(BF16), -1, LOOSE)
        if steps is not None:
            steps.append(moved)
        total = moved.astype(F32) + part.astype(F32)
    return total


def chip_order(size):
    return sorted(range(1, size), key=lambda c: (bin(c).count("1"), c))


def rel_blocks():
    size = lax.axis_size("dp")
    place = jnp.arange(size, dtype=jnp.int32)
    half = size // 2
    rel = (place % half) * 2 + place // half
    return jnp.bitwise_xor(rel, lax.axis_index("dp").astype(jnp.int32))


def dp_gather(shard):
    chips = lax.axis_size("dp") // 2
    half = shard.shape[0] // 2
    got = {0: [shard]}

    def top(c):
        return got[c][0] if len(got[c]) == 2 else got[c][0][:half]

    def bottom(c):
        return got[c][1] if len(got[c]) == 2 else got[c][0][half:]

    for c in chip_order(chips):
        high, low = 1 << (c.bit_length() - 1), c & -c
        if high == low:
            got[c] = [hop(shard, 2 * high)]
        else:
            got[c] = [hop(top(c ^ high), 2 * high), hop(bottom(c ^ low), 2 * low)]
    own = [piece for c in range(chips) for piece in got[c]]
    return own + [hop(piece, 1) for piece in own]


def chip_sums(own, other):
    chips = lax.axis_size("dp") // 2
    total = own.astype(F32) + hop(other, 1).astype(F32)
    return total.reshape(chips, -1, own.shape[1])


def send_blocks(blocks):
    size = lax.axis_size("dp")
    return [
        lax.ppermute(blocks[c].astype(BF16), "dp", [(d, d ^ (2 * c)) for d in range(size)])
        for c in range(1, size // 2)
    ]


def add_up(first, arrived):
    total = first
    for each in arrived:
        total = total + each.astype(F32)
    return total


def member_parts(values, layout):
    groups = lax.axis_size("mp")
    axis = values.ndim - 2
    parts = []
    for r in range(groups):
        which = (lax.axis_index("mp") - r) % groups
        cuts, start = [], 0
        for part in layout:
            cuts.append(lax.dynamic_slice_in_dim(values, start + which * part, part, axis))
            start += groups * part
        parts.append(jnp.concatenate(cuts, axis=axis))
    return parts


def _permute_blocks(inverse, order, *refs):
    half = len(refs) // 2
    for src, dst in zip(refs[:half], refs[half:]):
        block = src.shape[1] // order.shape[0]
        for g in range(order.shape[0]):
            here = slice(g * block, (g + 1) * block)
            there = pl.ds(pl.multiple_of(order[g] * block, block), block)
            if inverse:
                dst[:, there] = src[:, here]
            else:
                dst[:, here] = src[:, there]


def permute_columns(arrays, order, inverse=False):
    count = order.shape[0]
    if any(values.shape[1] // count % 128 for values in arrays):
        hit = order[:, None] == jnp.arange(count, dtype=order.dtype)[None, :]
        places = jnp.arange(count, dtype=order.dtype)
        back = jnp.sum(jnp.where(hit, places[:, None], 0), axis=0) if inverse else order
        outs = []
        for values in arrays:
            split = values.reshape(values.shape[0], count, -1)
            cuts = [lax.dynamic_slice_in_dim(split, back[g], 1, 1) for g in range(count)]
            outs.append(jnp.concatenate(cuts, axis=1).reshape(values.shape))
        return outs
    return pl.pallas_call(
        functools.partial(_permute_blocks, inverse),
        in_specs=[pl.BlockSpec(memory_space=pltpu.SMEM)]
        + [pl.BlockSpec(memory_space=pltpu.VMEM)] * len(arrays),
        out_specs=[pl.BlockSpec(memory_space=pltpu.VMEM)] * len(arrays),
        out_shape=[jax.ShapeDtypeStruct(values.shape, values.dtype) for values in arrays],
        compiler_params=pltpu.CompilerParams(vmem_limit_bytes=32 * 2**20),
    )(order, *arrays)


def _spread(count, order, pre, act, joint):
    rows = pre.shape[0]
    narrow = [value.shape[1] // count for value in (pre, act)]
    joint[...] = jnp.zeros_like(joint)
    for g in range(count):
        start = g * sum(narrow)
        there = pl.ds(pl.multiple_of(order[g] * narrow[0], narrow[0]), narrow[0])
        joint[:rows, start : start + narrow[0]] = pre[:, there]
        there = pl.ds(pl.multiple_of(order[g] * narrow[1], narrow[1]), narrow[1])
        joint[rows:, start + narrow[0] : start + sum(narrow)] = act[:, there]


def block_call(body, order, arrays, shapes):
    return pl.pallas_call(
        functools.partial(body, order.shape[0]),
        in_specs=[pl.BlockSpec(memory_space=pltpu.SMEM)]
        + [pl.BlockSpec(memory_space=pltpu.VMEM)] * len(arrays),
        out_specs=[pl.BlockSpec(memory_space=pltpu.VMEM)] * len(shapes),
        out_shape=shapes,
        compiler_params=pltpu.CompilerParams(vmem_limit_bytes=32 * 2**20),
    )(order, *arrays)


def spread(pre, act, order):
    count = order.shape[0]
    rows, lines = pre.shape[0], act.shape[0]
    wide, thin = pre.shape[1] // count, act.shape[1] // count
    if wide % 128 or thin % 128:
        upper, lower = permute_columns([pre, act], order)
        upper = jnp.pad(upper.reshape(rows, count, wide), ((0, lines), (0, 0), (0, thin)))
        lower = jnp.pad(lower.reshape(lines, count, thin), ((rows, 0), (0, 0), (wide, 0)))
        return (upper + lower).reshape(rows + lines, -1)
    shape = jax.ShapeDtypeStruct((rows + lines, pre.shape[1] + act.shape[1]), pre.dtype)
    return block_call(_spread, order, [pre, act], [shape])[0]


def inverse_rms(values):
    return lax.rsqrt(jnp.mean(values * values, axis=-1, keepdims=True) + NORM_EPS)


def rms_norm(values, gain_vec):
    return values * inverse_rms(values) * gain_vec


def rms_back(values, gain_vec, grads):
    inverse = inverse_rms(values)
    unit = values * inverse
    scaled = gain_vec * grads
    mean = jnp.mean(unit * scaled, axis=-1, keepdims=True)
    return inverse * (scaled - unit * mean), jnp.sum(grads * unit, axis=0)


def rope_tables(positions, head_dim):
    half_dim = head_dim // 2
    inverse = ROPE_BASE ** (-2.0 * jnp.arange(half_dim).astype(F32) / head_dim)
    angles = positions.astype(F32)[:, None] * inverse[None, :]
    return (jnp.cos(angles), jnp.sin(angles))


def rotate(values, cosine_tab, sine_tab):
    half_dim = values.shape[-1] // 2
    lower_half = values[..., :half_dim]
    upper_half = values[..., half_dim:]
    return jnp.concatenate(
        [
            lower_half * cosine_tab - upper_half * sine_tab,
            upper_half * cosine_tab + lower_half * sine_tab,
        ],
        axis=-1,
    )


def mm(left, right):
    return lax.dot_general(left, right, (((1,), (0,)), ((), ())), preferred_element_type=F32)


def mm_nt(left, right):
    return lax.dot_general(left, right, (((1,), (1,)), ((), ())), preferred_element_type=F32)


def mm_tn(left, right):
    return lax.dot_general(left, right, (((0,), (0,)), ((), ())), preferred_element_type=F32)


def geglu(gate_val, up_val, live_mask):
    return jax.nn.gelu(gate_val, approximate=True) * up_val * live_mask


def feed_forward(rows, cot_rows, gate, up, down_t, live_mask):
    gate_val = mm(rows, gate)
    up_val = mm(rows, up)
    hidden_back = mm(cot_rows, down_t)
    hidden, pull = jax.vjp(lambda g, u: geglu(g, u, live_mask), gate_val, up_val)
    gate_back, up_back = pull(hidden_back)
    return hidden.astype(BF16), gate_back.astype(BF16), up_back.astype(BF16)


def _feed_forward_tile(groups, *refs):
    pieces, (back_ref, gate_ref, up_ref) = refs[:groups], refs[groups : groups + 3]
    hidden_ref, gate_back_ref, up_back_ref, rows_ref = refs[groups + 3 :]
    count = pieces[0].shape[0]
    root, cube = 0.7978845608028654, 0.044715

    @pl.when(pl.program_id(0) == 0)
    def _():
        for r in range(groups):
            rows_ref[r * count : (r + 1) * count, :] = pieces[r][...]

    for r in range(groups):
        cut = slice(r * count, (r + 1) * count)
        rows = pieces[r][...]
        gate_val = jnp.dot(rows, gate_ref[...], preferred_element_type=F32)
        up_val = jnp.dot(rows, up_ref[...], preferred_element_type=F32)
        back = back_ref[cut, :].astype(F32)
        square = gate_val * gate_val
        bend = jnp.tanh(root * gate_val * (1.0 + cube * square))
        half_open = 0.5 * (1.0 + bend)
        active = gate_val * half_open
        inner = (0.5 * root) * gate_val * (1.0 - bend * bend) * (1.0 + 3.0 * cube * square)
        hidden_ref[cut, :] = (active * up_val).astype(BF16)
        gate_back_ref[cut, :] = (back * up_val * (half_open + inner)).astype(BF16)
        up_back_ref[cut, :] = (back * active).astype(BF16)


def feed_forward_kernel(pieces, hidden_back, gate, up, tile=512):
    groups = len(pieces)
    count, width = pieces[0].shape
    total = groups * count
    units = gate.shape[1]
    block = pl.BlockSpec((total, tile), lambda n: (0, n))
    weight = pl.BlockSpec((width, tile), lambda n: (0, n))
    fixed = pl.BlockSpec((count, width), lambda n: (0, 0), pipeline_mode=pl.Buffered(1))
    return pl.pallas_call(
        functools.partial(_feed_forward_tile, groups),
        grid=(units // tile,),
        in_specs=[fixed] * groups + [block, weight, weight],
        out_specs=[block] * 3 + [pl.BlockSpec((total, width), lambda n: (0, 0))],
        out_shape=[jax.ShapeDtypeStruct((total, units), BF16)] * 3
        + [jax.ShapeDtypeStruct((total, width), BF16)],
        compiler_params=pltpu.CompilerParams(vmem_limit_bytes=56 * 2**20),
        cost_estimate=pl.CostEstimate(
            flops=4 * total * width * units,
            bytes_accessed=4 * width * units + 8 * total * units + 4 * total * width,
            transcendentals=total * units,
        ),
    )(*pieces, hidden_back, gate, up)


def after(value, *first):
    return lax.optimization_barrier((value, *first))[0]


def shards(
    prefix_tokens,
    action_tokens,
    block_ids,
    live_dims,
    hidden_counts,
    pre_attn_gain,
    pre_mlp_gain,
    act_attn_gain,
    act_mlp_gain,
    pre_query,
    pre_keyval,
    pre_output,
    act_query,
    act_keyval,
    act_output,
    pre_gate,
    pre_up,
    pre_down,
    act_gate,
    act_up,
    act_down,
    action_head,
    prefix_cot,
    pred_cot,
):
    groups = lax.axis_size("mp")
    ways = lax.axis_size("dp")
    member = lax.axis_index("mp")
    items, pre_rows, width = prefix_tokens.shape
    act_rows, act_width = action_tokens.shape[1:]
    pre_len = pre_rows * groups
    head_dim = pre_keyval.shape[1] // 2
    query_width = pre_query.shape[1]
    heads = query_width // head_dim
    local_len = pre_rows + act_rows
    scale = head_dim ** (-0.5)
    order = rel_blocks()
    LINKS.done.clear()

    pre_part, act_part, out_part = pre_query.shape[0], act_query.shape[0], pre_output.shape[0]
    qkv_own = jnp.concatenate(
        [
            jnp.concatenate([pre_query, pre_keyval], axis=1),
            jnp.concatenate([act_query, act_keyval], axis=1),
        ],
        axis=0,
    )
    qkv_full = lax.all_gather(qkv_own, ("dp", "mp"), axis=0, tiled=True)
    act_stack = jnp.concatenate([act_gate, act_up, act_down.T], axis=0)
    def in_place(pieces):
        size = pieces[0].shape[0]
        twice = jnp.concatenate(pieces[::-1] * 2, axis=0)
        return lax.dynamic_slice_in_dim(twice, (groups - 1 - member) * size, groups * size, 0)

    out_ring = ring_gather(jnp.concatenate([pre_output, act_output], axis=1))
    out_block = in_place(out_ring)
    qkv_full, act_stack, out_block = lax.optimization_barrier((qkv_full, act_stack, out_block))
    out_full = jnp.concatenate(dp_gather(out_block), axis=0)
    qkv_full = qkv_full.reshape(ways * groups, -1, qkv_own.shape[1])
    pre_qkv = qkv_full[:, :pre_part].reshape(width, -1)
    act_qkv = qkv_full[:, pre_part:].reshape(act_width, -1)
    act_flat_w = lax.all_gather(act_stack, "dp", axis=0, tiled=True)
    act_all = act_flat_w.reshape(ways, 3, -1, act_gate.shape[1])
    act_gate_full, act_up_full, act_down_full = (
        act_all[:, n].reshape(act_width, -1) for n in range(3)
    )

    pre_flat = prefix_tokens.reshape(items * pre_rows, width)
    act_flat = action_tokens.reshape(items * act_rows, act_width)
    cot_flat = prefix_cot.reshape(items * pre_rows, width)
    pre_x = pre_flat.astype(F32)
    act_x = act_flat.astype(F32)
    live_mask = live_dims[:, None, :].astype(F32)
    pred_back = (pred_cot * live_mask).astype(BF16).reshape(items * act_rows, -1)
    act_final_back = mm_nt(pred_back, action_head)
    count = items * pre_rows
    padded = -(-count // 16) * 16
    act_count = items * act_rows

    def pad(values):
        return jnp.pad(values, ((0, padded - count), (0, 0)))

    def ring_stack(value):
        return jnp.concatenate(ring_gather(value), axis=0)

    local_pos = jnp.concatenate(
        [
            member * pre_rows + jnp.arange(pre_rows),
            pre_len + member * act_rows + jnp.arange(act_rows),
        ]
    )
    cosine_tab, sine_tab = rope_tables(local_pos, head_dim)

    def blocks_of(which):
        return jnp.concatenate(
            [
                lax.dynamic_slice_in_dim(block_ids, which * pre_rows, pre_rows, 1),
                lax.dynamic_slice_in_dim(block_ids, pre_len + which * act_rows, act_rows, 1),
            ],
            axis=1,
        )

    local_blocks = blocks_of(member)
    key_blocks = jnp.concatenate(
        [blocks_of((member - r) % groups) for r in range(groups)], axis=1
    )
    allowed = key_blocks[:, None, None, :] <= local_blocks[:, None, :, None]

    act_padded = -(-act_count // 16) * 16

    def stack(pre_part_rows, act_part_rows):
        return (
            jnp.pad(pre_part_rows, ((0, padded - count), (0, 0))),
            jnp.pad(act_part_rows, ((0, act_padded - act_count), (0, 0))),
        )

    def to_items(joint):
        return jnp.concatenate(
            [
                joint[:count].reshape(items, pre_rows, -1),
                joint[padded : padded + act_count].reshape(items, act_rows, -1),
            ],
            axis=1,
        )

    def from_items(values):
        return jnp.concatenate(
            stack(
                values[:, :pre_rows].reshape(count, -1),
                values[:, pre_rows:].reshape(act_count, -1),
            ),
            axis=0,
        )

    pre_normed, act_normed = stack(
        rms_norm(pre_x, pre_attn_gain).astype(BF16), rms_norm(act_x, act_attn_gain).astype(BF16)
    )
    normed = spread(pre_normed, act_normed, order)

    def project(columns):
        return to_items(
            jnp.concatenate(
                [mm(pre_normed, pre_qkv[:, columns]), mm(act_normed, act_qkv[:, columns])], axis=0
            )
        )

    keyval_raw = project(slice(query_width, None))
    keyval_rows = jnp.concatenate(
        [rotate(keyval_raw[..., :head_dim], cosine_tab, sine_tab), keyval_raw[..., head_dim:]],
        axis=-1,
    ).astype(BF16)
    keyval_rows, gate_own, up_own, down_own = lax.optimization_barrier(
        (keyval_rows, pre_gate, pre_up, pre_down)
    )
    down_full = lax.all_gather(down_own, "dp", axis=1, tiled=True)
    gate_full = lax.all_gather(gate_own, "dp", axis=0, tiled=True)
    up_full = lax.all_gather(up_own, "dp", axis=0, tiled=True)
    all_keyval = jnp.concatenate(ring_gather(keyval_rows), axis=1)
    cot_all = ring_stack(pad(cot_flat))
    act_cot_all = ring_stack(act_final_back.astype(BF16))
    hidden_back = mm_nt(cot_all, down_full).astype(BF16)
    key_rows = all_keyval[..., :head_dim]
    value_rows = all_keyval[..., head_dim:]
    query_raw = project(slice(0, query_width))
    query_rows = rotate(
        query_raw.reshape(items, local_len, heads, head_dim),
        cosine_tab[:, None, :],
        sine_tab[:, None, :],
    ).astype(BF16)
    scores = (
        jnp.einsum("iqhd,ikd->ihqk", query_rows, key_rows, preferred_element_type=F32) * scale
    )
    probs = jax.nn.softmax(jnp.where(allowed, scores, MASKED), axis=-1)
    probs_low = probs.astype(BF16)
    attended = jnp.einsum("ihqk,ikd->iqhd", probs_low, value_rows, preferred_element_type=F32)
    attended = attended.astype(BF16).reshape(items, local_len, query_width)
    (att_joint,) = permute_columns([from_items(attended)], order)
    mid = mm(att_joint, out_full)
    pre_mid = pre_x + mid[:count, :width]
    act_mid = act_x + mid[padded : padded + act_count, width:]

    act_second = rms_norm(act_mid, act_mlp_gain).astype(BF16)
    act_all_rows = jnp.concatenate(ring_gather(act_second, LOOSE), axis=0)
    slot_count = lax.dynamic_index_in_dim(hidden_counts, member, keepdims=False)
    slot_live = (jnp.arange(act_gate.shape[1]) < slot_count).astype(F32)

    def scatter_sum(value, dimension):
        return lax.psum_scatter(value, "dp", scatter_dimension=dimension, tiled=True)

    def split(partial):
        size = partial.shape[0] // groups
        return [partial[r * size : (r + 1) * size] for r in range(groups)]

    act_hidden, act_gate_back, act_up_back = feed_forward(
        act_all_rows, act_cot_all, act_gate_full, act_up_full, act_down_full, slot_live
    )
    act_terms = [
        mm_tn(act_all_rows, act_gate_back).astype(BF16),
        mm_tn(act_all_rows, act_up_back).astype(BF16),
        mm_tn(act_cot_all, act_hidden).astype(BF16),
    ]
    act_second_part = split(mm_nt(act_gate_back, act_gate_full) + mm_nt(act_up_back, act_up_full))
    act_sum_part = split(mm_nt(act_hidden, act_down_full))

    act_stacked = jnp.concatenate(
        [term.reshape(ways, -1, act_gate.shape[1]) for term in act_terms], axis=1
    ).reshape(-1, act_gate.shape[1])
    pre_second = pad(rms_norm(pre_mid, pre_mlp_gain).astype(BF16))
    second_pieces = [pre_second]
    for r in range(1, groups):
        piece = ring(second_pieces[-1], 1)
        if r == 1:
            piece, hidden_back = lax.optimization_barrier((piece, hidden_back))
        if r == groups - 1:
            piece, act_stacked = lax.optimization_barrier((piece, act_stacked))
        second_pieces.append(piece)
    grad_act = scatter_sum(act_stacked, 0)
    grad_act = grad_act.astype(F32).reshape(3, -1, act_gate.shape[1])
    grad_act_gate, grad_act_up, grad_act_down = grad_act[0], grad_act[1], grad_act[2].T

    pre_hidden, pre_gate_back, pre_up_back, pre_all = feed_forward_kernel(
        second_pieces, hidden_back, gate_full, up_full
    )
    gate_term = mm_tn(pre_all, pre_gate_back).astype(BF16)
    gate_term, pre_up_back = lax.optimization_barrier((gate_term, pre_up_back))
    grad_pre_gate = scatter_sum(gate_term, 0)
    half = groups // 2 * padded

    def second_rows(cut, gate_rows, up_rows):
        return mm_nt(gate_rows[cut], gate_full) + mm_nt(up_rows[cut], up_full)

    later = second_rows(slice(half, None), pre_gate_back, pre_up_back)
    later, gate_rows, up_rows = lax.optimization_barrier((later, pre_gate_back, pre_up_back))
    sooner = second_rows(slice(0, half), gate_rows, up_rows)

    act_lines = act_count * act_width // width

    def lines(value):
        return value.reshape(act_lines, width)

    def second_part(r):
        rows = sooner if r < groups // 2 else later
        rows = rows[r % (groups // 2) * padded :][:count]
        return jnp.concatenate([rows, lines(act_second_part[r]), lines(act_sum_part[r])], axis=0)

    up_term = down_term = None
    total = second_part(groups - 1)
    for r in range(groups - 2, -1, -1):
        moved = ring(total.astype(BF16), -1, LOOSE)
        if r == groups - 2:
            moved, up_rows = lax.optimization_barrier((moved, after(up_rows, sooner)))
            up_term = mm_tn(pre_all, up_rows).astype(BF16)
        elif r == groups - 3:
            moved, up_term, pre_hidden = lax.optimization_barrier((moved, up_term, pre_hidden))
            down_term = mm_tn(pre_hidden, cot_all).astype(BF16)
        elif r == groups - 4:
            moved, down_term = lax.optimization_barrier((moved, down_term))
        total = moved.astype(F32) + second_part(r)
    grad_pre_up = scatter_sum(up_term, 0)
    grad_pre_down = scatter_sum(down_term, 1)
    pre_second_back = total[:count]
    act_second_back = total[count : count + act_lines].reshape(act_count, act_width)
    act_sums = total[count + act_lines :].reshape(act_count, act_width)

    pre_mid_part, grad_pre_mlp_gain = rms_back(pre_mid, pre_mlp_gain, pre_second_back)
    act_mid_part, grad_act_mlp_gain = rms_back(act_mid, act_mlp_gain, act_second_back)
    pre_mid_grad = cot_flat.astype(F32) + pre_mid_part
    act_mid_grad = act_final_back + act_mid_part
    back_joint = jnp.concatenate(
        [
            jnp.pad(pre_mid_grad.astype(BF16), ((0, padded - count), (0, act_width))),
            jnp.pad(act_mid_grad.astype(BF16), ((0, act_padded - act_count), (width, 0))),
        ],
        axis=0,
    )
    attended_back = to_items(
        permute_columns([mm_nt(back_joint, out_full).astype(BF16)], order, True)[0]
    ).reshape(items, local_len, heads, head_dim)
    out_half = query_width // 2
    out_sums = chip_sums(
        mm_tn(att_joint[:, :out_half], back_joint).astype(BF16),
        mm_tn(att_joint[:, out_half:], back_joint).astype(BF16),
    )
    out_sums = ring_scatter(member_parts(out_sums, (out_part,)))
    grad_out = add_up(out_sums[0], send_blocks(out_sums))
    probs_back = jnp.einsum(
        "iqhd,ikd->ihqk", attended_back, value_rows, preferred_element_type=F32
    )
    value_back = jnp.einsum(
        "ihqk,iqhd->ikd", probs_low, attended_back, preferred_element_type=F32
    )
    scores_back = (
        probs * (probs_back - jnp.sum(probs * probs_back, axis=-1, keepdims=True))
    ).astype(BF16)
    key_back = (
        jnp.einsum("ihqk,iqhd->ikd", scores_back, query_rows, preferred_element_type=F32) * scale
    )
    query_back = (
        jnp.einsum("ihqk,ikd->iqhd", scores_back, key_rows, preferred_element_type=F32) * scale
    )
    keyval_back = jnp.concatenate([key_back, value_back], axis=-1).astype(BF16)
    own_kv_back = ring_scatter(
        [keyval_back[:, r * local_len : (r + 1) * local_len] for r in range(groups)]
    )
    keyval_low = jnp.concatenate(
        [rotate(own_kv_back[..., :head_dim], cosine_tab, -sine_tab), own_kv_back[..., head_dim:]],
        axis=-1,
    ).astype(BF16)
    query_low = rotate(query_back, cosine_tab[:, None, :], -sine_tab[:, None, :])
    query_low = query_low.reshape(items, local_len, query_width).astype(BF16)
    back_rows = from_items(jnp.concatenate([query_low, keyval_low], axis=-1))
    back_rows, grad_pre_gate = lax.optimization_barrier((back_rows, grad_pre_gate))
    qkv_half = normed.shape[1] // 2
    qkv_own_part = mm_tn(normed[:, :qkv_half], back_rows).astype(BF16)
    qkv_other_part = mm_tn(normed[:, qkv_half:], back_rows).astype(BF16)
    qkv_sums = chip_sums(qkv_own_part, qkv_other_part).astype(BF16)
    qkv_sums, pre_hidden = lax.optimization_barrier((qkv_sums, pre_hidden))
    arrived = send_blocks(qkv_sums)
    act_final_low = (act_mid + act_sums).astype(BF16)
    action_pred = mm(act_final_low, action_head).reshape(pred_cot.shape) * live_mask
    grad_head = mm_tn(act_final_low, pred_back)
    pre_normed_back = mm_nt(back_rows[:padded], pre_qkv)[:count]
    act_normed_back = mm_nt(back_rows[padded:], act_qkv)[:act_count]
    pre_x_part, grad_pre_attn_gain = rms_back(pre_x, pre_attn_gain, pre_normed_back)
    act_x_part, grad_act_attn_gain = rms_back(act_x, act_attn_gain, act_normed_back)
    prefix_grad = (pre_mid_grad + pre_x_part).reshape(prefix_tokens.shape)
    action_grad = (act_mid_grad + act_x_part).reshape(action_tokens.shape)

    devices = ways * groups
    small = jnp.concatenate(
        [
            value.reshape(devices, -1)
            for value in (
                grad_pre_attn_gain,
                grad_pre_mlp_gain,
                grad_act_attn_gain,
                grad_act_mlp_gain,
                grad_head,
            )
        ],
        axis=1,
    )
    arrived, small = lax.optimization_barrier((arrived, small))

    pre_sum_part = split(mm(pre_hidden, down_full))
    sum_parts = [each[:count] for each in pre_sum_part]
    total = sum_parts[-1]
    for r in range(groups - 2, -1, -1):
        total = total.astype(BF16)
        if r == 0:
            total, arrived = lax.optimization_barrier((total, arrived))
        total = ring(total, -1, LOOSE).astype(F32) + sum_parts[r]
    pre_sums = total
    prefix_out = (pre_mid + pre_sums).astype(BF16).reshape(prefix_tokens.shape)
    grad_qkv = ring_scatter(
        member_parts(add_up(qkv_sums[0].astype(F32), arrived), (pre_part, act_part))
    )

    bit = 1
    while bit < ways:
        small = small + hop(small, bit)
        bit *= 2
    mine = lax.axis_index("dp") * groups
    terms = [
        lax.dynamic_slice_in_dim(small, mine + (member - r) % groups, 1, 0) for r in range(groups)
    ]
    total = terms[-1]
    for term in terms[-2::-1]:
        total = ring(total, -1, LOOSE) + term
    sizes = [width // devices] * 2 + [act_width // devices] * 2
    gains, start = [], 0
    for size in sizes:
        gains.append(total[0, start : start + size])
        start += size
    grad_head = total[0, start:].reshape(act_width // devices, -1)

    return (
        prefix_out,
        action_pred,
        prefix_grad,
        action_grad,
        *gains,
        grad_qkv[:pre_part, :query_width],
        grad_qkv[:pre_part, query_width:],
        grad_out[:, :width],
        grad_qkv[pre_part:, :query_width],
        grad_qkv[pre_part:, query_width:],
        grad_out[:, width:],
        grad_pre_gate.astype(F32),
        grad_pre_up.astype(F32),
        grad_pre_down.astype(F32),
        grad_act_gate,
        grad_act_up,
        grad_act_down,
        grad_head,
    )


def solution(mesh):
    rows = P("dp", "mp", None)
    both = P(("dp", "mp"), None)
    wide = P("dp", "mp")
    tall = P("mp", "dp")
    in_specs = (
        (rows, rows, P("dp", None), P("dp", None))
        + (P(),) * 5
        + (both,) * 6
        + (wide, wide, tall, wide, wide, tall, P(), rows, rows)
    )
    out_specs = (
        (rows,) * 4
        + (P(("dp", "mp")),) * 4
        + (both,) * 6
        + (wide, wide, tall, wide, wide, tall, both)
    )
    return jax.shard_map(shards, mesh=mesh, in_specs=in_specs, out_specs=out_specs, check_vma=False)
```

```python
import functools

import jax
import jax.numpy as jnp
from jax import lax
from jax.experimental import pallas as pl
from jax.experimental.pallas import tpu as pltpu
from jax.sharding import PartitionSpec as P

NORM_EPS = 1e-06
ROPE_BASE = 10000.0
MASKED = -1e30
F32 = jnp.float32
BF16 = jnp.bfloat16


class Links:
    def __init__(self, window=2):
        self.window = window
        self.done = {}

    def send(self, value, axis, pairs, link):
        sent = self.done.setdefault(link, [])
        if len(sent) >= self.window:
            value, _ = lax.optimization_barrier((value, sent[-self.window]))
        result = lax.ppermute(value, axis, pairs)
        sent.append(result)
        return result


LINKS = Links()


def hop(value, bit):
    size = lax.axis_size("dp")
    pairs = [(d, d ^ bit) for d in range(size)]
    if bit == 1:
        return lax.ppermute(value, "dp", pairs)
    return LINKS.send(value, "dp", pairs, bit)


LOOSE = None


def ring(value, step, link="mp"):
    size = lax.axis_size("mp")
    pairs = [(d, (d + step) % size) for d in range(size)]
    if link is LOOSE:
        return lax.ppermute(value, "mp", pairs)
    return LINKS.send(value, "mp", pairs, link)


def ring_gather(value, link="mp"):
    out = [value]
    for _ in range(lax.axis_size("mp") - 1):
        out.append(ring(out[-1], 1, link))
    return out


def ring_scatter(parts, steps=None):
    total = parts[-1].astype(BF16)
    for part in parts[-2::-1]:
        moved = ring(total.astype(BF16), -1, LOOSE)
        if steps is not None:
            steps.append(moved)
        total = moved.astype(F32) + part.astype(F32)
    return total


def chip_order(size):
    return sorted(range(1, size), key=lambda c: (bin(c).count("1"), c))


def rel_blocks():
    size = lax.axis_size("dp")
    place = jnp.arange(size, dtype=jnp.int32)
    half = size // 2
    rel = (place % half) * 2 + place // half
    return jnp.bitwise_xor(rel, lax.axis_index("dp").astype(jnp.int32))


def direct_gather(shard):
    size = lax.axis_size("dp")
    own = [shard]
    for c in range(1, size // 2):
        own.append(lax.ppermute(shard, "dp", [(d, d ^ (2 * c)) for d in range(size)]))
    return own + [hop(piece, 1) for piece in own]


def dp_gather(shard):
    chips = lax.axis_size("dp") // 2
    half = shard.shape[0] // 2
    got = {0: [shard]}

    def top(c):
        return got[c][0] if len(got[c]) == 2 else got[c][0][:half]

    def bottom(c):
        return got[c][1] if len(got[c]) == 2 else got[c][0][half:]

    for c in chip_order(chips):
        high, low = 1 << (c.bit_length() - 1), c & -c
        if high == low:
            got[c] = [hop(shard, 2 * high)]
        else:
            got[c] = [hop(top(c ^ high), 2 * high), hop(bottom(c ^ low), 2 * low)]
    own = [piece for c in range(chips) for piece in got[c]]
    return own + [hop(piece, 1) for piece in own]


def chip_sums(own, other):
    chips = lax.axis_size("dp") // 2
    total = own.astype(F32) + hop(other, 1).astype(F32)
    return total.reshape(chips, -1, own.shape[1])


def send_blocks(blocks):
    size = lax.axis_size("dp")
    return [
        lax.ppermute(blocks[c].astype(BF16), "dp", [(d, d ^ (2 * c)) for d in range(size)])
        for c in range(1, size // 2)
    ]


def send_members(parts):
    size = lax.axis_size("mp")
    return [
        lax.ppermute(parts[r], "mp", [(d, (d - r) % size) for d in range(size)])
        for r in range(1, size)
    ]


def add_up(first, arrived):
    total = first
    for each in arrived:
        total = total + each.astype(F32)
    return total


def member_parts(values, layout):
    groups = lax.axis_size("mp")
    axis = values.ndim - 2
    parts = []
    for r in range(groups):
        which = (lax.axis_index("mp") - r) % groups
        cuts, start = [], 0
        for part in layout:
            cuts.append(lax.dynamic_slice_in_dim(values, start + which * part, part, axis))
            start += groups * part
        parts.append(jnp.concatenate(cuts, axis=axis))
    return parts


def _permute_blocks(inverse, order, *refs):
    half = len(refs) // 2
    for src, dst in zip(refs[:half], refs[half:]):
        block = src.shape[1] // order.shape[0]
        for g in range(order.shape[0]):
            here = slice(g * block, (g + 1) * block)
            there = pl.ds(pl.multiple_of(order[g] * block, block), block)
            if inverse:
                dst[:, there] = src[:, here]
            else:
                dst[:, here] = src[:, there]


def permute_columns(arrays, order, inverse=False):
    count = order.shape[0]
    if any(values.shape[1] // count % 128 for values in arrays):
        hit = order[:, None] == jnp.arange(count, dtype=order.dtype)[None, :]
        places = jnp.arange(count, dtype=order.dtype)
        back = jnp.sum(jnp.where(hit, places[:, None], 0), axis=0) if inverse else order
        outs = []
        for values in arrays:
            split = values.reshape(values.shape[0], count, -1)
            cuts = [lax.dynamic_slice_in_dim(split, back[g], 1, 1) for g in range(count)]
            outs.append(jnp.concatenate(cuts, axis=1).reshape(values.shape))
        return outs
    return pl.pallas_call(
        functools.partial(_permute_blocks, inverse),
        in_specs=[pl.BlockSpec(memory_space=pltpu.SMEM)]
        + [pl.BlockSpec(memory_space=pltpu.VMEM)] * len(arrays),
        out_specs=[pl.BlockSpec(memory_space=pltpu.VMEM)] * len(arrays),
        out_shape=[jax.ShapeDtypeStruct(values.shape, values.dtype) for values in arrays],
        compiler_params=pltpu.CompilerParams(vmem_limit_bytes=32 * 2**20),
    )(order, *arrays)


def _spread(count, order, pre, act, joint):
    rows = pre.shape[0]
    narrow = [value.shape[1] // count for value in (pre, act)]
    joint[...] = jnp.zeros_like(joint)
    for g in range(count):
        start = g * sum(narrow)
        there = pl.ds(pl.multiple_of(order[g] * narrow[0], narrow[0]), narrow[0])
        joint[:rows, start : start + narrow[0]] = pre[:, there]
        there = pl.ds(pl.multiple_of(order[g] * narrow[1], narrow[1]), narrow[1])
        joint[rows:, start + narrow[0] : start + sum(narrow)] = act[:, there]


def block_call(body, order, arrays, shapes):
    return pl.pallas_call(
        functools.partial(body, order.shape[0]),
        in_specs=[pl.BlockSpec(memory_space=pltpu.SMEM)]
        + [pl.BlockSpec(memory_space=pltpu.VMEM)] * len(arrays),
        out_specs=[pl.BlockSpec(memory_space=pltpu.VMEM)] * len(shapes),
        out_shape=shapes,
        compiler_params=pltpu.CompilerParams(vmem_limit_bytes=32 * 2**20),
    )(order, *arrays)


def spread(pre, act, order):
    count = order.shape[0]
    rows, lines = pre.shape[0], act.shape[0]
    wide, thin = pre.shape[1] // count, act.shape[1] // count
    if wide % 128 or thin % 128:
        upper, lower = permute_columns([pre, act], order)
        upper = jnp.pad(upper.reshape(rows, count, wide), ((0, lines), (0, 0), (0, thin)))
        lower = jnp.pad(lower.reshape(lines, count, thin), ((rows, 0), (0, 0), (wide, 0)))
        return (upper + lower).reshape(rows + lines, -1)
    shape = jax.ShapeDtypeStruct((rows + lines, pre.shape[1] + act.shape[1]), pre.dtype)
    return block_call(_spread, order, [pre, act], [shape])[0]


def inverse_rms(values):
    return lax.rsqrt(jnp.mean(values * values, axis=-1, keepdims=True) + NORM_EPS)


def rms_norm(values, gain_vec):
    return values * inverse_rms(values) * gain_vec


def rms_back(values, gain_vec, grads):
    inverse = inverse_rms(values)
    unit = values * inverse
    scaled = gain_vec * grads
    mean = jnp.mean(unit * scaled, axis=-1, keepdims=True)
    return inverse * (scaled - unit * mean), jnp.sum(grads * unit, axis=0)


def rope_tables(positions, head_dim):
    half_dim = head_dim // 2
    inverse = ROPE_BASE ** (-2.0 * jnp.arange(half_dim).astype(F32) / head_dim)
    angles = positions.astype(F32)[:, None] * inverse[None, :]
    return (jnp.cos(angles), jnp.sin(angles))


def rotate(values, cosine_tab, sine_tab):
    half_dim = values.shape[-1] // 2
    lower_half = values[..., :half_dim]
    upper_half = values[..., half_dim:]
    return jnp.concatenate(
        [
            lower_half * cosine_tab - upper_half * sine_tab,
            upper_half * cosine_tab + lower_half * sine_tab,
        ],
        axis=-1,
    )


def mm(left, right):
    return lax.dot_general(left, right, (((1,), (0,)), ((), ())), preferred_element_type=F32)


def mm_nt(left, right):
    return lax.dot_general(left, right, (((1,), (1,)), ((), ())), preferred_element_type=F32)


def mm_tn(left, right):
    return lax.dot_general(left, right, (((0,), (0,)), ((), ())), preferred_element_type=F32)


def geglu(gate_val, up_val, live_mask):
    return jax.nn.gelu(gate_val, approximate=True) * up_val * live_mask


def feed_forward(rows, cot_rows, gate, up, down_t, live_mask):
    gate_val = mm(rows, gate)
    up_val = mm(rows, up)
    hidden_back = mm(cot_rows, down_t)
    hidden, pull = jax.vjp(lambda g, u: geglu(g, u, live_mask), gate_val, up_val)
    gate_back, up_back = pull(hidden_back)
    return hidden.astype(BF16), gate_back.astype(BF16), up_back.astype(BF16)


def _feed_forward_tile(groups, order, *refs):
    pieces, (back_ref, gate_ref) = refs[:groups], refs[groups : groups + 2]
    up_pieces = refs[groups + 2 : -5]
    hidden_ref, gate_back_ref, up_back_ref, rows_ref, up_ref = refs[-5:]
    count = pieces[0].shape[0]
    for g, piece in enumerate(up_pieces):
        size = piece.shape[0]
        up_ref[pl.ds(pl.multiple_of(order[g] * size, size), size), :] = piece[...]
    root, cube = 0.7978845608028654, 0.044715

    @pl.when(pl.program_id(0) == 0)
    def _():
        for r in range(groups):
            rows_ref[r * count : (r + 1) * count, :] = pieces[r][...]

    for r in range(groups):
        cut = slice(r * count, (r + 1) * count)
        rows = pieces[r][...]
        gate_val = jnp.dot(rows, gate_ref[...], preferred_element_type=F32)
        up_val = jnp.dot(rows, up_ref[...], preferred_element_type=F32)
        back = back_ref[cut, :].astype(F32)
        square = gate_val * gate_val
        bend = jnp.tanh(root * gate_val * (1.0 + cube * square))
        half_open = 0.5 * (1.0 + bend)
        active = gate_val * half_open
        inner = (0.5 * root) * gate_val * (1.0 - bend * bend) * (1.0 + 3.0 * cube * square)
        hidden_ref[cut, :] = (active * up_val).astype(BF16)
        gate_back_ref[cut, :] = (back * up_val * (half_open + inner)).astype(BF16)
        up_back_ref[cut, :] = (back * active).astype(BF16)


def feed_forward_kernel(order, pieces, hidden_back, gate, up_pieces, tile=512):
    groups = len(pieces)
    count, width = pieces[0].shape
    total = groups * count
    units = gate.shape[1]
    block = pl.BlockSpec((total, tile), lambda n, idx: (0, n))
    weight = pl.BlockSpec((width, tile), lambda n, idx: (0, n))
    part = pl.BlockSpec((width // len(up_pieces), tile), lambda n, idx: (0, n))
    fixed = pl.BlockSpec((count, width), lambda n, idx: (0, 0), pipeline_mode=pl.Buffered(1))
    return pl.pallas_call(
        functools.partial(_feed_forward_tile, groups),
        grid_spec=pltpu.PrefetchScalarGridSpec(
            num_scalar_prefetch=1,
            grid=(units // tile,),
            in_specs=[fixed] * groups + [block, weight] + [part] * len(up_pieces),
            out_specs=[block] * 3
            + [pl.BlockSpec((total, width), lambda n, idx: (0, 0)), weight],
        ),
        out_shape=[jax.ShapeDtypeStruct((total, units), BF16)] * 3
        + [
            jax.ShapeDtypeStruct((total, width), BF16),
            jax.ShapeDtypeStruct((width, units), BF16),
        ],
        compiler_params=pltpu.CompilerParams(vmem_limit_bytes=56 * 2**20),
        cost_estimate=pl.CostEstimate(
            flops=4 * total * width * units,
            bytes_accessed=6 * width * units + 8 * total * units + 4 * total * width,
            transcendentals=total * units,
        ),
    )(order, *pieces, hidden_back, gate, *up_pieces)


def _stacked_grads(rows, cots, gate_back, up_back, hidden, out):
    size = rows.shape[1]
    for n, (left, right) in enumerate(((rows, gate_back), (rows, up_back), (cots, hidden))):
        out[n * size : (n + 1) * size, :] = lax.dot_general(
            left[...], right[...], (((0,), (0,)), ((), ())), preferred_element_type=F32
        ).astype(BF16)


def stacked_grads(ways, rows, cots, gate_back, up_back, hidden):
    lines, width = rows.shape
    units = hidden.shape[1]
    size = width // ways
    if size % 128:
        terms = [mm_tn(rows, gate_back), mm_tn(rows, up_back), mm_tn(cots, hidden)]
        cut = [term.astype(BF16).reshape(ways, size, units) for term in terms]
        return jnp.concatenate(cut, axis=1).reshape(-1, units)
    column = pl.BlockSpec((lines, size), lambda g: (0, g))
    whole = pl.BlockSpec((lines, units), lambda g: (0, 0))
    return pl.pallas_call(
        _stacked_grads,
        grid=(ways,),
        in_specs=[column, column, whole, whole, whole],
        out_specs=pl.BlockSpec((3 * size, units), lambda g: (g, 0)),
        out_shape=jax.ShapeDtypeStruct((3 * width, units), BF16),
        compiler_params=pltpu.CompilerParams(vmem_limit_bytes=32 * 2**20),
        cost_estimate=pl.CostEstimate(
            flops=6 * lines * width * units,
            bytes_accessed=6 * width * units + 6 * lines * units,
            transcendentals=0,
        ),
    )(rows, cots, gate_back, up_back, hidden)


def after(value, *first):
    return lax.optimization_barrier((value, *first))[0]


def shards(
    prefix_tokens,
    action_tokens,
    block_ids,
    live_dims,
    hidden_counts,
    pre_attn_gain,
    pre_mlp_gain,
    act_attn_gain,
    act_mlp_gain,
    pre_query,
    pre_keyval,
    pre_output,
    act_query,
    act_keyval,
    act_output,
    pre_gate,
    pre_up,
    pre_down,
    act_gate,
    act_up,
    act_down,
    action_head,
    prefix_cot,
    pred_cot,
):
    groups = lax.axis_size("mp")
    ways = lax.axis_size("dp")
    member = lax.axis_index("mp")
    items, pre_rows, width = prefix_tokens.shape
    act_rows, act_width = action_tokens.shape[1:]
    pre_len = pre_rows * groups
    head_dim = pre_keyval.shape[1] // 2
    query_width = pre_query.shape[1]
    heads = query_width // head_dim
    local_len = pre_rows + act_rows
    scale = head_dim ** (-0.5)
    order = rel_blocks()
    LINKS.done.clear()

    pre_part, act_part, out_part = pre_query.shape[0], act_query.shape[0], pre_output.shape[0]
    qkv_own = jnp.concatenate(
        [
            jnp.concatenate([pre_query, pre_keyval], axis=1),
            jnp.concatenate([act_query, act_keyval], axis=1),
        ],
        axis=0,
    )
    qkv_full = lax.all_gather(qkv_own, ("dp", "mp"), axis=0, tiled=True)
    act_stack = jnp.concatenate([act_gate, act_up, act_down.T], axis=0)
    def in_place(pieces):
        size = pieces[0].shape[0]
        twice = jnp.concatenate(pieces[::-1] * 2, axis=0)
        return lax.dynamic_slice_in_dim(twice, (groups - 1 - member) * size, groups * size, 0)

    out_ring = ring_gather(jnp.concatenate([pre_output, act_output], axis=1))
    out_block = in_place(out_ring)
    qkv_full, act_stack, out_block, up_own = lax.optimization_barrier(
        (qkv_full, act_stack, out_block, pre_up)
    )
    up_pieces = direct_gather(up_own)
    out_full = jnp.concatenate(dp_gather(out_block), axis=0)
    qkv_full = qkv_full.reshape(ways * groups, -1, qkv_own.shape[1])
    pre_qkv = qkv_full[:, :pre_part].reshape(width, -1)
    act_qkv = qkv_full[:, pre_part:].reshape(act_width, -1)
    act_flat_w = lax.all_gather(act_stack, "dp", axis=0, tiled=True)
    act_all = act_flat_w.reshape(ways, 3, -1, act_gate.shape[1])
    act_gate_full, act_up_full, act_down_full = (
        act_all[:, n].reshape(act_width, -1) for n in range(3)
    )

    pre_flat = prefix_tokens.reshape(items * pre_rows, width)
    act_flat = action_tokens.reshape(items * act_rows, act_width)
    cot_flat = prefix_cot.reshape(items * pre_rows, width)
    pre_x = pre_flat.astype(F32)
    act_x = act_flat.astype(F32)
    live_mask = live_dims[:, None, :].astype(F32)
    pred_back = (pred_cot * live_mask).astype(BF16).reshape(items * act_rows, -1)
    act_final_back = mm_nt(pred_back, action_head)
    count = items * pre_rows
    padded = -(-count // 16) * 16
    act_count = items * act_rows

    def pad(values):
        return jnp.pad(values, ((0, padded - count), (0, 0)))

    def ring_stack(value):
        return jnp.concatenate(ring_gather(value), axis=0)

    local_pos = jnp.concatenate(
        [
            member * pre_rows + jnp.arange(pre_rows),
            pre_len + member * act_rows + jnp.arange(act_rows),
        ]
    )
    cosine_tab, sine_tab = rope_tables(local_pos, head_dim)

    def blocks_of(which):
        return jnp.concatenate(
            [
                lax.dynamic_slice_in_dim(block_ids, which * pre_rows, pre_rows, 1),
                lax.dynamic_slice_in_dim(block_ids, pre_len + which * act_rows, act_rows, 1),
            ],
            axis=1,
        )

    local_blocks = blocks_of(member)
    key_blocks = jnp.concatenate(
        [blocks_of((member - r) % groups) for r in range(groups)], axis=1
    )
    allowed = key_blocks[:, None, None, :] <= local_blocks[:, None, :, None]

    act_padded = -(-act_count // 16) * 16

    def stack(pre_part_rows, act_part_rows):
        return (
            jnp.pad(pre_part_rows, ((0, padded - count), (0, 0))),
            jnp.pad(act_part_rows, ((0, act_padded - act_count), (0, 0))),
        )

    def to_items(joint):
        return jnp.concatenate(
            [
                joint[:count].reshape(items, pre_rows, -1),
                joint[padded : padded + act_count].reshape(items, act_rows, -1),
            ],
            axis=1,
        )

    def from_items(values):
        return jnp.concatenate(
            stack(
                values[:, :pre_rows].reshape(count, -1),
                values[:, pre_rows:].reshape(act_count, -1),
            ),
            axis=0,
        )

    pre_normed, act_normed = stack(
        rms_norm(pre_x, pre_attn_gain).astype(BF16), rms_norm(act_x, act_attn_gain).astype(BF16)
    )
    normed = spread(pre_normed, act_normed, order)

    def project(columns):
        return to_items(
            jnp.concatenate(
                [mm(pre_normed, pre_qkv[:, columns]), mm(act_normed, act_qkv[:, columns])], axis=0
            )
        )

    keyval_raw = project(slice(query_width, None))
    keyval_rows = jnp.concatenate(
        [rotate(keyval_raw[..., :head_dim], cosine_tab, sine_tab), keyval_raw[..., head_dim:]],
        axis=-1,
    ).astype(BF16)
    keyval_rows, gate_own, down_own = lax.optimization_barrier(
        (keyval_rows, pre_gate, pre_down)
    )
    down_full = lax.all_gather(down_own, "dp", axis=1, tiled=True)
    gate_full = lax.all_gather(gate_own, "dp", axis=0, tiled=True)
    all_keyval = jnp.concatenate(ring_gather(keyval_rows), axis=1)
    cot_all = ring_stack(pad(cot_flat))
    act_cot_all = ring_stack(act_final_back.astype(BF16))
    hidden_back = mm_nt(cot_all, down_full).astype(BF16)
    key_rows = all_keyval[..., :head_dim]
    value_rows = all_keyval[..., head_dim:]
    query_raw = project(slice(0, query_width))
    query_rows = rotate(
        query_raw.reshape(items, local_len, heads, head_dim),
        cosine_tab[:, None, :],
        sine_tab[:, None, :],
    ).astype(BF16)
    scores = (
        jnp.einsum("iqhd,ikd->ihqk", query_rows, key_rows, preferred_element_type=F32) * scale
    )
    probs = jax.nn.softmax(jnp.where(allowed, scores, MASKED), axis=-1)
    probs_low = probs.astype(BF16)
    attended = jnp.einsum("ihqk,ikd->iqhd", probs_low, value_rows, preferred_element_type=F32)
    attended = attended.astype(BF16).reshape(items, local_len, query_width)
    (att_joint,) = permute_columns([from_items(attended)], order)
    mid = mm(att_joint, out_full)
    pre_mid = pre_x + mid[:count, :width]
    act_mid = act_x + mid[padded : padded + act_count, width:]

    act_second = rms_norm(act_mid, act_mlp_gain).astype(BF16)
    act_all_rows = jnp.concatenate(ring_gather(act_second, LOOSE), axis=0)
    slot_count = lax.dynamic_index_in_dim(hidden_counts, member, keepdims=False)
    slot_live = (jnp.arange(act_gate.shape[1]) < slot_count).astype(F32)

    def scatter_sum(value, dimension):
        return lax.psum_scatter(value, "dp", scatter_dimension=dimension, tiled=True)

    def split(partial):
        size = partial.shape[0] // groups
        return [partial[r * size : (r + 1) * size] for r in range(groups)]

    act_hidden, act_gate_back, act_up_back = feed_forward(
        act_all_rows, act_cot_all, act_gate_full, act_up_full, act_down_full, slot_live
    )
    act_second_part = split(mm_nt(act_gate_back, act_gate_full) + mm_nt(act_up_back, act_up_full))
    act_sum_part = split(mm_nt(act_hidden, act_down_full))

    act_stacked = stacked_grads(
        ways, act_all_rows, act_cot_all, act_gate_back, act_up_back, act_hidden
    )
    pre_second = pad(rms_norm(pre_mid, pre_mlp_gain).astype(BF16))
    second_pieces = [pre_second]
    for r in range(1, groups):
        piece = ring(second_pieces[-1], 1)
        if r == 1:
            piece, hidden_back = lax.optimization_barrier((piece, hidden_back))
        if r == groups - 1:
            piece = after(piece, act_stacked)
        second_pieces.append(piece)
    grad_act = scatter_sum(act_stacked, 0)
    grad_act = grad_act.astype(F32).reshape(3, -1, act_gate.shape[1])
    grad_act_gate, grad_act_up, grad_act_down = grad_act[0], grad_act[1], grad_act[2].T

    pre_hidden, pre_gate_back, pre_up_back, pre_all, up_full = feed_forward_kernel(
        order, second_pieces, hidden_back, gate_full, up_pieces
    )
    gate_term = mm_tn(pre_all, pre_gate_back).astype(BF16)
    gate_term, pre_up_back = lax.optimization_barrier((gate_term, pre_up_back))
    grad_pre_gate = scatter_sum(gate_term, 0)
    half = groups // 2 * padded

    def second_rows(cut, gate_rows, up_rows):
        return mm_nt(gate_rows[cut], gate_full) + mm_nt(up_rows[cut], up_full)

    later = second_rows(slice(half, None), pre_gate_back, pre_up_back)
    later, gate_rows, up_rows = lax.optimization_barrier((later, pre_gate_back, pre_up_back))
    sooner = second_rows(slice(0, half), gate_rows, up_rows)

    act_lines = act_count * act_width // width

    def lines(value):
        return value.reshape(act_lines, width)

    def second_part(r):
        rows = sooner if r < groups // 2 else later
        rows = rows[r % (groups // 2) * padded :][:count]
        return jnp.concatenate([rows, lines(act_second_part[r]), lines(act_sum_part[r])], axis=0)

    up_term = down_term = None
    total = second_part(groups - 1)
    for r in range(groups - 2, -1, -1):
        moved = ring(total.astype(BF16), -1, LOOSE)
        if r == groups - 2:
            moved, up_rows = lax.optimization_barrier((moved, after(up_rows, sooner)))
            up_term = mm_tn(pre_all, up_rows).astype(BF16)
        elif r == groups - 3:
            moved, up_term, pre_hidden = lax.optimization_barrier((moved, up_term, pre_hidden))
            down_term = mm_tn(pre_hidden, cot_all).astype(BF16)
        elif r == groups - 4:
            moved, down_term = lax.optimization_barrier((moved, down_term))
        total = moved.astype(F32) + second_part(r)
    grad_pre_up = scatter_sum(up_term, 0)
    grad_pre_down = scatter_sum(down_term, 1)
    pre_second_back = total[:count]
    act_second_back = total[count : count + act_lines].reshape(act_count, act_width)
    act_sums = total[count + act_lines :].reshape(act_count, act_width)

    pre_mid_part, grad_pre_mlp_gain = rms_back(pre_mid, pre_mlp_gain, pre_second_back)
    act_mid_part, grad_act_mlp_gain = rms_back(act_mid, act_mlp_gain, act_second_back)
    pre_mid_grad = cot_flat.astype(F32) + pre_mid_part
    act_mid_grad = act_final_back + act_mid_part
    back_joint = jnp.concatenate(
        [
            jnp.pad(pre_mid_grad.astype(BF16), ((0, padded - count), (0, act_width))),
            jnp.pad(act_mid_grad.astype(BF16), ((0, act_padded - act_count), (width, 0))),
        ],
        axis=0,
    )
    attended_back = to_items(
        permute_columns([mm_nt(back_joint, out_full).astype(BF16)], order, True)[0]
    ).reshape(items, local_len, heads, head_dim)
    out_half = query_width // 2
    out_sums = chip_sums(
        mm_tn(att_joint[:, :out_half], back_joint).astype(BF16),
        mm_tn(att_joint[:, out_half:], back_joint).astype(BF16),
    ).astype(BF16)
    probs_back = jnp.einsum(
        "iqhd,ikd->ihqk", attended_back, value_rows, preferred_element_type=F32
    )
    value_back = jnp.einsum(
        "ihqk,iqhd->ikd", probs_low, attended_back, preferred_element_type=F32
    )
    scores_back = (
        probs * (probs_back - jnp.sum(probs * probs_back, axis=-1, keepdims=True))
    ).astype(BF16)
    key_back = (
        jnp.einsum("ihqk,iqhd->ikd", scores_back, query_rows, preferred_element_type=F32) * scale
    )
    query_back = (
        jnp.einsum("ihqk,ikd->iqhd", scores_back, key_rows, preferred_element_type=F32) * scale
    )
    keyval_back = jnp.concatenate([key_back, value_back], axis=-1).astype(BF16)
    own_kv_back = ring_scatter(
        [keyval_back[:, r * local_len : (r + 1) * local_len] for r in range(groups)]
    )
    keyval_low = jnp.concatenate(
        [rotate(own_kv_back[..., :head_dim], cosine_tab, -sine_tab), own_kv_back[..., head_dim:]],
        axis=-1,
    ).astype(BF16)
    query_low = rotate(query_back, cosine_tab[:, None, :], -sine_tab[:, None, :])
    query_low = query_low.reshape(items, local_len, query_width).astype(BF16)
    back_rows = from_items(jnp.concatenate([query_low, keyval_low], axis=-1))
    back_rows, grad_pre_gate, out_sums = lax.optimization_barrier(
        (back_rows, grad_pre_gate, out_sums)
    )
    out_arrived = send_blocks(out_sums)
    qkv_half = normed.shape[1] // 2
    qkv_own_part = mm_tn(normed[:, :qkv_half], back_rows).astype(BF16)
    qkv_other_part = mm_tn(normed[:, qkv_half:], back_rows).astype(BF16)
    qkv_sums = chip_sums(qkv_own_part, qkv_other_part).astype(BF16)
    act_final_low = (act_mid + act_sums).astype(BF16)
    action_pred = mm(act_final_low, action_head).reshape(pred_cot.shape) * live_mask
    grad_head = mm_tn(act_final_low, pred_back)
    back_rows, out_arrived = lax.optimization_barrier((back_rows, out_arrived))
    pre_normed_back = mm_nt(back_rows[:padded], pre_qkv)[:count]
    act_normed_back = mm_nt(back_rows[padded:], act_qkv)[:act_count]
    pre_x_part, grad_pre_attn_gain = rms_back(pre_x, pre_attn_gain, pre_normed_back)
    act_x_part, grad_act_attn_gain = rms_back(act_x, act_attn_gain, act_normed_back)
    prefix_grad = (pre_mid_grad + pre_x_part).reshape(prefix_tokens.shape)
    action_grad = (act_mid_grad + act_x_part).reshape(action_tokens.shape)

    devices = ways * groups
    small = jnp.concatenate(
        [
            value.reshape(devices, -1)
            for value in (
                grad_pre_attn_gain,
                grad_pre_mlp_gain,
                grad_act_attn_gain,
                grad_act_mlp_gain,
                grad_head,
            )
        ],
        axis=1,
    )
    small = small + hop(small, 1)
    spare = -(-groups // 8) * 8 - groups
    sent_blocks = []
    for c in range(ways // 2):
        start = jnp.bitwise_xor(lax.axis_index("dp"), 2 * c) * groups
        lines = lax.dynamic_slice_in_dim(small, start, groups, 0)
        lines = jnp.pad(lines, ((0, spare), (0, qkv_sums.shape[2] - small.shape[1])))
        sent_blocks.append(jnp.concatenate([qkv_sums[c], lines.astype(BF16)], axis=0))
    sent_blocks, out_arrived, pre_hidden = lax.optimization_barrier(
        (sent_blocks, out_arrived, pre_hidden)
    )
    arrived = send_blocks(sent_blocks)
    pre_sum_part = split(mm(pre_hidden, down_full).astype(BF16))
    sum_parts = [each[:count] for each in pre_sum_part]
    sums_arrived = send_members(sum_parts)
    arrived, out_arrived = lax.optimization_barrier((arrived, out_arrived))
    qkv_parts = member_parts(
        add_up(sent_blocks[0].astype(F32), arrived).astype(BF16), (pre_part, act_part, 1)
    )
    qkv_arrived = send_members(qkv_parts)
    out_parts = member_parts(
        add_up(out_sums[0].astype(F32), out_arrived).astype(BF16), (out_part,)
    )
    out_arrived = send_members(out_parts)
    sums_arrived, grad_pre_up, grad_pre_down, qkv_first = lax.optimization_barrier(
        (sums_arrived, grad_pre_up, grad_pre_down, qkv_parts[0])
    )
    pre_sums = add_up(sum_parts[0].astype(F32), sums_arrived)
    prefix_out = (pre_mid + pre_sums).astype(BF16).reshape(prefix_tokens.shape)
    grad_out = add_up(out_parts[0].astype(F32), out_arrived)
    grad_qkv = add_up(qkv_first.astype(F32), qkv_arrived)
    total = grad_qkv[pre_part + act_part :, : small.shape[1]]
    sizes = [width // devices] * 2 + [act_width // devices] * 2
    gains, start = [], 0
    for size in sizes:
        gains.append(total[0, start : start + size])
        start += size
    grad_head = total[0, start:].reshape(act_width // devices, -1)

    return (
        prefix_out,
        action_pred,
        prefix_grad,
        action_grad,
        *gains,
        grad_qkv[:pre_part, :query_width],
        grad_qkv[:pre_part, query_width:],
        grad_out[:, :width],
        grad_qkv[pre_part : pre_part + act_part, :query_width],
        grad_qkv[pre_part : pre_part + act_part, query_width:],
        grad_out[:, width:],
        grad_pre_gate.astype(F32),
        grad_pre_up.astype(F32),
        grad_pre_down.astype(F32),
        grad_act_gate,
        grad_act_up,
        grad_act_down,
        grad_head,
    )


def solution(mesh):
    rows = P("dp", "mp", None)
    both = P(("dp", "mp"), None)
    wide = P("dp", "mp")
    tall = P("mp", "dp")
    in_specs = (
        (rows, rows, P("dp", None), P("dp", None))
        + (P(),) * 5
        + (both,) * 6
        + (wide, wide, tall, wide, wide, tall, P(), rows, rows)
    )
    out_specs = (
        (rows,) * 4
        + (P(("dp", "mp")),) * 4
        + (both,) * 6
        + (wide, wide, tall, wide, wide, tall, both)
    )
    return jax.shard_map(shards, mesh=mesh, in_specs=in_specs, out_specs=out_specs, check_vma=False)
```

```python
import functools

import jax
import jax.numpy as jnp
from jax import lax
from jax.experimental import pallas as pl
from jax.experimental.pallas import tpu as pltpu
from jax.sharding import PartitionSpec as P

NORM_EPS = 1e-06
ROPE_BASE = 10000.0
MASKED = -1e30
F32 = jnp.float32
BF16 = jnp.bfloat16


class Links:
    def __init__(self, window=2):
        self.window = window
        self.done = {}

    def send(self, value, axis, pairs, link):
        sent = self.done.setdefault(link, [])
        if len(sent) >= self.window:
            value, _ = lax.optimization_barrier((value, sent[-self.window]))
        result = lax.ppermute(value, axis, pairs)
        sent.append(result)
        return result


LINKS = Links()


def hop(value, bit):
    size = lax.axis_size("dp")
    pairs = [(d, d ^ bit) for d in range(size)]
    if bit == 1:
        return lax.ppermute(value, "dp", pairs)
    return LINKS.send(value, "dp", pairs, bit)


LOOSE = None


def ring(value, step, link="mp"):
    size = lax.axis_size("mp")
    pairs = [(d, (d + step) % size) for d in range(size)]
    if link is LOOSE:
        return lax.ppermute(value, "mp", pairs)
    return LINKS.send(value, "mp", pairs, link)


def ring_gather(value, link="mp"):
    out = [value]
    for _ in range(lax.axis_size("mp") - 1):
        out.append(ring(out[-1], 1, link))
    return out


def ring_scatter(parts, steps=None):
    total = parts[-1].astype(BF16)
    for part in parts[-2::-1]:
        moved = ring(total.astype(BF16), -1, LOOSE)
        if steps is not None:
            steps.append(moved)
        total = moved.astype(F32) + part.astype(F32)
    return total


def chip_order(size):
    return sorted(range(1, size), key=lambda c: (bin(c).count("1"), c))


def rel_blocks():
    size = lax.axis_size("dp")
    place = jnp.arange(size, dtype=jnp.int32)
    half = size // 2
    rel = (place % half) * 2 + place // half
    return jnp.bitwise_xor(rel, lax.axis_index("dp").astype(jnp.int32))


def dp_gather(shard, hold=None):
    chips = lax.axis_size("dp") // 2
    half = shard.shape[0] // 2
    got = {0: [shard]}

    def top(c):
        return got[c][0] if len(got[c]) == 2 else got[c][0][:half]

    def bottom(c):
        return got[c][1] if len(got[c]) == 2 else got[c][0][half:]

    for c in chip_order(chips):
        high, low = 1 << (c.bit_length() - 1), c & -c
        if high == low:
            got[c] = [hop(shard, 2 * high)]
        else:
            got[c] = [hop(top(c ^ high), 2 * high), hop(bottom(c ^ low), 2 * low)]
    own = [piece for c in range(chips) for piece in got[c]]
    if hold is not None:
        own, hold = lax.optimization_barrier((own, hold))
        return own + [hop(piece, 1) for piece in own], hold
    return own + [hop(piece, 1) for piece in own]


def chip_sums(own, other):
    chips = lax.axis_size("dp") // 2
    total = own.astype(F32) + hop(other, 1).astype(F32)
    return total.reshape(chips, -1, own.shape[1])


def send_blocks(blocks):
    size = lax.axis_size("dp")
    return [
        lax.ppermute(blocks[c].astype(BF16), "dp", [(d, d ^ (2 * c)) for d in range(size)])
        for c in range(1, size // 2)
    ]


def send_members(parts):
    size = lax.axis_size("mp")
    return [
        lax.ppermute(parts[r], "mp", [(d, (d - r) % size) for d in range(size)])
        for r in range(1, size)
    ]


def add_up(first, arrived):
    total = first
    for each in arrived:
        total = total + each.astype(F32)
    return total


def member_parts(values, layout):
    groups = lax.axis_size("mp")
    axis = values.ndim - 2
    parts = []
    for r in range(groups):
        which = (lax.axis_index("mp") - r) % groups
        cuts, start = [], 0
        for part in layout:
            cuts.append(lax.dynamic_slice_in_dim(values, start + which * part, part, axis))
            start += groups * part
        parts.append(jnp.concatenate(cuts, axis=axis))
    return parts


def _permute_blocks(inverse, order, *refs):
    half = len(refs) // 2
    for src, dst in zip(refs[:half], refs[half:]):
        block = src.shape[1] // order.shape[0]
        for g in range(order.shape[0]):
            here = slice(g * block, (g + 1) * block)
            there = pl.ds(pl.multiple_of(order[g] * block, block), block)
            if inverse:
                dst[:, there] = src[:, here]
            else:
                dst[:, here] = src[:, there]


def permute_columns(arrays, order, inverse=False):
    count = order.shape[0]
    if any(values.shape[1] // count % 128 for values in arrays):
        hit = order[:, None] == jnp.arange(count, dtype=order.dtype)[None, :]
        places = jnp.arange(count, dtype=order.dtype)
        back = jnp.sum(jnp.where(hit, places[:, None], 0), axis=0) if inverse else order
        outs = []
        for values in arrays:
            split = values.reshape(values.shape[0], count, -1)
            cuts = [lax.dynamic_slice_in_dim(split, back[g], 1, 1) for g in range(count)]
            outs.append(jnp.concatenate(cuts, axis=1).reshape(values.shape))
        return outs
    return pl.pallas_call(
        functools.partial(_permute_blocks, inverse),
        in_specs=[pl.BlockSpec(memory_space=pltpu.SMEM)]
        + [pl.BlockSpec(memory_space=pltpu.VMEM)] * len(arrays),
        out_specs=[pl.BlockSpec(memory_space=pltpu.VMEM)] * len(arrays),
        out_shape=[jax.ShapeDtypeStruct(values.shape, values.dtype) for values in arrays],
        compiler_params=pltpu.CompilerParams(vmem_limit_bytes=32 * 2**20),
    )(order, *arrays)


def _spread(count, order, pre, act, joint):
    rows = pre.shape[0]
    narrow = [value.shape[1] // count for value in (pre, act)]
    joint[...] = jnp.zeros_like(joint)
    for g in range(count):
        start = g * sum(narrow)
        there = pl.ds(pl.multiple_of(order[g] * narrow[0], narrow[0]), narrow[0])
        joint[:rows, start : start + narrow[0]] = pre[:, there]
        there = pl.ds(pl.multiple_of(order[g] * narrow[1], narrow[1]), narrow[1])
        joint[rows:, start + narrow[0] : start + sum(narrow)] = act[:, there]


def _unspread(count, order, joint, pre, act):
    rows = pre.shape[0]
    narrow = [value.shape[1] // count for value in (pre, act)]
    for g in range(count):
        start = g * sum(narrow)
        there = pl.ds(pl.multiple_of(order[g] * narrow[0], narrow[0]), narrow[0])
        pre[:, there] = joint[:rows, start : start + narrow[0]]
        there = pl.ds(pl.multiple_of(order[g] * narrow[1], narrow[1]), narrow[1])
        act[:, there] = joint[rows:, start + narrow[0] : start + sum(narrow)]


def block_call(body, order, arrays, shapes):
    return pl.pallas_call(
        functools.partial(body, order.shape[0]),
        in_specs=[pl.BlockSpec(memory_space=pltpu.SMEM)]
        + [pl.BlockSpec(memory_space=pltpu.VMEM)] * len(arrays),
        out_specs=[pl.BlockSpec(memory_space=pltpu.VMEM)] * len(shapes),
        out_shape=shapes,
        compiler_params=pltpu.CompilerParams(vmem_limit_bytes=32 * 2**20),
    )(order, *arrays)


def spread(pre, act, order):
    count = order.shape[0]
    rows, lines = pre.shape[0], act.shape[0]
    wide, thin = pre.shape[1] // count, act.shape[1] // count
    if wide % 128 or thin % 128:
        upper, lower = permute_columns([pre, act], order)
        upper = jnp.pad(upper.reshape(rows, count, wide), ((0, lines), (0, 0), (0, thin)))
        lower = jnp.pad(lower.reshape(lines, count, thin), ((rows, 0), (0, 0), (wide, 0)))
        return (upper + lower).reshape(rows + lines, -1)
    shape = jax.ShapeDtypeStruct((rows + lines, pre.shape[1] + act.shape[1]), pre.dtype)
    return block_call(_spread, order, [pre, act], [shape])[0]


def unspread(joint, rows, wide, thin, order):
    count = order.shape[0]
    lines = joint.shape[0] - rows
    if wide // count % 128 or thin // count % 128:
        blocks = joint.reshape(joint.shape[0], count, -1)
        upper = blocks[:rows, :, : wide // count].reshape(rows, wide)
        lower = blocks[rows:, :, wide // count :].reshape(lines, thin)
        return permute_columns([upper, lower], order, True)
    shapes = [
        jax.ShapeDtypeStruct((rows, wide), joint.dtype),
        jax.ShapeDtypeStruct((lines, thin), joint.dtype),
    ]
    return block_call(_unspread, order, [joint], shapes)


def inverse_rms(values):
    return lax.rsqrt(jnp.mean(values * values, axis=-1, keepdims=True) + NORM_EPS)


def rms_norm(values, gain_vec):
    return values * inverse_rms(values) * gain_vec


def rms_back(values, gain_vec, grads):
    inverse = inverse_rms(values)
    unit = values * inverse
    scaled = gain_vec * grads
    mean = jnp.mean(unit * scaled, axis=-1, keepdims=True)
    return inverse * (scaled - unit * mean), jnp.sum(grads * unit, axis=0)


def rope_tables(positions, head_dim):
    half_dim = head_dim // 2
    inverse = ROPE_BASE ** (-2.0 * jnp.arange(half_dim).astype(F32) / head_dim)
    angles = positions.astype(F32)[:, None] * inverse[None, :]
    return (jnp.cos(angles), jnp.sin(angles))


def rotate(values, cosine_tab, sine_tab):
    half_dim = values.shape[-1] // 2
    lower_half = values[..., :half_dim]
    upper_half = values[..., half_dim:]
    return jnp.concatenate(
        [
            lower_half * cosine_tab - upper_half * sine_tab,
            upper_half * cosine_tab + lower_half * sine_tab,
        ],
        axis=-1,
    )


def mm(left, right):
    return lax.dot_general(left, right, (((1,), (0,)), ((), ())), preferred_element_type=F32)


def mm_nt(left, right):
    return lax.dot_general(left, right, (((1,), (1,)), ((), ())), preferred_element_type=F32)


def mm_tn(left, right):
    return lax.dot_general(left, right, (((0,), (0,)), ((), ())), preferred_element_type=F32)


def geglu(gate_val, up_val, live_mask):
    return jax.nn.gelu(gate_val, approximate=True) * up_val * live_mask


def feed_forward(rows, cot_rows, gate, up, down_t, live_mask):
    gate_val = mm(rows, gate)
    up_val = mm(rows, up)
    hidden_back = mm(cot_rows, down_t)
    hidden, pull = jax.vjp(lambda g, u: geglu(g, u, live_mask), gate_val, up_val)
    gate_back, up_back = pull(hidden_back)
    return hidden.astype(BF16), gate_back.astype(BF16), up_back.astype(BF16)


def _feed_forward_tile(groups, *refs):
    pieces, (back_ref, gate_ref, up_ref) = refs[:groups], refs[groups : groups + 3]
    hidden_ref, gate_back_ref, up_back_ref, rows_ref = refs[groups + 3 :]
    count = pieces[0].shape[0]
    root, cube = 0.7978845608028654, 0.044715

    @pl.when(pl.program_id(0) == 0)
    def _():
        for r in range(groups):
            rows_ref[r * count : (r + 1) * count, :] = pieces[r][...]

    for r in range(groups):
        cut = slice(r * count, (r + 1) * count)
        rows = pieces[r][...]
        gate_val = jnp.dot(rows, gate_ref[...], preferred_element_type=F32)
        up_val = jnp.dot(rows, up_ref[...], preferred_element_type=F32)
        back = back_ref[cut, :].astype(F32)
        square = gate_val * gate_val
        bend = jnp.tanh(root * gate_val * (1.0 + cube * square))
        half_open = 0.5 * (1.0 + bend)
        active = gate_val * half_open
        inner = (0.5 * root) * gate_val * (1.0 - bend * bend) * (1.0 + 3.0 * cube * square)
        hidden_ref[cut, :] = (active * up_val).astype(BF16)
        gate_back_ref[cut, :] = (back * up_val * (half_open + inner)).astype(BF16)
        up_back_ref[cut, :] = (back * active).astype(BF16)


def feed_forward_kernel(pieces, hidden_back, gate, up, tile=512):
    groups = len(pieces)
    count, width = pieces[0].shape
    total = groups * count
    units = gate.shape[1]
    block = pl.BlockSpec((total, tile), lambda n: (0, n))
    weight = pl.BlockSpec((width, tile), lambda n: (0, n))
    fixed = pl.BlockSpec((count, width), lambda n: (0, 0), pipeline_mode=pl.Buffered(1))
    return pl.pallas_call(
        functools.partial(_feed_forward_tile, groups),
        grid=(units // tile,),
        in_specs=[fixed] * groups + [block, weight, weight],
        out_specs=[block] * 3 + [pl.BlockSpec((total, width), lambda n: (0, 0))],
        out_shape=[jax.ShapeDtypeStruct((total, units), BF16)] * 3
        + [jax.ShapeDtypeStruct((total, width), BF16)],
        compiler_params=pltpu.CompilerParams(vmem_limit_bytes=56 * 2**20),
        cost_estimate=pl.CostEstimate(
            flops=4 * total * width * units,
            bytes_accessed=4 * width * units + 8 * total * units + 4 * total * width,
            transcendentals=total * units,
        ),
    )(*pieces, hidden_back, gate, up)


def _stacked_grads(rows, cots, gate_back, up_back, hidden, out):
    size = rows.shape[1]
    for n, (left, right) in enumerate(((rows, gate_back), (rows, up_back), (cots, hidden))):
        out[n * size : (n + 1) * size, :] = lax.dot_general(
            left[...], right[...], (((0,), (0,)), ((), ())), preferred_element_type=F32
        ).astype(BF16)


def stacked_grads(ways, rows, cots, gate_back, up_back, hidden):
    lines, width = rows.shape
    units = hidden.shape[1]
    size = width // ways
    if size % 128:
        terms = [mm_tn(rows, gate_back), mm_tn(rows, up_back), mm_tn(cots, hidden)]
        cut = [term.astype(BF16).reshape(ways, size, units) for term in terms]
        return jnp.concatenate(cut, axis=1).reshape(-1, units)
    column = pl.BlockSpec((lines, size), lambda g: (0, g))
    whole = pl.BlockSpec((lines, units), lambda g: (0, 0))
    return pl.pallas_call(
        _stacked_grads,
        grid=(ways,),
        in_specs=[column, column, whole, whole, whole],
        out_specs=pl.BlockSpec((3 * size, units), lambda g: (g, 0)),
        out_shape=jax.ShapeDtypeStruct((3 * width, units), BF16),
        compiler_params=pltpu.CompilerParams(vmem_limit_bytes=32 * 2**20),
        cost_estimate=pl.CostEstimate(
            flops=6 * lines * width * units,
            bytes_accessed=6 * width * units + 6 * lines * units,
            transcendentals=0,
        ),
    )(rows, cots, gate_back, up_back, hidden)


def after(value, *first):
    return lax.optimization_barrier((value, *first))[0]


def shards(
    prefix_tokens,
    action_tokens,
    block_ids,
    live_dims,
    hidden_counts,
    pre_attn_gain,
    pre_mlp_gain,
    act_attn_gain,
    act_mlp_gain,
    pre_query,
    pre_keyval,
    pre_output,
    act_query,
    act_keyval,
    act_output,
    pre_gate,
    pre_up,
    pre_down,
    act_gate,
    act_up,
    act_down,
    action_head,
    prefix_cot,
    pred_cot,
):
    groups = lax.axis_size("mp")
    ways = lax.axis_size("dp")
    member = lax.axis_index("mp")
    items, pre_rows, width = prefix_tokens.shape
    act_rows, act_width = action_tokens.shape[1:]
    pre_len = pre_rows * groups
    head_dim = pre_keyval.shape[1] // 2
    query_width = pre_query.shape[1]
    heads = query_width // head_dim
    local_len = pre_rows + act_rows
    scale = head_dim ** (-0.5)
    order = rel_blocks()
    LINKS.done.clear()

    pre_part, act_part, out_part = pre_query.shape[0], act_query.shape[0], pre_output.shape[0]
    qkv_own = jnp.concatenate(
        [
            jnp.concatenate([pre_query, pre_keyval], axis=1),
            jnp.concatenate([act_query, act_keyval], axis=1),
        ],
        axis=0,
    )
    out_own = jnp.concatenate([pre_output, act_output], axis=1)

    def in_place(pieces):
        size = pieces[0].shape[0]
        twice = jnp.concatenate(pieces[::-1] * 2, axis=0)
        return lax.dynamic_slice_in_dim(twice, (groups - 1 - member) * size, groups * size, 0)

    qkv_ring = ring_gather(qkv_own)
    out_ring = ring_gather(out_own)
    qkv_block = jnp.concatenate(
        [
            in_place([piece[:pre_part] for piece in qkv_ring]),
            in_place([piece[pre_part:] for piece in qkv_ring]),
        ],
        axis=0,
    )
    pre_block = groups * pre_part
    out_block = in_place(out_ring)
    gate_full = lax.all_gather(pre_gate, "dp", axis=0, tiled=True)
    down_full = lax.all_gather(pre_down, "dp", axis=1, tiled=True)
    act_stack = jnp.concatenate([act_gate, act_up, act_down.T], axis=0)
    act_flat_w = lax.all_gather(act_stack, "dp", axis=0, tiled=True)
    up_full = lax.all_gather(after(pre_up, act_flat_w), "dp", axis=0, tiled=True)
    act_all = act_flat_w.reshape(ways, 3, -1, act_gate.shape[1])
    act_gate_full, act_up_full, act_down_full = (
        act_all[:, n].reshape(act_width, -1) for n in range(3)
    )

    pre_flat = prefix_tokens.reshape(items * pre_rows, width)
    act_flat = action_tokens.reshape(items * act_rows, act_width)
    cot_flat = prefix_cot.reshape(items * pre_rows, width)
    pre_x = pre_flat.astype(F32)
    act_x = act_flat.astype(F32)
    live_mask = live_dims[:, None, :].astype(F32)
    pred_back = (pred_cot * live_mask).astype(BF16).reshape(items * act_rows, -1)
    act_final_back = mm_nt(pred_back, action_head)
    count = items * pre_rows
    padded = -(-count // 16) * 16
    act_count = items * act_rows

    def pad(values):
        return jnp.pad(values, ((0, padded - count), (0, 0)))

    def ring_stack(value):
        return jnp.concatenate(ring_gather(value), axis=0)

    cot_pieces = ring_gather(pad(cot_flat))
    qkv_pieces, cot_pieces = dp_gather(qkv_block, cot_pieces)
    qkv_full = jnp.concatenate(qkv_pieces, axis=0)
    out_full = jnp.concatenate(dp_gather(out_block), axis=0)
    cot_all = jnp.concatenate(cot_pieces, axis=0)
    act_cot_all = ring_stack(act_final_back.astype(BF16))
    hidden_back = mm_nt(cot_all, down_full).astype(BF16)

    local_pos = jnp.concatenate(
        [
            member * pre_rows + jnp.arange(pre_rows),
            pre_len + member * act_rows + jnp.arange(act_rows),
        ]
    )
    cosine_tab, sine_tab = rope_tables(local_pos, head_dim)

    def blocks_of(which):
        return jnp.concatenate(
            [
                lax.dynamic_slice_in_dim(block_ids, which * pre_rows, pre_rows, 1),
                lax.dynamic_slice_in_dim(block_ids, pre_len + which * act_rows, act_rows, 1),
            ],
            axis=1,
        )

    local_blocks = blocks_of(member)
    key_blocks = jnp.concatenate(
        [blocks_of((member - r) % groups) for r in range(groups)], axis=1
    )
    allowed = key_blocks[:, None, None, :] <= local_blocks[:, None, :, None]

    act_padded = -(-act_count // 16) * 16

    def stack(pre_part_rows, act_part_rows):
        return (
            jnp.pad(pre_part_rows, ((0, padded - count), (0, 0))),
            jnp.pad(act_part_rows, ((0, act_padded - act_count), (0, 0))),
        )

    def to_items(joint):
        return jnp.concatenate(
            [
                joint[:count].reshape(items, pre_rows, -1),
                joint[padded : padded + act_count].reshape(items, act_rows, -1),
            ],
            axis=1,
        )

    def from_items(values):
        return jnp.concatenate(
            stack(
                values[:, :pre_rows].reshape(count, -1),
                values[:, pre_rows:].reshape(act_count, -1),
            ),
            axis=0,
        )

    normed = spread(
        *stack(
            rms_norm(pre_x, pre_attn_gain).astype(BF16),
            rms_norm(act_x, act_attn_gain).astype(BF16),
        ),
        order,
    )
    keyval_raw = to_items(mm(normed, qkv_full[:, query_width:]))
    keyval_rows = jnp.concatenate(
        [rotate(keyval_raw[..., :head_dim], cosine_tab, sine_tab), keyval_raw[..., head_dim:]],
        axis=-1,
    ).astype(BF16)
    all_keyval = jnp.concatenate(ring_gather(keyval_rows), axis=1)
    key_rows = all_keyval[..., :head_dim]
    value_rows = all_keyval[..., head_dim:]
    query_raw = to_items(mm(normed, qkv_full[:, :query_width]))
    query_rows = rotate(
        query_raw.reshape(items, local_len, heads, head_dim),
        cosine_tab[:, None, :],
        sine_tab[:, None, :],
    ).astype(BF16)
    scores = (
        jnp.einsum("iqhd,ikd->ihqk", query_rows, key_rows, preferred_element_type=F32) * scale
    )
    probs = jax.nn.softmax(jnp.where(allowed, scores, MASKED), axis=-1)
    probs_low = probs.astype(BF16)
    attended = jnp.einsum("ihqk,ikd->iqhd", probs_low, value_rows, preferred_element_type=F32)
    attended = attended.astype(BF16).reshape(items, local_len, query_width)
    (att_joint,) = permute_columns([from_items(attended)], order)
    mid = mm(att_joint, out_full)
    pre_mid = pre_x + mid[:count, :width]
    act_mid = act_x + mid[padded : padded + act_count, width:]

    act_second = rms_norm(act_mid, act_mlp_gain).astype(BF16)
    act_all_rows = jnp.concatenate(ring_gather(act_second, LOOSE), axis=0)
    pre_second = pad(rms_norm(pre_mid, pre_mlp_gain).astype(BF16))
    first_piece, hidden_back, act_all_rows = lax.optimization_barrier(
        (ring(pre_second, 1), hidden_back, act_all_rows)
    )
    second_pieces = [pre_second, first_piece]
    slot_count = lax.dynamic_index_in_dim(hidden_counts, member, keepdims=False)
    slot_live = (jnp.arange(act_gate.shape[1]) < slot_count).astype(F32)

    def scatter_sum(value, dimension):
        return lax.psum_scatter(value, "dp", scatter_dimension=dimension, tiled=True)

    def split(partial):
        size = partial.shape[0] // groups
        return [partial[r * size : (r + 1) * size] for r in range(groups)]

    act_hidden, act_gate_back, act_up_back = feed_forward(
        act_all_rows, act_cot_all, act_gate_full, act_up_full, act_down_full, slot_live
    )
    act_second_part = split(mm_nt(act_gate_back, act_gate_full) + mm_nt(act_up_back, act_up_full))
    act_sum_part = split(mm_nt(act_hidden, act_down_full))

    for r in range(2, groups):
        piece = ring(second_pieces[-1], 1)
        if r == 2:
            piece, act_gate_back, act_up_back, act_hidden = lax.optimization_barrier(
                (piece, act_gate_back, act_up_back, act_hidden)
            )
            act_stacked = stacked_grads(
                ways, act_all_rows, act_cot_all, act_gate_back, act_up_back, act_hidden
            )
        if r == groups - 1:
            piece = after(piece, act_stacked)
        second_pieces.append(piece)
    grad_act = scatter_sum(act_stacked, 0)

    pre_hidden, pre_gate_back, pre_up_back, pre_all = feed_forward_kernel(
        second_pieces, hidden_back, gate_full, up_full
    )
    gate_term = mm_tn(pre_all, pre_gate_back).astype(BF16)
    gate_term, pre_up_back, grad_act = lax.optimization_barrier(
        (gate_term, pre_up_back, grad_act)
    )
    grad_act = grad_act.astype(F32).reshape(3, -1, act_gate.shape[1])
    grad_act_gate, grad_act_up, grad_act_down = grad_act[0], grad_act[1], grad_act[2].T
    grad_pre_gate = scatter_sum(gate_term, 0)
    half = groups // 2 * padded

    def second_rows(cut, gate_rows, up_rows):
        return mm_nt(gate_rows[cut], gate_full) + mm_nt(up_rows[cut], up_full)

    later = second_rows(slice(half, None), pre_gate_back, pre_up_back)
    later, gate_rows, up_rows = lax.optimization_barrier((later, pre_gate_back, pre_up_back))
    sooner = second_rows(slice(0, half), gate_rows, up_rows)

    act_lines = act_count * act_width // width

    def lines(value):
        return value.reshape(act_lines, width)

    def second_part(r):
        rows = sooner if r < groups // 2 else later
        rows = rows[r % (groups // 2) * padded :][:count]
        return jnp.concatenate([rows, lines(act_second_part[r]), lines(act_sum_part[r])], axis=0)

    up_term = down_term = None
    total = second_part(groups - 1)
    for r in range(groups - 2, -1, -1):
        moved = ring(total.astype(BF16), -1, LOOSE)
        if r == groups - 2:
            moved, up_rows = lax.optimization_barrier((moved, after(up_rows, sooner)))
            up_term = mm_tn(pre_all, up_rows).astype(BF16)
        elif r == groups - 3:
            moved, up_term, pre_hidden = lax.optimization_barrier((moved, up_term, pre_hidden))
            down_term = mm_tn(pre_hidden, cot_all).astype(BF16)
        elif r == groups - 4:
            moved, down_term = lax.optimization_barrier((moved, down_term))
        total = moved.astype(F32) + second_part(r)
    grad_pre_up = scatter_sum(up_term, 0)
    grad_pre_down = scatter_sum(down_term, 1)
    pre_second_back = total[:count]
    act_second_back = total[count : count + act_lines].reshape(act_count, act_width)
    act_sums = total[count + act_lines :].reshape(act_count, act_width)

    pre_mid_part, grad_pre_mlp_gain = rms_back(pre_mid, pre_mlp_gain, pre_second_back)
    act_mid_part, grad_act_mlp_gain = rms_back(act_mid, act_mlp_gain, act_second_back)
    pre_mid_grad = cot_flat.astype(F32) + pre_mid_part
    act_mid_grad = act_final_back + act_mid_part
    back_joint = jnp.concatenate(
        [
            jnp.pad(pre_mid_grad.astype(BF16), ((0, padded - count), (0, act_width))),
            jnp.pad(act_mid_grad.astype(BF16), ((0, act_padded - act_count), (width, 0))),
        ],
        axis=0,
    )
    attended_back = to_items(
        permute_columns([mm_nt(back_joint, out_full).astype(BF16)], order, True)[0]
    ).reshape(items, local_len, heads, head_dim)
    out_half = query_width // 2
    out_sums = chip_sums(
        mm_tn(att_joint[:, :out_half], back_joint).astype(BF16),
        mm_tn(att_joint[:, out_half:], back_joint).astype(BF16),
    ).astype(BF16)
    probs_back = jnp.einsum(
        "iqhd,ikd->ihqk", attended_back, value_rows, preferred_element_type=F32
    )
    value_back = jnp.einsum(
        "ihqk,iqhd->ikd", probs_low, attended_back, preferred_element_type=F32
    )
    scores_back = (
        probs * (probs_back - jnp.sum(probs * probs_back, axis=-1, keepdims=True))
    ).astype(BF16)
    key_back = (
        jnp.einsum("ihqk,iqhd->ikd", scores_back, query_rows, preferred_element_type=F32) * scale
    )
    query_back = (
        jnp.einsum("ihqk,ikd->iqhd", scores_back, key_rows, preferred_element_type=F32) * scale
    )
    keyval_back = jnp.concatenate([key_back, value_back], axis=-1).astype(BF16)
    own_kv_back = ring_scatter(
        [keyval_back[:, r * local_len : (r + 1) * local_len] for r in range(groups)]
    )
    keyval_low = jnp.concatenate(
        [rotate(own_kv_back[..., :head_dim], cosine_tab, -sine_tab), own_kv_back[..., head_dim:]],
        axis=-1,
    ).astype(BF16)
    query_low = rotate(query_back, cosine_tab[:, None, :], -sine_tab[:, None, :])
    query_low = query_low.reshape(items, local_len, query_width).astype(BF16)
    back_rows = from_items(jnp.concatenate([query_low, keyval_low], axis=-1))
    back_rows, grad_pre_gate, out_sums = lax.optimization_barrier(
        (back_rows, grad_pre_gate, out_sums)
    )
    qkv_half = normed.shape[1] // 2
    qkv_own_part = mm_tn(normed[:, :qkv_half], back_rows).astype(BF16)
    qkv_other_part = mm_tn(normed[:, qkv_half:], back_rows).astype(BF16)
    qkv_sums = chip_sums(qkv_own_part, qkv_other_part).astype(BF16)
    act_final_low = (act_mid + act_sums).astype(BF16)
    action_pred = mm(act_final_low, action_head).reshape(pred_cot.shape) * live_mask
    grad_head = mm_tn(act_final_low, pred_back)
    pre_normed_back, act_normed_back = unspread(
        mm_nt(back_rows, qkv_full), padded, width, act_width, order
    )
    pre_normed_back, act_normed_back = pre_normed_back[:count], act_normed_back[:act_count]
    pre_x_part, grad_pre_attn_gain = rms_back(pre_x, pre_attn_gain, pre_normed_back)
    act_x_part, grad_act_attn_gain = rms_back(act_x, act_attn_gain, act_normed_back)
    prefix_grad = (pre_mid_grad + pre_x_part).reshape(prefix_tokens.shape)
    action_grad = (act_mid_grad + act_x_part).reshape(action_tokens.shape)

    devices = ways * groups
    small = jnp.concatenate(
        [
            value.reshape(devices, -1)
            for value in (
                grad_pre_attn_gain,
                grad_pre_mlp_gain,
                grad_act_attn_gain,
                grad_act_mlp_gain,
                grad_head,
            )
        ],
        axis=1,
    )
    small = small + hop(small, 1)
    spare = -(-groups // 8) * 8 - groups
    sent_blocks = []
    for c in range(ways // 2):
        start = jnp.bitwise_xor(lax.axis_index("dp"), 2 * c) * groups
        lines = lax.dynamic_slice_in_dim(small, start, groups, 0)
        lines = jnp.pad(lines, ((0, spare), (0, qkv_sums.shape[2] - small.shape[1])))
        sent_blocks.append(jnp.concatenate([qkv_sums[c], lines.astype(BF16)], axis=0))
    sent_blocks, out_sums, pre_hidden = lax.optimization_barrier(
        (sent_blocks, out_sums, pre_hidden)
    )
    arrived = send_blocks(sent_blocks)
    out_arrived = send_blocks(out_sums)
    pre_sum_part = split(mm(pre_hidden, down_full).astype(BF16))
    sum_parts = [each[:count] for each in pre_sum_part]
    sums_arrived = send_members(sum_parts)
    arrived, out_arrived = lax.optimization_barrier((arrived, out_arrived))
    qkv_parts = member_parts(
        add_up(sent_blocks[0].astype(F32), arrived).astype(BF16), (pre_part, act_part, 1)
    )
    qkv_arrived = send_members(qkv_parts)
    out_parts = member_parts(
        add_up(out_sums[0].astype(F32), out_arrived).astype(BF16), (out_part,)
    )
    out_arrived = send_members(out_parts)
    sums_arrived, grad_pre_up, grad_pre_down, qkv_first = lax.optimization_barrier(
        (sums_arrived, grad_pre_up, grad_pre_down, qkv_parts[0])
    )
    pre_sums = add_up(sum_parts[0].astype(F32), sums_arrived)
    prefix_out = (pre_mid + pre_sums).astype(BF16).reshape(prefix_tokens.shape)
    grad_out = add_up(out_parts[0].astype(F32), out_arrived)
    grad_qkv = add_up(qkv_first.astype(F32), qkv_arrived)
    total = grad_qkv[pre_part + act_part :, : small.shape[1]]
    sizes = [width // devices] * 2 + [act_width // devices] * 2
    gains, start = [], 0
    for size in sizes:
        gains.append(total[0, start : start + size])
        start += size
    grad_head = total[0, start:].reshape(act_width // devices, -1)

    return (
        prefix_out,
        action_pred,
        prefix_grad,
        action_grad,
        *gains,
        grad_qkv[:pre_part, :query_width],
        grad_qkv[:pre_part, query_width:],
        grad_out[:, :width],
        grad_qkv[pre_part : pre_part + act_part, :query_width],
        grad_qkv[pre_part : pre_part + act_part, query_width:],
        grad_out[:, width:],
        grad_pre_gate.astype(F32),
        grad_pre_up.astype(F32),
        grad_pre_down.astype(F32),
        grad_act_gate,
        grad_act_up,
        grad_act_down,
        grad_head,
    )


def solution(mesh):
    rows = P("dp", "mp", None)
    both = P(("dp", "mp"), None)
    wide = P("dp", "mp")
    tall = P("mp", "dp")
    in_specs = (
        (rows, rows, P("dp", None), P("dp", None))
        + (P(),) * 5
        + (both,) * 6
        + (wide, wide, tall, wide, wide, tall, P(), rows, rows)
    )
    out_specs = (
        (rows,) * 4
        + (P(("dp", "mp")),) * 4
        + (both,) * 6
        + (wide, wide, tall, wide, wide, tall, both)
    )
    return jax.shard_map(shards, mesh=mesh, in_specs=in_specs, out_specs=out_specs, check_vma=False)
```

```python
import functools

import jax
import jax.numpy as jnp
from jax import lax
from jax.experimental import pallas as pl
from jax.experimental.pallas import tpu as pltpu
from jax.sharding import PartitionSpec as P

NORM_EPS = 1e-06
ROPE_BASE = 10000.0
MASKED = -1e30
F32 = jnp.float32
BF16 = jnp.bfloat16


class Links:
    def __init__(self, window=2):
        self.window = window
        self.done = {}

    def send(self, value, axis, pairs, link):
        sent = self.done.setdefault(link, [])
        if len(sent) >= self.window:
            value, _ = lax.optimization_barrier((value, sent[-self.window]))
        result = lax.ppermute(value, axis, pairs)
        sent.append(result)
        return result


LINKS = Links()


def hop(value, bit):
    size = lax.axis_size("dp")
    pairs = [(d, d ^ bit) for d in range(size)]
    if bit == 1:
        return lax.ppermute(value, "dp", pairs)
    return LINKS.send(value, "dp", pairs, bit)


LOOSE = None


def ring(value, step, link="mp"):
    size = lax.axis_size("mp")
    pairs = [(d, (d + step) % size) for d in range(size)]
    if link is LOOSE:
        return lax.ppermute(value, "mp", pairs)
    return LINKS.send(value, "mp", pairs, link)


def ring_gather(value, link="mp"):
    out = [value]
    for _ in range(lax.axis_size("mp") - 1):
        out.append(ring(out[-1], 1, link))
    return out


def ring_scatter(parts, steps=None):
    total = parts[-1].astype(BF16)
    for part in parts[-2::-1]:
        moved = ring(total.astype(BF16), -1, LOOSE)
        if steps is not None:
            steps.append(moved)
        total = moved.astype(F32) + part.astype(F32)
    return total


def chip_order(size):
    return sorted(range(1, size), key=lambda c: (bin(c).count("1"), c))


def rel_blocks():
    size = lax.axis_size("dp")
    place = jnp.arange(size, dtype=jnp.int32)
    half = size // 2
    rel = (place % half) * 2 + place // half
    return jnp.bitwise_xor(rel, lax.axis_index("dp").astype(jnp.int32))


def dp_gather(shard, hold=None):
    chips = lax.axis_size("dp") // 2
    half = shard.shape[0] // 2
    got = {0: [shard]}

    def top(c):
        return got[c][0] if len(got[c]) == 2 else got[c][0][:half]

    def bottom(c):
        return got[c][1] if len(got[c]) == 2 else got[c][0][half:]

    for c in chip_order(chips):
        high, low = 1 << (c.bit_length() - 1), c & -c
        if high == low:
            got[c] = [hop(shard, 2 * high)]
        else:
            got[c] = [hop(top(c ^ high), 2 * high), hop(bottom(c ^ low), 2 * low)]
    own = [piece for c in range(chips) for piece in got[c]]
    if hold is not None:
        own, hold = lax.optimization_barrier((own, hold))
        return own + [hop(piece, 1) for piece in own], hold
    return own + [hop(piece, 1) for piece in own]


def chip_sums(own, other):
    chips = lax.axis_size("dp") // 2
    total = own.astype(F32) + hop(other, 1).astype(F32)
    return total.reshape(chips, -1, own.shape[1])


def chips_sum(blocks):
    size = lax.axis_size("dp")
    cut = blocks[0].shape[0] // 16 * 8
    bits = [1 << n for n in range((size // 2).bit_length() - 1)]
    halves = []
    for rows, turns in ((slice(0, cut), bits), (slice(cut, None), bits[::-1])):
        kept = {c: block[rows].astype(F32) for c, block in enumerate(blocks)}
        for bit in turns:
            sent = sorted(c for c in kept if c & bit)
            moved = jnp.concatenate([kept.pop(c).astype(BF16) for c in sent], axis=0)
            moved = lax.ppermute(moved, "dp", [(d, d ^ (2 * bit)) for d in range(size)])
            lines = moved.shape[0] // len(sent)
            for n, c in enumerate(sent):
                kept[c ^ bit] = kept[c ^ bit] + moved[n * lines : (n + 1) * lines].astype(F32)
        halves.append(kept[0])
    return jnp.concatenate(halves, axis=0)


def send_members(parts):
    size = lax.axis_size("mp")
    return [
        lax.ppermute(parts[r], "mp", [(d, (d - r) % size) for d in range(size)])
        for r in range(1, size)
    ]


def add_up(first, arrived):
    total = first
    for each in arrived:
        total = total + each.astype(F32)
    return total


def member_parts(values, layout):
    groups = lax.axis_size("mp")
    axis = values.ndim - 2
    parts = []
    for r in range(groups):
        which = (lax.axis_index("mp") - r) % groups
        cuts, start = [], 0
        for part in layout:
            cuts.append(lax.dynamic_slice_in_dim(values, start + which * part, part, axis))
            start += groups * part
        parts.append(jnp.concatenate(cuts, axis=axis))
    return parts


def _permute_blocks(inverse, order, *refs):
    half = len(refs) // 2
    for src, dst in zip(refs[:half], refs[half:]):
        block = src.shape[1] // order.shape[0]
        for g in range(order.shape[0]):
            here = slice(g * block, (g + 1) * block)
            there = pl.ds(pl.multiple_of(order[g] * block, block), block)
            if inverse:
                dst[:, there] = src[:, here]
            else:
                dst[:, here] = src[:, there]


def permute_columns(arrays, order, inverse=False):
    count = order.shape[0]
    if any(values.shape[1] // count % 128 for values in arrays):
        hit = order[:, None] == jnp.arange(count, dtype=order.dtype)[None, :]
        places = jnp.arange(count, dtype=order.dtype)
        back = jnp.sum(jnp.where(hit, places[:, None], 0), axis=0) if inverse else order
        outs = []
        for values in arrays:
            split = values.reshape(values.shape[0], count, -1)
            cuts = [lax.dynamic_slice_in_dim(split, back[g], 1, 1) for g in range(count)]
            outs.append(jnp.concatenate(cuts, axis=1).reshape(values.shape))
        return outs
    return pl.pallas_call(
        functools.partial(_permute_blocks, inverse),
        in_specs=[pl.BlockSpec(memory_space=pltpu.SMEM)]
        + [pl.BlockSpec(memory_space=pltpu.VMEM)] * len(arrays),
        out_specs=[pl.BlockSpec(memory_space=pltpu.VMEM)] * len(arrays),
        out_shape=[jax.ShapeDtypeStruct(values.shape, values.dtype) for values in arrays],
        compiler_params=pltpu.CompilerParams(vmem_limit_bytes=32 * 2**20),
    )(order, *arrays)


def _spread(count, order, pre, act, joint):
    rows = pre.shape[0]
    narrow = [value.shape[1] // count for value in (pre, act)]
    joint[...] = jnp.zeros_like(joint)
    for g in range(count):
        start = g * sum(narrow)
        there = pl.ds(pl.multiple_of(order[g] * narrow[0], narrow[0]), narrow[0])
        joint[:rows, start : start + narrow[0]] = pre[:, there]
        there = pl.ds(pl.multiple_of(order[g] * narrow[1], narrow[1]), narrow[1])
        joint[rows:, start + narrow[0] : start + sum(narrow)] = act[:, there]


def _unspread(count, order, joint, pre, act):
    rows = pre.shape[0]
    narrow = [value.shape[1] // count for value in (pre, act)]
    for g in range(count):
        start = g * sum(narrow)
        there = pl.ds(pl.multiple_of(order[g] * narrow[0], narrow[0]), narrow[0])
        pre[:, there] = joint[:rows, start : start + narrow[0]]
        there = pl.ds(pl.multiple_of(order[g] * narrow[1], narrow[1]), narrow[1])
        act[:, there] = joint[rows:, start + narrow[0] : start + sum(narrow)]


def block_call(body, order, arrays, shapes):
    return pl.pallas_call(
        functools.partial(body, order.shape[0]),
        in_specs=[pl.BlockSpec(memory_space=pltpu.SMEM)]
        + [pl.BlockSpec(memory_space=pltpu.VMEM)] * len(arrays),
        out_specs=[pl.BlockSpec(memory_space=pltpu.VMEM)] * len(shapes),
        out_shape=shapes,
        compiler_params=pltpu.CompilerParams(vmem_limit_bytes=32 * 2**20),
    )(order, *arrays)


def spread(pre, act, order):
    count = order.shape[0]
    rows, lines = pre.shape[0], act.shape[0]
    wide, thin = pre.shape[1] // count, act.shape[1] // count
    if wide % 128 or thin % 128:
        upper, lower = permute_columns([pre, act], order)
        upper = jnp.pad(upper.reshape(rows, count, wide), ((0, lines), (0, 0), (0, thin)))
        lower = jnp.pad(lower.reshape(lines, count, thin), ((rows, 0), (0, 0), (wide, 0)))
        return (upper + lower).reshape(rows + lines, -1)
    shape = jax.ShapeDtypeStruct((rows + lines, pre.shape[1] + act.shape[1]), pre.dtype)
    return block_call(_spread, order, [pre, act], [shape])[0]


def unspread(joint, rows, wide, thin, order):
    count = order.shape[0]
    lines = joint.shape[0] - rows
    if wide // count % 128 or thin // count % 128:
        blocks = joint.reshape(joint.shape[0], count, -1)
        upper = blocks[:rows, :, : wide // count].reshape(rows, wide)
        lower = blocks[rows:, :, wide // count :].reshape(lines, thin)
        return permute_columns([upper, lower], order, True)
    shapes = [
        jax.ShapeDtypeStruct((rows, wide), joint.dtype),
        jax.ShapeDtypeStruct((lines, thin), joint.dtype),
    ]
    return block_call(_unspread, order, [joint], shapes)


def inverse_rms(values):
    return lax.rsqrt(jnp.mean(values * values, axis=-1, keepdims=True) + NORM_EPS)


def rms_norm(values, gain_vec):
    return values * inverse_rms(values) * gain_vec


def rms_back(values, gain_vec, grads):
    inverse = inverse_rms(values)
    unit = values * inverse
    scaled = gain_vec * grads
    mean = jnp.mean(unit * scaled, axis=-1, keepdims=True)
    return inverse * (scaled - unit * mean), jnp.sum(grads * unit, axis=0)


def rope_tables(positions, head_dim):
    half_dim = head_dim // 2
    inverse = ROPE_BASE ** (-2.0 * jnp.arange(half_dim).astype(F32) / head_dim)
    angles = positions.astype(F32)[:, None] * inverse[None, :]
    return (jnp.cos(angles), jnp.sin(angles))


def rotate(values, cosine_tab, sine_tab):
    half_dim = values.shape[-1] // 2
    lower_half = values[..., :half_dim]
    upper_half = values[..., half_dim:]
    return jnp.concatenate(
        [
            lower_half * cosine_tab - upper_half * sine_tab,
            upper_half * cosine_tab + lower_half * sine_tab,
        ],
        axis=-1,
    )


def mm(left, right):
    return lax.dot_general(left, right, (((1,), (0,)), ((), ())), preferred_element_type=F32)


def mm_nt(left, right):
    return lax.dot_general(left, right, (((1,), (1,)), ((), ())), preferred_element_type=F32)


def mm_tn(left, right):
    return lax.dot_general(left, right, (((0,), (0,)), ((), ())), preferred_element_type=F32)


def geglu(gate_val, up_val, live_mask):
    return jax.nn.gelu(gate_val, approximate=True) * up_val * live_mask


def feed_forward(rows, cot_rows, gate, up, down_t, live_mask):
    gate_val = mm(rows, gate)
    up_val = mm(rows, up)
    hidden_back = mm(cot_rows, down_t)
    hidden, pull = jax.vjp(lambda g, u: geglu(g, u, live_mask), gate_val, up_val)
    gate_back, up_back = pull(hidden_back)
    return hidden.astype(BF16), gate_back.astype(BF16), up_back.astype(BF16)


def _feed_forward_tile(groups, *refs):
    pieces, (back_ref, gate_ref, up_ref) = refs[:groups], refs[groups : groups + 3]
    hidden_ref, gate_back_ref, up_back_ref, rows_ref = refs[groups + 3 :]
    count = pieces[0].shape[0]
    root, cube = 0.7978845608028654, 0.044715

    @pl.when(pl.program_id(0) == 0)
    def _():
        for r in range(groups):
            rows_ref[r * count : (r + 1) * count, :] = pieces[r][...]

    for r in range(groups):
        cut = slice(r * count, (r + 1) * count)
        rows = pieces[r][...]
        gate_val = jnp.dot(rows, gate_ref[...], preferred_element_type=F32)
        up_val = jnp.dot(rows, up_ref[...], preferred_element_type=F32)
        back = back_ref[cut, :].astype(F32)
        square = gate_val * gate_val
        bend = jnp.tanh(root * gate_val * (1.0 + cube * square))
        half_open = 0.5 * (1.0 + bend)
        active = gate_val * half_open
        inner = (0.5 * root) * gate_val * (1.0 - bend * bend) * (1.0 + 3.0 * cube * square)
        hidden_ref[cut, :] = (active * up_val).astype(BF16)
        gate_back_ref[cut, :] = (back * up_val * (half_open + inner)).astype(BF16)
        up_back_ref[cut, :] = (back * active).astype(BF16)


def feed_forward_kernel(pieces, hidden_back, gate, up, tile=512):
    groups = len(pieces)
    count, width = pieces[0].shape
    total = groups * count
    units = gate.shape[1]
    block = pl.BlockSpec((total, tile), lambda n: (0, n))
    weight = pl.BlockSpec((width, tile), lambda n: (0, n))
    fixed = pl.BlockSpec((count, width), lambda n: (0, 0), pipeline_mode=pl.Buffered(1))
    return pl.pallas_call(
        functools.partial(_feed_forward_tile, groups),
        grid=(units // tile,),
        in_specs=[fixed] * groups + [block, weight, weight],
        out_specs=[block] * 3 + [pl.BlockSpec((total, width), lambda n: (0, 0))],
        out_shape=[jax.ShapeDtypeStruct((total, units), BF16)] * 3
        + [jax.ShapeDtypeStruct((total, width), BF16)],
        compiler_params=pltpu.CompilerParams(vmem_limit_bytes=56 * 2**20),
        cost_estimate=pl.CostEstimate(
            flops=4 * total * width * units,
            bytes_accessed=4 * width * units + 8 * total * units + 4 * total * width,
            transcendentals=total * units,
        ),
    )(*pieces, hidden_back, gate, up)


def _stacked_grads(rows, cots, gate_back, up_back, hidden, out):
    size = rows.shape[1]
    for n, (left, right) in enumerate(((rows, gate_back), (rows, up_back), (cots, hidden))):
        out[n * size : (n + 1) * size, :] = lax.dot_general(
            left[...], right[...], (((0,), (0,)), ((), ())), preferred_element_type=F32
        ).astype(BF16)


def stacked_grads(ways, rows, cots, gate_back, up_back, hidden):
    lines, width = rows.shape
    units = hidden.shape[1]
    size = width // ways
    if size % 128:
        terms = [mm_tn(rows, gate_back), mm_tn(rows, up_back), mm_tn(cots, hidden)]
        cut = [term.astype(BF16).reshape(ways, size, units) for term in terms]
        return jnp.concatenate(cut, axis=1).reshape(-1, units)
    column = pl.BlockSpec((lines, size), lambda g: (0, g))
    whole = pl.BlockSpec((lines, units), lambda g: (0, 0))
    return pl.pallas_call(
        _stacked_grads,
        grid=(ways,),
        in_specs=[column, column, whole, whole, whole],
        out_specs=pl.BlockSpec((3 * size, units), lambda g: (g, 0)),
        out_shape=jax.ShapeDtypeStruct((3 * width, units), BF16),
        compiler_params=pltpu.CompilerParams(vmem_limit_bytes=32 * 2**20),
        cost_estimate=pl.CostEstimate(
            flops=6 * lines * width * units,
            bytes_accessed=6 * width * units + 6 * lines * units,
            transcendentals=0,
        ),
    )(rows, cots, gate_back, up_back, hidden)


def after(value, *first):
    return lax.optimization_barrier((value, *first))[0]


def shards(
    prefix_tokens,
    action_tokens,
    block_ids,
    live_dims,
    hidden_counts,
    pre_attn_gain,
    pre_mlp_gain,
    act_attn_gain,
    act_mlp_gain,
    pre_query,
    pre_keyval,
    pre_output,
    act_query,
    act_keyval,
    act_output,
    pre_gate,
    pre_up,
    pre_down,
    act_gate,
    act_up,
    act_down,
    action_head,
    prefix_cot,
    pred_cot,
):
    groups = lax.axis_size("mp")
    ways = lax.axis_size("dp")
    member = lax.axis_index("mp")
    items, pre_rows, width = prefix_tokens.shape
    act_rows, act_width = action_tokens.shape[1:]
    pre_len = pre_rows * groups
    head_dim = pre_keyval.shape[1] // 2
    query_width = pre_query.shape[1]
    heads = query_width // head_dim
    local_len = pre_rows + act_rows
    scale = head_dim ** (-0.5)
    order = rel_blocks()
    LINKS.done.clear()

    pre_part, act_part, out_part = pre_query.shape[0], act_query.shape[0], pre_output.shape[0]
    qkv_own = jnp.concatenate(
        [
            jnp.concatenate([pre_query, pre_keyval], axis=1),
            jnp.concatenate([act_query, act_keyval], axis=1),
        ],
        axis=0,
    )
    out_own = jnp.concatenate([pre_output, act_output], axis=1)

    def in_place(pieces):
        size = pieces[0].shape[0]
        twice = jnp.concatenate(pieces[::-1] * 2, axis=0)
        return lax.dynamic_slice_in_dim(twice, (groups - 1 - member) * size, groups * size, 0)

    qkv_ring = ring_gather(qkv_own)
    out_ring = ring_gather(out_own)
    qkv_block = jnp.concatenate(
        [
            in_place([piece[:pre_part] for piece in qkv_ring]),
            in_place([piece[pre_part:] for piece in qkv_ring]),
        ],
        axis=0,
    )
    pre_block = groups * pre_part
    out_block = in_place(out_ring)
    gate_full = lax.all_gather(pre_gate, "dp", axis=0, tiled=True)
    down_full = lax.all_gather(pre_down, "dp", axis=1, tiled=True)
    act_stack = jnp.concatenate([act_gate, act_up, act_down.T], axis=0)
    act_flat_w = lax.all_gather(act_stack, "dp", axis=0, tiled=True)
    up_full = lax.all_gather(after(pre_up, act_flat_w), "dp", axis=0, tiled=True)
    act_all = act_flat_w.reshape(ways, 3, -1, act_gate.shape[1])
    act_gate_full, act_up_full, act_down_full = (
        act_all[:, n].reshape(act_width, -1) for n in range(3)
    )

    pre_flat = prefix_tokens.reshape(items * pre_rows, width)
    act_flat = action_tokens.reshape(items * act_rows, act_width)
    cot_flat = prefix_cot.reshape(items * pre_rows, width)
    pre_x = pre_flat.astype(F32)
    act_x = act_flat.astype(F32)
    live_mask = live_dims[:, None, :].astype(F32)
    pred_back = (pred_cot * live_mask).astype(BF16).reshape(items * act_rows, -1)
    act_final_back = mm_nt(pred_back, action_head)
    count = items * pre_rows
    padded = -(-count // 16) * 16
    act_count = items * act_rows

    def pad(values):
        return jnp.pad(values, ((0, padded - count), (0, 0)))

    def ring_stack(value):
        return jnp.concatenate(ring_gather(value), axis=0)

    cot_pieces = ring_gather(pad(cot_flat))
    qkv_pieces, cot_pieces = dp_gather(qkv_block, cot_pieces)
    qkv_full = jnp.concatenate(qkv_pieces, axis=0)
    out_full = jnp.concatenate(dp_gather(out_block), axis=0)
    cot_all = jnp.concatenate(cot_pieces, axis=0)
    act_cot_all = ring_stack(act_final_back.astype(BF16))
    hidden_back = mm_nt(cot_all, down_full).astype(BF16)

    local_pos = jnp.concatenate(
        [
            member * pre_rows + jnp.arange(pre_rows),
            pre_len + member * act_rows + jnp.arange(act_rows),
        ]
    )
    cosine_tab, sine_tab = rope_tables(local_pos, head_dim)

    def blocks_of(which):
        return jnp.concatenate(
            [
                lax.dynamic_slice_in_dim(block_ids, which * pre_rows, pre_rows, 1),
                lax.dynamic_slice_in_dim(block_ids, pre_len + which * act_rows, act_rows, 1),
            ],
            axis=1,
        )

    local_blocks = blocks_of(member)
    key_blocks = jnp.concatenate(
        [blocks_of((member - r) % groups) for r in range(groups)], axis=1
    )
    allowed = key_blocks[:, None, None, :] <= local_blocks[:, None, :, None]

    act_padded = -(-act_count // 16) * 16

    def stack(pre_part_rows, act_part_rows):
        return (
            jnp.pad(pre_part_rows, ((0, padded - count), (0, 0))),
            jnp.pad(act_part_rows, ((0, act_padded - act_count), (0, 0))),
        )

    def to_items(joint):
        return jnp.concatenate(
            [
                joint[:count].reshape(items, pre_rows, -1),
                joint[padded : padded + act_count].reshape(items, act_rows, -1),
            ],
            axis=1,
        )

    def from_items(values):
        return jnp.concatenate(
            stack(
                values[:, :pre_rows].reshape(count, -1),
                values[:, pre_rows:].reshape(act_count, -1),
            ),
            axis=0,
        )

    normed = spread(
        *stack(
            rms_norm(pre_x, pre_attn_gain).astype(BF16),
            rms_norm(act_x, act_attn_gain).astype(BF16),
        ),
        order,
    )
    keyval_raw = to_items(mm(normed, qkv_full[:, query_width:]))
    keyval_rows = jnp.concatenate(
        [rotate(keyval_raw[..., :head_dim], cosine_tab, sine_tab), keyval_raw[..., head_dim:]],
        axis=-1,
    ).astype(BF16)
    all_keyval = jnp.concatenate(ring_gather(keyval_rows), axis=1)
    key_rows = all_keyval[..., :head_dim]
    value_rows = all_keyval[..., head_dim:]
    query_raw = to_items(mm(normed, qkv_full[:, :query_width]))
    query_rows = rotate(
        query_raw.reshape(items, local_len, heads, head_dim),
        cosine_tab[:, None, :],
        sine_tab[:, None, :],
    ).astype(BF16)
    scores = (
        jnp.einsum("iqhd,ikd->ihqk", query_rows, key_rows, preferred_element_type=F32) * scale
    )
    probs = jax.nn.softmax(jnp.where(allowed, scores, MASKED), axis=-1)
    probs_low = probs.astype(BF16)
    attended = jnp.einsum("ihqk,ikd->iqhd", probs_low, value_rows, preferred_element_type=F32)
    attended = attended.astype(BF16).reshape(items, local_len, query_width)
    (att_joint,) = permute_columns([from_items(attended)], order)
    mid = mm(att_joint, out_full)
    pre_mid = pre_x + mid[:count, :width]
    act_mid = act_x + mid[padded : padded + act_count, width:]

    act_second = rms_norm(act_mid, act_mlp_gain).astype(BF16)
    act_all_rows = jnp.concatenate(ring_gather(act_second, LOOSE), axis=0)
    pre_second = pad(rms_norm(pre_mid, pre_mlp_gain).astype(BF16))
    first_piece, hidden_back, act_all_rows = lax.optimization_barrier(
        (ring(pre_second, 1), hidden_back, act_all_rows)
    )
    second_pieces = [pre_second, first_piece]
    slot_count = lax.dynamic_index_in_dim(hidden_counts, member, keepdims=False)
    slot_live = (jnp.arange(act_gate.shape[1]) < slot_count).astype(F32)

    def scatter_sum(value, dimension):
        return lax.psum_scatter(value, "dp", scatter_dimension=dimension, tiled=True)

    def split(partial):
        size = partial.shape[0] // groups
        return [partial[r * size : (r + 1) * size] for r in range(groups)]

    act_hidden, act_gate_back, act_up_back = feed_forward(
        act_all_rows, act_cot_all, act_gate_full, act_up_full, act_down_full, slot_live
    )
    act_second_part = split(mm_nt(act_gate_back, act_gate_full) + mm_nt(act_up_back, act_up_full))
    act_sum_part = split(mm_nt(act_hidden, act_down_full))

    for r in range(2, groups):
        piece = ring(second_pieces[-1], 1)
        if r == 2:
            piece, act_gate_back, act_up_back, act_hidden = lax.optimization_barrier(
                (piece, act_gate_back, act_up_back, act_hidden)
            )
            act_stacked = stacked_grads(
                ways, act_all_rows, act_cot_all, act_gate_back, act_up_back, act_hidden
            )
        if r == groups - 1:
            piece = after(piece, act_stacked)
        second_pieces.append(piece)
    grad_act = scatter_sum(act_stacked, 0)

    pre_hidden, pre_gate_back, pre_up_back, pre_all = feed_forward_kernel(
        second_pieces, hidden_back, gate_full, up_full
    )
    gate_term = mm_tn(pre_all, pre_gate_back).astype(BF16)
    gate_term, pre_up_back, grad_act = lax.optimization_barrier(
        (gate_term, pre_up_back, grad_act)
    )
    grad_act = grad_act.astype(F32).reshape(3, -1, act_gate.shape[1])
    grad_act_gate, grad_act_up, grad_act_down = grad_act[0], grad_act[1], grad_act[2].T
    grad_pre_gate = scatter_sum(gate_term, 0)
    half = groups // 2 * padded

    def second_rows(cut, gate_rows, up_rows):
        return mm_nt(gate_rows[cut], gate_full) + mm_nt(up_rows[cut], up_full)

    later = second_rows(slice(half, None), pre_gate_back, pre_up_back)
    later, gate_rows, up_rows = lax.optimization_barrier((later, pre_gate_back, pre_up_back))
    sooner = second_rows(slice(0, half), gate_rows, up_rows)

    act_lines = act_count * act_width // width

    def lines(value):
        return value.reshape(act_lines, width)

    def second_part(r):
        rows = sooner if r < groups // 2 else later
        rows = rows[r % (groups // 2) * padded :][:count]
        return jnp.concatenate([rows, lines(act_second_part[r]), lines(act_sum_part[r])], axis=0)

    up_term = down_term = None
    total = second_part(groups - 1)
    for r in range(groups - 2, -1, -1):
        moved = ring(total.astype(BF16), -1, LOOSE)
        if r == groups - 2:
            moved, up_rows = lax.optimization_barrier((moved, after(up_rows, sooner)))
            up_term = mm_tn(pre_all, up_rows).astype(BF16)
        elif r == groups - 3:
            moved, up_term, pre_hidden = lax.optimization_barrier((moved, up_term, pre_hidden))
            down_term = mm_tn(pre_hidden, cot_all).astype(BF16)
        elif r == groups - 4:
            down_term, pre_hidden = lax.optimization_barrier((down_term, pre_hidden))
            pre_sum_part = mm(pre_hidden, down_full).astype(BF16)
            moved, pre_sum_part = lax.optimization_barrier((moved, pre_sum_part))
        total = moved.astype(F32) + second_part(r)
    grad_pre_up = scatter_sum(up_term, 0)
    grad_pre_down = scatter_sum(down_term, 1)
    sum_parts = [each[:count] for each in split(pre_sum_part)]
    sums_arrived = send_members(sum_parts)
    pre_second_back = total[:count]
    act_second_back = total[count : count + act_lines].reshape(act_count, act_width)
    act_sums = total[count + act_lines :].reshape(act_count, act_width)

    pre_mid_part, grad_pre_mlp_gain = rms_back(pre_mid, pre_mlp_gain, pre_second_back)
    act_mid_part, grad_act_mlp_gain = rms_back(act_mid, act_mlp_gain, act_second_back)
    pre_mid_grad = cot_flat.astype(F32) + pre_mid_part
    act_mid_grad = act_final_back + act_mid_part
    back_joint = jnp.concatenate(
        [
            jnp.pad(pre_mid_grad.astype(BF16), ((0, padded - count), (0, act_width))),
            jnp.pad(act_mid_grad.astype(BF16), ((0, act_padded - act_count), (width, 0))),
        ],
        axis=0,
    )
    attended_back = to_items(
        permute_columns([mm_nt(back_joint, out_full).astype(BF16)], order, True)[0]
    ).reshape(items, local_len, heads, head_dim)
    out_half = query_width // 2
    out_sums = chip_sums(
        mm_tn(att_joint[:, :out_half], back_joint).astype(BF16),
        mm_tn(att_joint[:, out_half:], back_joint).astype(BF16),
    ).astype(BF16)
    probs_back = jnp.einsum(
        "iqhd,ikd->ihqk", attended_back, value_rows, preferred_element_type=F32
    )
    value_back = jnp.einsum(
        "ihqk,iqhd->ikd", probs_low, attended_back, preferred_element_type=F32
    )
    scores_back = (
        probs * (probs_back - jnp.sum(probs * probs_back, axis=-1, keepdims=True))
    ).astype(BF16)
    key_back = (
        jnp.einsum("ihqk,iqhd->ikd", scores_back, query_rows, preferred_element_type=F32) * scale
    )
    query_back = (
        jnp.einsum("ihqk,ikd->iqhd", scores_back, key_rows, preferred_element_type=F32) * scale
    )
    keyval_back = jnp.concatenate([key_back, value_back], axis=-1).astype(BF16)
    own_kv_back = ring_scatter(
        [keyval_back[:, r * local_len : (r + 1) * local_len] for r in range(groups)]
    )
    keyval_low = jnp.concatenate(
        [rotate(own_kv_back[..., :head_dim], cosine_tab, -sine_tab), own_kv_back[..., head_dim:]],
        axis=-1,
    ).astype(BF16)
    query_low = rotate(query_back, cosine_tab[:, None, :], -sine_tab[:, None, :])
    query_low = query_low.reshape(items, local_len, query_width).astype(BF16)
    back_rows = from_items(jnp.concatenate([query_low, keyval_low], axis=-1))
    back_rows, grad_pre_gate, out_sums = lax.optimization_barrier(
        (back_rows, grad_pre_gate, out_sums)
    )
    qkv_half = normed.shape[1] // 2
    qkv_own_part = mm_tn(normed[:, :qkv_half], back_rows).astype(BF16)
    qkv_other_part = mm_tn(normed[:, qkv_half:], back_rows).astype(BF16)
    qkv_sums = chip_sums(qkv_own_part, qkv_other_part).astype(BF16)
    act_final_low = (act_mid + act_sums).astype(BF16)
    action_pred = mm(act_final_low, action_head).reshape(pred_cot.shape) * live_mask
    grad_head = mm_tn(act_final_low, pred_back)
    pre_normed_back, act_normed_back = unspread(
        mm_nt(back_rows, qkv_full), padded, width, act_width, order
    )
    pre_normed_back, act_normed_back = pre_normed_back[:count], act_normed_back[:act_count]
    pre_x_part, grad_pre_attn_gain = rms_back(pre_x, pre_attn_gain, pre_normed_back)
    act_x_part, grad_act_attn_gain = rms_back(act_x, act_attn_gain, act_normed_back)
    prefix_grad = (pre_mid_grad + pre_x_part).reshape(prefix_tokens.shape)
    action_grad = (act_mid_grad + act_x_part).reshape(action_tokens.shape)

    devices = ways * groups
    small = jnp.concatenate(
        [
            value.reshape(devices, -1)
            for value in (
                grad_pre_attn_gain,
                grad_pre_mlp_gain,
                grad_act_attn_gain,
                grad_act_mlp_gain,
                grad_head,
            )
        ],
        axis=1,
    )
    small = small + hop(small, 1)
    spare = -(-groups // 8) * 8 - groups
    sent_blocks = []
    for c in range(ways // 2):
        start = jnp.bitwise_xor(lax.axis_index("dp"), 2 * c) * groups
        lines = lax.dynamic_slice_in_dim(small, start, groups, 0)
        lines = jnp.pad(lines, ((0, spare), (0, qkv_sums.shape[2] - small.shape[1])))
        sent_blocks.append(jnp.concatenate([qkv_sums[c], lines.astype(BF16)], axis=0))
    sent_blocks, out_sums = lax.optimization_barrier((sent_blocks, out_sums))
    qkv_total = chips_sum(sent_blocks)
    out_total = chips_sum([out_sums[c] for c in range(ways // 2)])
    qkv_parts = member_parts(qkv_total.astype(BF16), (pre_part, act_part, 1))
    qkv_arrived = send_members(qkv_parts)
    out_parts = member_parts(out_total.astype(BF16), (out_part,))
    out_arrived = send_members(out_parts)
    qkv_arrived, sums_arrived, grad_pre_up, grad_pre_down = lax.optimization_barrier(
        (qkv_arrived, sums_arrived, grad_pre_up, grad_pre_down)
    )
    pre_sums = add_up(sum_parts[0].astype(F32), sums_arrived)
    prefix_out = (pre_mid + pre_sums).astype(BF16).reshape(prefix_tokens.shape)
    grad_out = add_up(out_parts[0].astype(F32), out_arrived)
    grad_qkv = add_up(qkv_parts[0].astype(F32), qkv_arrived)
    total = grad_qkv[pre_part + act_part :, : small.shape[1]]
    sizes = [width // devices] * 2 + [act_width // devices] * 2
    gains, start = [], 0
    for size in sizes:
        gains.append(total[0, start : start + size])
        start += size
    grad_head = total[0, start:].reshape(act_width // devices, -1)

    return (
        prefix_out,
        action_pred,
        prefix_grad,
        action_grad,
        *gains,
        grad_qkv[:pre_part, :query_width],
        grad_qkv[:pre_part, query_width:],
        grad_out[:, :width],
        grad_qkv[pre_part : pre_part + act_part, :query_width],
        grad_qkv[pre_part : pre_part + act_part, query_width:],
        grad_out[:, width:],
        grad_pre_gate.astype(F32),
        grad_pre_up.astype(F32),
        grad_pre_down.astype(F32),
        grad_act_gate,
        grad_act_up,
        grad_act_down,
        grad_head,
    )


def solution(mesh):
    rows = P("dp", "mp", None)
    both = P(("dp", "mp"), None)
    wide = P("dp", "mp")
    tall = P("mp", "dp")
    in_specs = (
        (rows, rows, P("dp", None), P("dp", None))
        + (P(),) * 5
        + (both,) * 6
        + (wide, wide, tall, wide, wide, tall, P(), rows, rows)
    )
    out_specs = (
        (rows,) * 4
        + (P(("dp", "mp")),) * 4
        + (both,) * 6
        + (wide, wide, tall, wide, wide, tall, both)
    )
    return jax.shard_map(shards, mesh=mesh, in_specs=in_specs, out_specs=out_specs, check_vma=False)
```
